32 devices in a mesh: win: 8 (over z, y), seq: 4 (over x, core).
Axes of the slice: x: 2, y: 2, z: 4, core: 2. Of those that a mesh axis runs over, the one named last changes fastest.
Arguments:
- inputs: float32 [24, 512, 512], P('win', 'seq'), may hold values from -6 to 6
- species: int32 [24], P('win'), may hold values from 0 to 7
- lengths: int32 [24], P('win'), may hold values from 0 to 512, as said below
- species_table: float32 [8, 512], replicated, may hold values from -5 to 5
- near_conv_weight: float32 [9, 512, 512], replicated, may hold values from -0.09375 to 0.09375
- near_conv_bias: float32 [512], replicated, may hold values from -3 to 3
- near_conv_gain: float32 [512], replicated, may hold values from 0.5 to 1.5
- near_conv_shift: float32 [512], replicated, may hold values from -1.75 to 1.75
- near_up_weight: float32 [512, 2048], replicated, may hold values from -0.25 to 0.25
- near_up_bias: float32 [2048], replicated, may hold values from -3 to 3
- near_down_weight: float32 [2048, 512], replicated, may hold values from -0.125 to 0.125
- near_down_bias: float32 [512], replicated, may hold values from -3 to 3
- near_ffn_gain: float32 [512], replicated, may hold values from 0.5 to 1.5
- near_ffn_shift: float32 [512], replicated, may hold values from -1.75 to 1.75
- far_conv_weight: float32 [9, 512, 512], replicated, may hold values from -0.09375 to 0.09375
- far_conv_bias: float32 [512], replicated, may hold values from -3 to 3
- far_conv_gain: float32 [512], replicated, may hold values from 0.5 to 1.5
- far_conv_shift: float32 [512], replicated, may hold values from -1.75 to 1.75
- far_up_weight: float32 [512, 2048], replicated, may hold values from -0.25 to 0.25
- far_up_bias: float32 [2048], replicated, may hold values from -3 to 3
- far_down_weight: float32 [2048, 512], replicated, may hold values from -0.125 to 0.125
- far_down_bias: float32 [512], replicated, may hold values from -3 to 3
- far_ffn_gain: float32 [512], replicated, may hold values from 0.5 to 1.5
- far_ffn_shift: float32 [512], replicated, may hold values from -1.75 to 1.75
- cotangent: float32 [24, 512, 512], P('win', 'seq'), may hold values from -6 to 6
Outputs:
- output: float32 [24, 512, 512], P('win', 'seq')
- input_grad: float32 [24, 512, 512], P('win', 'seq')
- grad_species_table: float32 [8, 512], P(None, 'seq')
- grad_near_conv_weight: float32 [9, 512, 512], P(None, None, 'seq')
- grad_near_conv_bias: float32 [512], P('seq')
- grad_near_conv_gain: float32 [512], P('seq')
- grad_near_conv_shift: float32 [512], P('seq')
- grad_near_up_weight: float32 [512, 2048], P(None, 'seq')
- grad_near_up_bias: float32 [2048], P('seq')
- grad_near_down_weight: float32 [2048, 512], P(None, 'seq')
- grad_near_down_bias: float32 [512], P('seq')
- grad_near_ffn_gain: float32 [512], P('seq')
- grad_near_ffn_shift: float32 [512], P('seq')
- grad_far_conv_weight: float32 [9, 512, 512], P(None, None, 'seq')
- grad_far_conv_bias: float32 [512], P('seq')
- grad_far_conv_gain: float32 [512], P('seq')
- grad_far_conv_shift: float32 [512], P('seq')
- grad_far_up_weight: float32 [512, 2048], P(None, 'seq')
- grad_far_up_bias: float32 [2048], P('seq')
- grad_far_down_weight: float32 [2048, 512], P(None, 'seq')
- grad_far_down_bias: float32 [512], P('seq')
- grad_far_ffn_gain: float32 [512], P('seq')
- grad_far_ffn_shift: float32 [512], P('seq')
The draws below stay inside these ranges and needn't reach their ends.
Inputs may be any that keep to these rules, and one draw needn't show every extreme that they name: `lengths`: in each aligned block of 3 window slots the live slots come first and at least one is live; one live slot of each block, drawn from the seed, has the full length 512; a length of 0 marks an empty slot.
All inputs are finite; a program needn't handle non-finite values.
Results may differ from the reference program's by a relative error of at most 0.0003.
Values sent between devices are 32-bit elements; how exact they have to be, the bound alone decides.
A program may use at most 192 MiB of HBM per device.

```python
import jax
import jax.numpy as jnp
from jax import lax

D = 512
FF = 2048
KERNEL = 9
FIRST_DILATION = 1
SECOND_DILATION = 32
LEN = 512
SPECIES = 8
W_DEV = 3
WINDOWS = 24


def draw_lengths(key, part):
    key = jax.random.fold_in(key, 7)
    first, second, third = jax.random.split(key, 3)
    spans = jax.random.randint(first, (WINDOWS,), LEN // 4, LEN + 1)
    live = jax.random.randint(second, (WINDOWS // W_DEV,), 1, W_DEV + 1)
    chosen = jax.random.randint(third, (WINDOWS // W_DEV,), 0, W_DEV) % live
    slot = jnp.arange(WINDOWS, dtype=jnp.int32) % W_DEV
    owner_live = jnp.repeat(live, W_DEV)
    owner_full = jnp.repeat(chosen, W_DEV)
    spans = jnp.where(slot == owner_full, LEN, spans)
    return jnp.where(slot < owner_live, spans, 0).astype(jnp.int32)


def place_ends(values, rng, low, top_value):
    longest = values.shape.index(max(values.shape))
    spots = []
    for shift in (0, 1):
        where = [jax.random.randint(jax.random.fold_in(rng, axis), (), 0, length) for axis, length in enumerate(values.shape)]
        where[longest] = (where[longest] + shift) % values.shape[longest]
        spots.append(tuple(where))
    return values.at[spots[0]].set(low).at[spots[1]].set(top_value)


def steps_of(rng, extent, pieces, low, top_value):
    def one(position, parts):
        draws = jax.random.uniform(jax.random.fold_in(jax.random.fold_in(rng, 6), position), (parts,), jnp.float32, low / len(pieces), top_value / len(pieces))
        return jnp.repeat(jnp.exp(draws), extent[position] // parts).reshape((-1,) + (1,) * (len(extent) - position - 1))

    level = one(*pieces[0])
    for cut in pieces[1:]:
        level = level * one(*cut)
    return level


def gaussian(key, shape, scale, most, cuts=(), held_as=jnp.bfloat16):
    values = jax.random.normal(key, shape, jnp.float32) * scale
    if len(cuts) > 0:
        values = steps_of(key, shape, cuts, -0.22, 0.18) * values
    return jnp.clip(values, min=-most, max=most).astype(held_as)


def setup_inputs(seed: int = 0) -> dict:
    key_list = jax.random.split(jax.random.key(seed), 26)
    return {
        "inputs": gaussian(key_list[0], (WINDOWS, LEN, D), 1.0, 6.0, ((0, 8), (1, 4)), jnp.float32),
        "species": place_ends(jax.random.randint(key_list[1], (WINDOWS,), 0, SPECIES), jax.random.fold_in(key_list[1], 1), 0, SPECIES - 1).astype(jnp.int32),
        "lengths": draw_lengths(jax.random.fold_in(key_list[25], 71), 0),
        "species_table": gaussian(key_list[3], (SPECIES, D), 1.0, 5.0, (), jnp.float32),
        "near_conv_weight": gaussian(key_list[4], (KERNEL, D, D), (KERNEL * D) ** -0.5, 0.09375, (), jnp.float32),
        "near_conv_bias": gaussian(key_list[5], (D,), 0.5, 3.0, (), jnp.float32),
        "near_conv_gain": jnp.clip(1.0 + 0.1 * jax.random.normal(key_list[6], (D,), jnp.float32), 0.5, 1.5),
        "near_conv_shift": gaussian(key_list[7], (D,), 0.3, 1.75, (), jnp.float32),
        "near_up_weight": gaussian(key_list[8], (D, FF), D ** -0.5, 0.25, (), jnp.float32),
        "near_up_bias": gaussian(key_list[9], (FF,), 0.5, 3.0, (), jnp.float32),
        "near_down_weight": gaussian(key_list[10], (FF, D), FF ** -0.5, 0.125, (), jnp.float32),
        "near_down_bias": gaussian(key_list[11], (D,), 0.5, 3.0, (), jnp.float32),
        "near_ffn_gain": jnp.clip(1.0 + 0.1 * jax.random.normal(key_list[12], (D,), jnp.float32), 0.5, 1.5),
        "near_ffn_shift": gaussian(key_list[13], (D,), 0.3, 1.75, (), jnp.float32),
        "far_conv_weight": gaussian(key_list[14], (KERNEL, D, D), (KERNEL * D) ** -0.5, 0.09375, (), jnp.float32),
        "far_conv_bias": gaussian(key_list[15], (D,), 0.5, 3.0, (), jnp.float32),
        "far_conv_gain": jnp.clip(1.0 + 0.1 * jax.random.normal(key_list[16], (D,), jnp.float32), 0.5, 1.5),
        "far_conv_shift": gaussian(key_list[17], (D,), 0.3, 1.75, (), jnp.float32),
        "far_up_weight": gaussian(key_list[18], (D, FF), D ** -0.5, 0.25, (), jnp.float32),
        "far_up_bias": gaussian(key_list[19], (FF,), 0.5, 3.0, (), jnp.float32),
        "far_down_weight": gaussian(key_list[20], (FF, D), FF ** -0.5, 0.125, (), jnp.float32),
        "far_down_bias": gaussian(key_list[21], (D,), 0.5, 3.0, (), jnp.float32),
        "far_ffn_gain": jnp.clip(1.0 + 0.1 * jax.random.normal(key_list[22], (D,), jnp.float32), 0.5, 1.5),
        "far_ffn_shift": gaussian(key_list[23], (D,), 0.3, 1.75, (), jnp.float32),
        "cotangent": gaussian(key_list[24], (WINDOWS, LEN, D), 1.0, 6.0, ((0, 8), (1, 4)), jnp.float32),
    }


@jax.custom_vjp
def low(v):
    return lax.optimization_barrier(v.astype(jnp.bfloat16)).astype(jnp.float32)

@jax.custom_vjp
def low_back(v):
    return v

def low_keep(v):
    return (low(v), None)

def low_pass(kept, grad):
    return (grad,)

def back_keep(v):
    return (v, None)

def back_low(kept, grad):
    return (low(grad),)
low.defvjp(low_keep, low_pass)
low_back.defvjp(back_keep, back_low)
norm_eps = 1e-05
precise = lax.Precision.HIGHEST

def matmul(left, right):
    return jnp.dot(left, right, precision=precise, preferred_element_type=jnp.float32)

def layer_norm(values, gain, shift):
    center = values - lax.optimization_barrier(jnp.mean(values, axis=-1, keepdims=True))
    spread = lax.optimization_barrier(jnp.mean(center * center, axis=-1, keepdims=True))
    return center * lax.rsqrt(spread + norm_eps) * gain + shift

def gelu(values):
    return jax.nn.gelu(values, approximate=False)

def convolve(masked_tokens, weight, bias, dilation_step):
    length = masked_tokens.shape[0]
    width = 4 * dilation_step
    padded_input = jnp.pad(masked_tokens, ((width, width), (0, 0)))
    total = bias + jnp.zeros_like(masked_tokens)
    for tap in range(weight.shape[0]):
        total = total + matmul(padded_input[tap * dilation_step:tap * dilation_step + length], weight[tap])
    return total

def conv_block(values, token_mask, params, dilation_step):
    conv_w, conv_b, conv_g, conv_s, up_w, up_b, down_w, down_b, ffn_g, ffn_s = params
    conv = convolve(values * token_mask, conv_w, conv_b, dilation_step)
    middle_state = values + layer_norm(gelu(conv), conv_g, conv_s)
    hidden = gelu(matmul(middle_state, up_w) + up_b)
    return middle_state + layer_norm(matmul(hidden, down_w) + down_b, ffn_g, ffn_s)

def reference(inputs, species, lengths, species_table, near_conv_weight, near_conv_bias, near_conv_gain, near_conv_shift, near_up_weight, near_up_bias, near_down_weight, near_down_bias, near_ffn_gain, near_ffn_shift, far_conv_weight, far_conv_bias, far_conv_gain, far_conv_shift, far_up_weight, far_up_bias, far_down_weight, far_down_bias, far_ffn_gain, far_ffn_shift, cotangent):
    close_block = (near_conv_weight, near_conv_bias, near_conv_gain, near_conv_shift, near_up_weight, near_up_bias, near_down_weight, near_down_bias, near_ffn_gain, near_ffn_shift)
    distant_block = (far_conv_weight, far_conv_bias, far_conv_gain, far_conv_shift, far_up_weight, far_up_bias, far_down_weight, far_down_bias, far_ffn_gain, far_ffn_shift)
    positions = jnp.arange(LEN, dtype=jnp.int32)
    labels = jnp.arange(SPECIES, dtype=jnp.int32)

    def one_window(totals, items):
        window, label, length, cot = items
        token_mask = (positions < length).astype(jnp.float32)[:, None]
        onehot = (labels == label).astype(jnp.float32)[None, :]

        def forward(window, table, close_block, distant_block):
            start_index = window + matmul(onehot, table)
            middle_state = conv_block(start_index, token_mask, close_block, FIRST_DILATION)
            return conv_block(middle_state, token_mask, distant_block, SECOND_DILATION) * token_mask
        result, back = jax.vjp(forward, window, species_table, close_block, distant_block)
        d_window, d_table, d_near, d_far = back(cot)
        totals = jax.tree.map(jnp.add, totals, (d_table, d_near, d_far))
        return (totals, (result, d_window))
    zeros = jax.tree.map(jnp.zeros_like, (species_table, close_block, distant_block))
    totals, outs = lax.scan(one_window, zeros, (inputs, species, lengths, cotangent))
    output, input_grad = outs
    d_table, d_near, d_far = totals
    g1, g2, g3, g4, g5, g6, g7, g8, g9, g10 = d_near
    h1, h2, h3, h4, h5, h6, h7, h8, h9, h10 = d_far
    return (output, input_grad, d_table, g1, g2, g3, g4, g5, g6, g7, g8, g9, g10, h1, h2, h3, h4, h5, h6, h7, h8, h9, h10)
```

```python
import functools

import jax
import jax.numpy as jnp
from jax import lax
from jax.experimental import pallas as pl
from jax.experimental.pallas import tpu as pltpu
from jax.sharding import PartitionSpec as P

FIRST_DILATION = 1
SECOND_DILATION = 32


norm_eps = 1e-05
precise = lax.Precision.HIGH


def with_halo(x, sides, width):
    for axis, dim in sides:
        peers, length = (lax.axis_size(axis), x.shape[dim])
        up = [(i, (i + 1) % peers) for i in range(peers - 1)]
        down = [(j, i) for i, j in up]
        last = lax.slice_in_dim(x, length - width, length, axis=dim)
        leading = lax.slice_in_dim(x, 0, width, axis=dim)
        before = lax.ppermute(last, axis, up)
        after = lax.ppermute(leading, axis, down)
        x = jnp.concatenate([before, x, after], axis=dim)
    return x


def passed_along(x, axis, by):
    peers = lax.axis_size(axis)
    pairs = [(i, i + by) for i in range(peers) if 0 <= i + by < peers]
    return lax.ppermute(x, axis, pairs)


def matmul(left, right):
    return jnp.dot(left, right, precision=precise, preferred_element_type=jnp.float32)


def layer_norm(values, gain, shift):
    center = values - jnp.mean(values, axis=-1, keepdims=True)
    spread = jnp.mean(center * center, axis=-1, keepdims=True)
    return center * lax.rsqrt(spread + norm_eps) * gain + shift


def gelu(values):
    return jax.nn.gelu(values, approximate=False)


def conv_tail(raw, bias, values, gain, shift):
    return values + layer_norm(gelu(raw + bias), gain, shift)


def ffn_part(middle_state, up_w, up_b, down_w, down_b, gain, shift):
    hidden = gelu(matmul(middle_state, up_w) + up_b)
    return middle_state + layer_norm(matmul(hidden, down_w) + down_b, gain, shift)


def conv_rows(padded_input, weight, dilation_step, rows):
    total = matmul(padded_input[:, 0:rows], weight[0])
    for tap in range(1, weight.shape[0]):
        total = total + matmul(
            padded_input[:, tap * dilation_step : tap * dilation_step + rows], weight[tap]
        )
    return total


def conv_back(padded_input, weight, grad, dilation_step, rows):
    weight_grads = []
    back = jnp.zeros(padded_input.shape, jnp.float32)
    for tap in range(weight.shape[0]):
        piece = padded_input[:, tap * dilation_step : tap * dilation_step + rows]
        weight_grads.append(jnp.einsum("wrd,wre->de", piece, grad, precision=precise))
        back = back.at[:, tap * dilation_step : tap * dilation_step + rows].add(
            matmul(grad, weight[tap].T)
        )
    return (jnp.stack(weight_grads), back)


def block_forward(values, token_mask, params, distant_block):
    conv_w, conv_b, conv_g, conv_s, up_w, up_b, down_w, down_b, ffn_g, ffn_s = params
    rows = values.shape[1]
    masked_tokens = values * token_mask
    if distant_block:
        dilation_step = SECOND_DILATION
        padded_input = with_halo(masked_tokens, (("seq", 1),), 4 * SECOND_DILATION)
    else:
        dilation_step = FIRST_DILATION
        padded_input = with_halo(masked_tokens, (("seq", 1),), 4 * FIRST_DILATION)
    raw = conv_rows(padded_input, conv_w, dilation_step, rows)
    middle_state, tail_back = jax.vjp(conv_tail, raw, conv_b, values, conv_g, conv_s)
    result, ffn_back = jax.vjp(ffn_part, middle_state, up_w, up_b, down_w, down_b, ffn_g, ffn_s)
    return (result, (padded_input, middle_state, tail_back, ffn_back))


def block_backward(grad, token_mask, params, saved, distant_block):
    conv_w, conv_b, conv_g, conv_s, up_w, up_b, down_w, down_b, ffn_g, ffn_s = params
    padded_input, middle_state, tail_back, ffn_back = saved
    rows = grad.shape[1]
    d_mid, d_up, d_upb, d_down, d_downb, d_fgain, d_fshift = ffn_back(grad)
    d_raw, d_cbias, d_values, d_cgain, d_cshift = tail_back(d_mid)
    dilation_step = SECOND_DILATION if distant_block else FIRST_DILATION
    width = 4 * dilation_step
    d_conv, d_padded = conv_back(padded_input, conv_w, d_raw, dilation_step, rows)
    lower = d_padded[:, :width]
    upper = d_padded[:, rows + width :]
    inner = d_padded[:, width : rows + width]
    if distant_block:
        from_next = passed_along(lower, "seq", -1)
        from_prev = passed_along(upper, "seq", 1)
    else:
        from_next = passed_along(lower, "seq", -1)
        from_prev = passed_along(upper, "seq", 1)
    inner = inner.at[:, rows - width :].add(from_next)
    inner = inner.at[:, :width].add(from_prev)
    d_values = d_values + inner * token_mask
    return (
        d_values,
        (d_conv, d_cbias, d_cgain, d_cshift, d_up, d_upb, d_down, d_downb, d_fgain, d_fshift),
    )


MESH_ID = pl.DeviceIdType.MESH


class Place:
    def __init__(self, line):
        w, s = lax.axis_index("win"), lax.axis_index("seq")
        self.line = line
        self.z, self.y = lax.div(w, 2), lax.rem(w, 2)
        self.x, self.c = lax.div(s, 2), lax.rem(s, 2)
        self.sib = (w, 2 * self.x + 1 - self.c)
        self.across = (w, 2 * (1 - self.x) + self.c)
        self.pair = (2 * self.z + 1 - self.y, s)
        self.up = (w + 2, s)
        self.down = (w - 2, s)
        self.has_up = self.z < line - 1
        self.has_down = self.z > 0

    def greet(self):
        barrier = pltpu.get_barrier_semaphore()
        for device in (self.sib, self.across, self.pair):
            pl.semaphore_signal(barrier, inc=1, device_id=device, device_id_type=MESH_ID)

        @pl.when(self.has_up)
        def _():
            pl.semaphore_signal(barrier, inc=1, device_id=self.up, device_id_type=MESH_ID)

        @pl.when(self.has_down)
        def _():
            pl.semaphore_signal(barrier, inc=1, device_id=self.down, device_id_type=MESH_ID)

        pl.semaphore_wait(barrier, 3 + self.has_up.astype(jnp.int32) + self.has_down.astype(jnp.int32))


def remote(src, dst, send, recv, device):
    return pltpu.make_async_remote_copy(
        src_ref=src, dst_ref=dst, send_sem=send, recv_sem=recv, device_id=device, device_id_type=MESH_ID
    )


class Exchange:
    def __init__(self, place, n, unit, hop, refs):
        self.p, self.n, self.unit, self.hop = place, n, unit, hop
        self.__dict__.update(refs)
        line = place.line
        self.roots = (line // 2 - 1, line // 2)
        self.reach = line // 2
        self.at_y = 3 * hop
        self.at_final = self.at_y + (self.reach + 1) * hop
        self.ticks = n + self.at_final + self.reach * hop + 1

    def own(self, a):
        u = self.unit
        return pl.ds(pl.multiple_of(a * (u // 2) + self.p.y * (3 * u // 8), 8), u // 8)

    def mid(self, a):
        u = self.unit
        return pl.ds(a * (u // 2) + u // 8, u // 4)

    def message(self, a):
        u = self.unit
        return pl.ds(pl.multiple_of(a * (u // 2) + self.p.y * (u // 8), 8), 3 * u // 8)

    def c_copy(self, j):
        return remote(
            self.parts.at[j, :, 1 - self.p.c], self.c_got.at[j], self.sem_s.at[j, 0], self.sem_r.at[j, 0], self.p.sib
        )

    def x_copy(self, j):
        return remote(
            self.c_got.at[j, 1 - self.p.x], self.x_got.at[j], self.sem_s.at[j, 1], self.sem_r.at[j, 1], self.p.across
        )

    def y_copy(self, j, a):
        u = self.unit
        other = pl.ds(pl.multiple_of(a * (u // 2) + (1 - self.p.y) * (3 * u // 8), 8), u // 8)
        return remote(
            self.acc.at[j, other],
            self.y_got.at[j, a],
            self.sem_s.at[j, 2 + a],
            self.sem_r.at[j, 2 + a],
            self.p.pair,
        )

    def r_copy(self, j, a, to_up):
        side = 1 if to_up else 0
        return remote(
            self.acc.at[j, self.message(a)],
            self.r_got.at[j, a, side],
            self.sem_s.at[j, 4 + a],
            self.sem_r.at[j, 4 + 2 * a + side],
            self.p.up if to_up else self.p.down,
        )

    def yz_copy(self, j, a):
        return remote(
            self.acc.at[j, self.mid(a)], self.yz_got.at[j], self.sem_s.at[j, 6], self.sem_r.at[j, 8], self.p.pair
        )

    def b_copy(self, j, a, to_up, from_acc):
        src = self.acc if from_acc else self.final
        return remote(
            src.at[j, self.message(a)],
            self.final.at[j, self.message(a)],
            self.sem_s.at[j, 7 + 2 * a + (1 if to_up else 0)],
            self.sem_r.at[j, 9 + a],
            self.p.up if to_up else self.p.down,
        )

    def keep_copy(self, j, a):
        return pltpu.make_async_copy(
            self.acc.at[j, self.message(a)], self.final.at[j, self.message(a)], self.sem_r.at[j, 9 + a]
        )

    def last_copy(self, j, a, from_acc):
        src = self.acc if from_acc else self.final
        return remote(
            src.at[j, self.own(a)],
            self.final.at[j, self.own(a)],
            self.sem_s.at[j, 11 + a],
            self.sem_r.at[j, 11 + a],
            self.p.pair,
        )

    def tick(self, t):
        p, n, hop = self.p, self.n, self.hop

        def stage(offset, body, cond=None):
            j = t - offset
            ok = (j >= 0) & (j < n)
            if cond is not None:
                ok = ok & cond
            pl.when(ok)(lambda: body(j))

        for a in (0, 1):
            root = self.roots[a]
            above, below = p.z > root, p.z < root
            far = jnp.abs(p.z - root)

            def forward(j, a=a, above=above, below=below):
                self.b_copy(j, a, True, False).wait_recv()

                @pl.when(above & p.has_up)
                def _():
                    self.b_copy(j, a, True, False).start()

                @pl.when(below & p.has_down)
                def _():
                    self.b_copy(j, a, False, False).start()

                self.last_copy(j, a, False).start()

            stage(self.at_final + far * hop, forward, above | below)

            def settle(j, a=a):
                self.yz_copy(j, a).wait()
                self.acc[j, self.mid(a), :] += self.yz_got[j]

                @pl.when(p.has_up)
                def _():
                    self.b_copy(j, a, True, True).start()

                @pl.when(p.has_down)
                def _():
                    self.b_copy(j, a, False, True).start()

                self.last_copy(j, a, True).start()
                self.keep_copy(j, a).start()

            stage(self.at_final, settle, p.z == root)

        def own_half(j):
            for a in (0, 1):
                self.y_copy(j, a).wait_recv()
                self.acc[j, self.own(a), :] += self.y_got[j, a]

        stage(self.at_y, own_half)

        for a in (0, 1):
            root = self.roots[a]
            above, below = p.z > root, p.z < root
            far = jnp.abs(p.z - root)

            def reduce(j, a=a, root=root, above=above, below=below):
                @pl.when((p.z >= root) & p.has_up)
                def _():
                    self.r_copy(j, a, False).wait_recv()
                    self.acc[j, self.message(a), :] += self.r_got[j, a, 0]

                @pl.when((p.z <= root) & p.has_down)
                def _():
                    self.r_copy(j, a, True).wait_recv()
                    self.acc[j, self.message(a), :] += self.r_got[j, a, 1]

                @pl.when(above)
                def _():
                    self.r_copy(j, a, False).start()

                @pl.when(below)
                def _():
                    self.r_copy(j, a, True).start()

                @pl.when(p.z == root)
                def _():
                    self.yz_copy(j, a).start()

            stage(self.at_y + (self.reach - far) * hop, reduce)

        def gather(j):
            self.x_copy(j).wait_recv()
            self.acc[j] = self.c_got[j, p.x] + self.x_got[j]
            for a in (0, 1):
                self.y_copy(j, a).start()

        stage(2 * hop, gather)

        def cross(j):
            self.c_copy(j).wait_recv()
            for x in (0, 1):
                self.c_got[j, x] += self.parts[j, x, p.c]
            self.x_copy(j).start()

        stage(hop, cross)
        stage(0, lambda j: self.c_copy(j).start())

    def drain(self):
        p = self.p

        def body(j, carry):
            self.c_copy(j).wait_send()
            self.x_copy(j).wait_send()
            for a in (0, 1):
                root = self.roots[a]
                self.y_copy(j, a).wait_send()
                self.last_copy(j, a, False).wait()

                @pl.when(p.z != root)
                def _():
                    self.r_copy(j, a, True).wait_send()

                @pl.when(p.z == root)
                def _():
                    self.keep_copy(j, a).wait()

                @pl.when((p.z >= root) & p.has_up)
                def _():
                    self.b_copy(j, a, True, False).wait_send()

                @pl.when((p.z <= root) & p.has_down)
                def _():
                    self.b_copy(j, a, False, False).wait_send()

            return carry

        lax.fori_loop(0, self.n, body, 0)


def sum_kernel(n, unit, hop, line, parts, final, c_got, x_got, y_got, r_got, yz_got, acc, sem_s, sem_r):
    place = Place(line)
    place.greet()
    ex = Exchange(
        place,
        n,
        unit,
        hop,
        dict(
            parts=parts,
            final=final,
            c_got=c_got,
            x_got=x_got,
            y_got=y_got,
            r_got=r_got,
            yz_got=yz_got,
            acc=acc,
            sem_s=sem_s,
            sem_r=sem_r,
        ),
    )

    def body(t, carry):
        ex.tick(t)
        return carry

    lax.fori_loop(0, ex.ticks, body, 0)
    ex.drain()


def summed(parts, line, hop):
    n, _, _, unit, lanes = parts.shape
    f32 = jnp.float32
    return pl.pallas_call(
        functools.partial(sum_kernel, n, unit, hop, line),
        out_shape=jax.ShapeDtypeStruct((n, unit, lanes), f32),
        in_specs=[pl.BlockSpec(memory_space=pltpu.VMEM)],
        out_specs=pl.BlockSpec(memory_space=pl.ANY),
        scratch_shapes=[
            pltpu.VMEM((n, 2, unit, lanes), f32),
            pltpu.VMEM((n, unit, lanes), f32),
            pltpu.VMEM((n, 2, unit // 8, lanes), f32),
            pltpu.VMEM((n, 2, 2, 3 * unit // 8, lanes), f32),
            pltpu.VMEM((n, unit // 4, lanes), f32),
            pltpu.VMEM((n, unit, lanes), f32),
            pltpu.SemaphoreType.DMA((n, 13)),
            pltpu.SemaphoreType.DMA((n, 13)),
        ],
        compiler_params=pltpu.CompilerParams(
            collective_id=0, has_side_effects=True, vmem_limit_bytes=60 * 1024 * 1024
        ),
        name="sum_grads",
    )(parts)


def on_device(
    inputs,
    species,
    lengths,
    species_table,
    near_conv_weight,
    near_conv_bias,
    near_conv_gain,
    near_conv_shift,
    near_up_weight,
    near_up_bias,
    near_down_weight,
    near_down_bias,
    near_ffn_gain,
    near_ffn_shift,
    far_conv_weight,
    far_conv_bias,
    far_conv_gain,
    far_conv_shift,
    far_up_weight,
    far_up_bias,
    far_down_weight,
    far_down_bias,
    far_ffn_gain,
    far_ffn_shift,
    cotangent,
):
    close_block = (
        near_conv_weight,
        near_conv_bias,
        near_conv_gain,
        near_conv_shift,
        near_up_weight,
        near_up_bias,
        near_down_weight,
        near_down_bias,
        near_ffn_gain,
        near_ffn_shift,
    )
    distant_block = (
        far_conv_weight,
        far_conv_bias,
        far_conv_gain,
        far_conv_shift,
        far_up_weight,
        far_up_bias,
        far_down_weight,
        far_down_bias,
        far_ffn_gain,
        far_ffn_shift,
    )
    rows = inputs.shape[1]
    positions = lax.axis_index("seq") * rows + jnp.arange(rows, dtype=jnp.int32)
    token_mask = (positions[None, :] < lengths[:, None]).astype(jnp.float32)[:, :, None]
    labels = jnp.arange(species_table.shape[0], dtype=jnp.int32)
    onehot = (species[:, None] == labels[None, :]).astype(jnp.float32)
    start_index = inputs + matmul(onehot, species_table)[:, None, :]
    middle_state, near_saved = block_forward(start_index, token_mask, close_block, False)
    final, far_saved = block_forward(middle_state, token_mask, distant_block, True)
    output = final * token_mask
    grad, far_grads = block_backward(
        cotangent * token_mask, token_mask, distant_block, far_saved, True
    )
    h1, h2, h3, h4, h5, h6, h7, h8, h9, h10 = far_grads
    input_grad, near_grads = block_backward(grad, token_mask, close_block, near_saved, False)
    g1, g2, g3, g4, g5, g6, g7, g8, g9, g10 = near_grads
    table_grad = matmul(onehot.T, jnp.sum(input_grad, axis=1))
    line = lax.axis_size("win") // 2
    unit = 256

    def columns(v):
        return jnp.transpose(v.reshape(v.shape[0], 4, -1), (1, 0, 2))

    def packed(conv, up, down, small):
        pieces = [columns(conv.reshape(-1, conv.shape[-1])), columns(down)]
        wide = columns(up)
        lanes = pieces[0].shape[-1]
        wide = jnp.transpose(wide.reshape(4, wide.shape[1], -1, lanes), (0, 2, 1, 3))
        pieces.append(wide.reshape(4, -1, lanes))
        pieces.append(jnp.pad(small, ((0, 0), (0, unit - small.shape[1]), (0, 0))))
        v = jnp.concatenate(pieces, axis=1)
        return jnp.transpose(v.reshape(2, 2, -1, unit, lanes), (2, 0, 1, 3, 4))

    def small_rows(grads, table):
        rows = [columns(g.reshape(1, -1)) for g in grads[1:4] + (grads[7], grads[8], grads[9])]
        rows.append(grads[5].reshape(4, -1, rows[0].shape[-1]))
        if table is not None:
            rows.append(columns(table))
        return jnp.concatenate(rows, axis=1)

    def unpacked(v, conv, up, down):
        lanes = v.shape[-1]
        taps, width = conv.shape[:2]
        v = v.reshape(-1, lanes)
        at = taps * width
        g1 = v[:at].reshape(taps, width, lanes)
        g7 = v[at : at + down.shape[0]]
        at += down.shape[0]
        high = up.shape[0]
        wide = up.shape[1] // 4
        g5 = v[at : at + high * wide // lanes].reshape(-1, high, lanes)
        g5 = jnp.transpose(g5, (1, 0, 2)).reshape(high, wide)
        at += high * wide // lanes
        s = v[at:]
        g6 = s[6 : 6 + wide // lanes].reshape(-1)
        return (g1, s[0], s[1], s[2], g5, g6, g7, s[3], s[4], s[5]), s[6 + wide // lanes :]

    far_sum = summed(packed(h1, h5, h7, small_rows(far_grads, None)), line, 2)
    near_sum = summed(packed(g1, g5, g7, small_rows(near_grads, table_grad)), line, 2)
    (h1, h2, h3, h4, h5, h6, h7, h8, h9, h10), _ = unpacked(far_sum, h1, h5, h7)
    (g1, g2, g3, g4, g5, g6, g7, g8, g9, g10), rest = unpacked(near_sum, g1, g5, g7)
    table_grad = rest[: species_table.shape[0]]
    return (
        output,
        input_grad,
        table_grad,
        g1,
        g2,
        g3,
        g4,
        g5,
        g6,
        g7,
        g8,
        g9,
        g10,
        h1,
        h2,
        h3,
        h4,
        h5,
        h6,
        h7,
        h8,
        h9,
        h10,
    )


def solution(mesh):
    return jax.shard_map(
        on_device,
        mesh=mesh,
        in_specs=(
            P("win", "seq", None),
            P("win"),
            P("win"),
            P(),
            P(),
            P(),
            P(),
            P(),
            P(),
            P(),
            P(),
            P(),
            P(),
            P(),
            P(),
            P(),
            P(),
            P(),
            P(),
            P(),
            P(),
            P(),
            P(),
            P(),
            P("win", "seq", None),
        ),
        out_specs=(
            P("win", "seq", None),
            P("win", "seq", None),
            P(None, "seq"),
            P(None, None, "seq"),
            P("seq"),
            P("seq"),
            P("seq"),
            P(None, "seq"),
            P("seq"),
            P(None, "seq"),
            P("seq"),
            P("seq"),
            P("seq"),
            P(None, None, "seq"),
            P("seq"),
            P("seq"),
            P("seq"),
            P(None, "seq"),
            P("seq"),
            P(None, "seq"),
            P("seq"),
            P("seq"),
            P("seq"),
        ),
        check_vma=False,
    )
```

```python
import functools

import jax
import jax.numpy as jnp
from jax import lax
from jax.experimental import pallas as pl
from jax.experimental.pallas import tpu as pltpu
from jax.sharding import PartitionSpec as P

FIRST_DILATION = 1
SECOND_DILATION = 32
EPS = 1e-05
ROWS = 32
HALO = 8
SEQ = 4
f32, bf16 = jnp.float32, jnp.bfloat16
MESH_ID = pl.DeviceIdType.MESH


def split(v):
    high = v.astype(bf16)
    return high, (v - high.astype(f32)).astype(bf16)


def dot(left, right, dims):
    return lax.dot_general(left, right, (dims, ((), ())), preferred_element_type=f32)


def dot3(left, right, dims=((1,), (0,))):
    (lh, ll), (rh, rl) = left, right
    return dot(lh, rh, dims) + (dot(lh, rl, dims) + dot(ll, rh, dims))


NT = ((1,), (1,))
TN = ((0,), (0,))


def gauss(z):
    size = jnp.abs(z)
    t = 1.0 / (1.0 + (0.3275911 * 0.7071067811865476) * size)
    e = jnp.exp(-0.5 * z * z)
    poly = 0.5 * 1.061405429
    for term in (-1.453152027, 1.421413741, -0.284496736, 0.254829592):
        poly = poly * t + 0.5 * term
    tail = poly * t * e
    return jnp.where(z >= 0, 1.0 - tail, tail), (z * 0.3989422804014327) * e


def row_mean(v):
    return jnp.mean(v, axis=-1, keepdims=True)


def remote(src, dst, send, recv, device):
    return pltpu.make_async_remote_copy(
        src_ref=src, dst_ref=dst, send_sem=send, recv_sem=recv, device_id=device, device_id_type=MESH_ID
    )


class Refs:
    def __init__(self, names, refs):
        for name, ref in zip(names, refs, strict=True):
            setattr(self, name, ref)

    def of(self, side, name):
        return getattr(self, side + "_" + name)


class Place:
    def __init__(self, line):
        w, s = lax.axis_index("win"), lax.axis_index("seq")
        self.w, self.s, self.line = w, s, line
        self.z, self.y = lax.div(w, 2), lax.rem(w, 2)
        self.x, self.c = lax.div(s, 2), lax.rem(s, 2)
        self.sib_s = 2 * self.x + 1 - self.c
        self.across_s = 2 * (1 - self.x) + self.c
        self.diag_s = SEQ - 1 - s
        self.sib, self.across, self.diag = (w, self.sib_s), (w, self.across_s), (w, self.diag_s)
        self.pair = (2 * self.z + 1 - self.y, s)
        self.up, self.down = (w + 2, s), (w - 2, s)
        self.next, self.prev = (w, s + 1), (w, s - 1)
        self.has_up, self.has_down = self.z < line - 1, self.z > 0
        self.has_next, self.has_prev = s < SEQ - 1, s > 0
        self.inner = self.c != self.x

    def greet(self, whole):
        barrier = pltpu.get_barrier_semaphore()

        def signal(device):
            pl.semaphore_signal(barrier, inc=1, device_id=device, device_id_type=MESH_ID)

        for device in (self.sib, self.across, self.diag):
            signal(device)
        if not whole:
            pl.semaphore_wait(barrier, 3)
            return
        signal(self.pair)
        pl.when(self.has_up)(lambda: signal(self.up))
        pl.when(self.has_down)(lambda: signal(self.down))
        pl.semaphore_wait(barrier, 4 + self.has_up.astype(jnp.int32) + self.has_down.astype(jnp.int32))


SAVED = ("mid", "n1", "gr1", "n2", "rs2", "hid_h", "hid_l", "gp")


def saved_shapes(rows, d, ff):
    blocks = ff // d
    return dict(
        mid=((rows, d), f32),
        n1=((rows, d), f32),
        gr1=((rows, d), f32),
        n2=((rows, d), f32),
        rs2=((rows, 128), f32),
        hid_h=((blocks, rows, d), bf16),
        hid_l=((blocks, rows, d), bf16),
        gp=((blocks, rows, d), f32),
    )


def ff_columns(ref, b, d, parts, lanes):
    wide = d * parts // SEQ
    return [ref[:, pl.ds(pl.multiple_of(q * wide + b * lanes, lanes), lanes)] for q in range(SEQ)]


def ff_rows(ref, b, d, parts, lanes):
    wide = d * parts // SEQ
    return [ref[pl.ds(pl.multiple_of(q * wide + b * lanes, lanes), lanes), :] for q in range(SEQ)]


def forward_kernel(dims, *refs):
    windows, base, d, ff, taps, line = dims
    rows = windows * base
    blocks = ff // d
    lanes = d // SEQ
    names = ["lengths", "species", "table", "inputs"]
    weights = ("conv", "up", "down")
    vectors = ("cb", "g1", "s1", "ub", "vb", "g2", "s2")
    for side in ("near", "far"):
        names += [side + "_" + v for v in weights + vectors]
    names += ["output", "near_full", "far_full"]
    for side in ("near", "far"):
        names += [side + "_out_" + v for v in SAVED]
    for side in ("near", "far"):
        names += [side + "_" + v for v in SAVED]
    names += ["cw", "uw", "vw", "x", "acc", "zb", "mid_h", "mid_l", "hp", "hq", "hq_h", "hq_l", "own"]
    names += ["out_buf", "csem", "wsem", "osem", "ssem", "rsem"]
    r = Refs(names, refs)
    p = Place(line)

    def conv_weights(side, k):
        return pltpu.make_async_copy(r.of(side, "conv").at[k], r.cw.at[k], r.csem.at[k])

    def wide_weights(side, i):
        src, dst = (("up", r.uw), ("down", r.vw))[i]
        return pltpu.make_async_copy(r.of(side, src), dst, r.wsem.at[i])

    order = [taps // 2] + [k for k in range(taps) if k != taps // 2]
    for k in order:
        conv_weights("near", k).start()
    for i in (0, 1):
        wide_weights("near", i).start()

    def live(w):
        where = p.s * base + lax.broadcasted_iota(jnp.int32, (base, 1), 0)
        return where < r.lengths[w]

    def window(w):
        return pl.ds(pl.multiple_of(w * base, base), base)

    def step_rows(i):
        return pl.ds(pl.multiple_of(i * ROWS, ROWS), ROWS)

    def loop(n, body):
        def run(i, carry):
            body(i)
            return carry

        lax.fori_loop(0, n, run, 0)

    def begin(w):
        v = r.inputs[w] + r.table[pl.ds(r.species[w], 1), :]
        r.x[window(w), :] = v
        h = jnp.where(live(w), v, 0.0)
        r.hp[w, HALO : HALO + base, :] = h
        r.own[w] = h

    loop(windows, begin)

    @pl.when(p.s == 0)
    def _():
        r.hp[:, 0:HALO, :] = jnp.zeros((windows, HALO, d), f32)
        r.hq[:, 0:base, :] = jnp.zeros((windows, base, d), f32)

    @pl.when(p.s == SEQ - 1)
    def _():
        r.hp[:, HALO + base :, :] = jnp.zeros((windows, HALO, d), f32)
        r.hq[:, 2 * base :, :] = jnp.zeros((windows, base, d), f32)

    p.greet(False)
    ssem, rsem = r.ssem, r.rsem

    def halo_next():
        return remote(
            r.hp.at[:, pl.ds(base, HALO)], r.hp.at[:, pl.ds(0, HALO)], ssem.at[0], rsem.at[0], p.next
        )

    def halo_prev():
        return remote(
            r.hp.at[:, pl.ds(HALO, HALO)], r.hp.at[:, pl.ds(HALO + base, HALO)], ssem.at[1], rsem.at[1], p.prev
        )

    pl.when(p.has_next)(lambda: halo_next().start())
    pl.when(p.has_prev)(lambda: halo_prev().start())

    other_inner = (p.w, jnp.where(p.x == 0, 2, 1))
    first_other = 2 * (1 - p.x)
    other_outer = jnp.where(p.x == 0, 3, 0)

    def bulk_keep(full, at):
        return pltpu.make_async_copy(r.own, r.of(full, "full").at[p.s], ssem.at[at])

    def bulk_sib(full, at, block, src=None):
        return remote(
            r.own if src is None else src, r.of(full, "full").at[block], ssem.at[at + 1], rsem.at[at + 1], p.sib
        )

    def bulk_across(full, at):
        return remote(r.own, r.of(full, "full").at[p.s], ssem.at[at + 2], rsem.at[at + 2 + lax.rem(p.s, 2)], other_inner)

    def bulk_relay(full, at, block, i, src=None):
        src = r.of(full, "full").at[block] if src is None else src
        return remote(src, r.of(full, "full").at[block], ssem.at[at + 3 + i], rsem.at[at + 4 + i], p.sib)

    NEAR, FAR = 4, 12
    bulk_keep("near", NEAR).start()
    bulk_sib("near", NEAR, p.s).start()
    bulk_across("near", NEAR).start()

    def tap_product(side, k, lhs):
        conv_weights(side, k).wait()
        return dot3(lhs, split(r.cw[k]))

    def near_tap(k):
        lhs = r.hp[:, HALO + (k - taps // 2) * FIRST_DILATION : HALO + (k - taps // 2) * FIRST_DILATION + base, :]
        return tap_product("near", k, split(lhs.reshape(rows, d)))

    def conv_tail(side):
        def body(w):
            at = window(w)
            v = r.acc[at, :] + r.of(side, "cb")[...]
            cdf, zd = gauss(v)
            a = v * cdf
            center = a - row_mean(a)
            rs = lax.rsqrt(row_mean(center * center) + EPS)
            n = center * rs
            mid = r.x[at, :] + (n * r.of(side, "g1")[...] + r.of(side, "s1")[...])
            r.of(side, "n1")[at, :] = n
            r.of(side, "gr1")[at, :] = (cdf + zd) * rs
            r.of(side, "mid")[at, :] = mid
            h, l = split(mid)
            r.mid_h[at, :] = h
            r.mid_l[at, :] = l

        loop(windows, body)

    def ffn(side):
        def body(b):
            up = jnp.concatenate(ff_columns(r.uw, b, d, blocks, lanes), axis=1)
            r.zb[...] = dot3((r.mid_h[...], r.mid_l[...]), split(up))
            bias = jnp.concatenate(ff_columns(r.of(side, "ub"), b, d, blocks, lanes), axis=1)

            def act(i):
                at = step_rows(i)
                z = r.zb[at, :] + bias
                cdf, zd = gauss(z)
                h, l = split(z * cdf)
                r.of(side, "hid_h")[b, at, :] = h
                r.of(side, "hid_l")[b, at, :] = l
                r.of(side, "gp")[b, at, :] = cdf + zd

            loop(rows // ROWS, act)
            down = jnp.concatenate(ff_rows(r.vw, b, d, blocks, lanes), axis=0)
            f = dot3((r.of(side, "hid_h")[b], r.of(side, "hid_l")[b]), split(down))

            @pl.when(b == 0)
            def _():
                r.acc[...] = f

            @pl.when(b > 0)
            def _():
                r.acc[...] += f

        loop(blocks, body)

    def ffn_tail(side, keep):
        def body(w):
            at = window(w)
            f = r.acc[at, :] + r.of(side, "vb")[...]
            center = f - row_mean(f)
            rs = lax.rsqrt(row_mean(center * center) + EPS)
            n = center * rs
            r.of(side, "n2")[at, :] = n
            r.of(side, "rs2")[at, :] = jnp.broadcast_to(rs, (base, 128))
            keep(w, at, r.of(side, "mid")[at, :] + (n * r.of(side, "g2")[...] + r.of(side, "s2")[...]))

        loop(windows, body)

    def save(side):
        at = 0 if side == "near" else len(SAVED)
        for i, name in enumerate(SAVED):
            pltpu.make_async_copy(r.of(side, name), r.of(side, "out_" + name), r.osem.at[at + i]).start()

    r.acc[...] = near_tap(order[0])
    pl.when(p.has_prev)(lambda: halo_next().wait_recv())
    pl.when(p.has_next)(lambda: halo_prev().wait_recv())
    for k in order[1:]:
        r.acc[...] += near_tap(k)
    for k in order:
        conv_weights("far", k).start()
    conv_tail("near")
    for i in (0, 1):
        wide_weights("near", i).wait()
    ffn("near")
    for i in (0, 1):
        wide_weights("far", i).start()

    bulk_keep("near", NEAR).wait()
    bulk_sib("near", NEAR, p.s).wait_send()
    bulk_across("near", NEAR).wait_send()

    def middle(w, at, v):
        r.x[at, :] = v
        h = jnp.where(live(w), v, 0.0)
        r.hq[w, base : 2 * base, :] = h
        r.own[w] = h
        hh, hl = split(h)
        r.hq_h[w, base : 2 * base, :] = hh
        r.hq_l[w, base : 2 * base, :] = hl

    ffn_tail("near", middle)

    def block_next():
        return remote(r.own, r.hq.at[:, pl.ds(0, base)], ssem.at[2], rsem.at[2], p.next)

    def block_prev():
        return remote(r.own, r.hq.at[:, pl.ds(2 * base, base)], ssem.at[3], rsem.at[3], p.prev)

    pl.when(p.has_next)(lambda: block_next().start())
    pl.when(p.has_prev)(lambda: block_prev().start())
    bulk_keep("far", FAR).start()
    bulk_sib("far", FAR, p.s).start()
    save("near")

    @pl.when(p.inner)
    def _():
        for i in (0, 1):
            remote(
                r.own, r.near_full.at[first_other + i], ssem.at[NEAR + 2], rsem.at[NEAR + 2 + i], other_inner
            ).wait_recv()
            bulk_relay("near", NEAR, first_other + i, i).start()

    def far_tap(k):
        at = pl.ds(pl.multiple_of(base + (k - taps // 2) * SECOND_DILATION, SECOND_DILATION), base)
        lhs = (r.hq_h[:, at, :].reshape(rows, d), r.hq_l[:, at, :].reshape(rows, d))
        conv_weights("far", k).wait()
        r.acc[...] += dot3(lhs, split(r.cw[k]))

    r.acc[...] = jnp.zeros((rows, d), f32)
    far_tap(taps // 2)
    pl.when(p.has_prev)(lambda: block_next().wait_recv())
    pl.when(p.has_next)(lambda: block_prev().wait_recv())

    @pl.when(jnp.logical_not(p.inner))
    def _():
        bulk_across("far", FAR).start()

    def halves(w):
        for at in (0, 2 * base):
            h, l = split(r.hq[w, at : at + base, :])
            r.hq_h[w, at : at + base, :] = h
            r.hq_l[w, at : at + base, :] = l

    loop(windows, halves)

    def keep_inner(at):
        return pltpu.make_async_copy(
            r.hq.at[:, pl.ds(at, base)], r.far_full.at[other_inner[1]], ssem.at[FAR + 2]
        )

    def relay_inner(at):
        return bulk_relay("far", FAR, other_inner[1], 0, r.hq.at[:, pl.ds(at, base)])

    inner_at = pl.multiple_of(jnp.where(p.x == 0, 2 * base, 0), base)

    @pl.when(p.inner)
    def _():
        keep_inner(inner_at).start()
        relay_inner(inner_at).start()

    loop(taps // 2, far_tap)
    loop(taps // 2, lambda i: far_tap(i + taps // 2 + 1))
    conv_tail("far")
    for i in (0, 1):
        wide_weights("far", i).wait()
    ffn("far")

    def finish(w, at, v):
        r.out_buf[at, :] = jnp.where(live(w), v, 0.0)

    ffn_tail("far", finish)
    save("far")
    result = pltpu.make_async_copy(r.out_buf, r.output, r.osem.at[2 * len(SAVED)])
    result.start()

    @pl.when(p.inner)
    def _():
        remote(
            r.own, r.far_full.at[other_outer], ssem.at[FAR + 2], rsem.at[FAR + 2 + lax.rem(other_outer, 2)], other_inner
        ).wait_recv()
        bulk_relay("far", FAR, other_outer, 1).start()
        keep_inner(inner_at).wait()
        relay_inner(inner_at).wait_send()
        bulk_relay("far", FAR, other_outer, 1).wait_send()
        for i in (0, 1):
            bulk_relay("near", NEAR, first_other + i, i).wait_send()

    @pl.when(jnp.logical_not(p.inner))
    def _():
        bulk_across("far", FAR).wait_send()
        for full, at in (("near", NEAR), ("far", FAR)):
            for i in (0, 1):
                bulk_relay(full, at, first_other + i, i).wait_recv()

    for full, at in (("near", NEAR), ("far", FAR)):
        bulk_sib(full, at, p.sib_s).wait_recv()
    bulk_sib("far", FAR, p.s).wait_send()
    bulk_keep("far", FAR).wait()

    @pl.when(p.has_next)
    def _():
        halo_next().wait_send()
        block_next().wait_send()

    @pl.when(p.has_prev)
    def _():
        halo_prev().wait_send()
        block_prev().wait_send()

    result.wait()
    for s, side in enumerate(("near", "far")):
        for i, name in enumerate(SAVED):
            pltpu.make_async_copy(
                r.of(side, name), r.of(side, "out_" + name), r.osem.at[s * len(SAVED) + i]
            ).wait()


def forward(line, lengths, species, table, inputs, near, far):
    windows, base, d = inputs.shape
    taps, ff = near[0].shape[0], near[4].shape[1]
    rows, blocks = windows * base, ff // d
    smem = pl.BlockSpec(memory_space=pltpu.SMEM)
    vmem = pl.BlockSpec(memory_space=pltpu.VMEM)
    hbm = pl.BlockSpec(memory_space=pl.ANY)
    args, specs = [lengths, species, table, inputs], [smem, smem, vmem, vmem]
    for cw, cb, g1, s1, uw, ub, vw, vb, g2, s2 in (near, far):
        args += [cw, uw, vw] + [v.reshape(1, -1) for v in (cb, g1, s1, ub, vb, g2, s2)]
        specs += [hbm] * 3 + [vmem] * 7
    kept = saved_shapes(rows, d, ff)
    full = ((SEQ, windows, base, d), f32)
    outs = [((rows, d), f32), full, full] + 2 * [kept[v] for v in SAVED]
    scratch = 2 * [pltpu.VMEM(*kept[v]) for v in SAVED]
    scratch += [
        pltpu.VMEM((taps, d, d), f32),
        pltpu.VMEM((d, ff), f32),
        pltpu.VMEM((ff, d), f32),
        pltpu.VMEM((rows, d), f32),
        pltpu.VMEM((rows, d), f32),
        pltpu.VMEM((rows, d), f32),
        pltpu.VMEM((rows, d), bf16),
        pltpu.VMEM((rows, d), bf16),
        pltpu.VMEM((windows, base + 2 * HALO, d), f32),
        pltpu.VMEM((windows, 3 * base, d), f32),
        pltpu.VMEM((windows, 3 * base, d), bf16),
        pltpu.VMEM((windows, 3 * base, d), bf16),
        pltpu.VMEM((windows, base, d), f32),
        pltpu.VMEM((rows, d), f32),
        pltpu.SemaphoreType.DMA((taps,)),
        pltpu.SemaphoreType.DMA((2,)),
        pltpu.SemaphoreType.DMA((2 * len(SAVED) + 1,)),
        pltpu.SemaphoreType.DMA((20,)),
        pltpu.SemaphoreType.DMA((20,)),
    ]
    got = pl.pallas_call(
        functools.partial(forward_kernel, (windows, base, d, ff, taps, line)),
        out_shape=[jax.ShapeDtypeStruct(*v) for v in outs],
        in_specs=specs,
        out_specs=[hbm] * len(outs),
        scratch_shapes=scratch,
        compiler_params=pltpu.CompilerParams(
            collective_id=0, has_side_effects=True, vmem_limit_bytes=60 * 1024 * 1024
        ),
        name="forward",
    )(*args)
    n = len(SAVED)
    return got[0].reshape(inputs.shape), got[1], got[2], got[3 : 3 + n], got[3 + n :]


RING = 16
FEW = 8
EXCHANGE_REFS = tuple(
    dict(parts=0, c_got=0, x_got=0, y_got=0, r_got=0, yz_got=0, acc=0, final=0, fs=0, fr=0, us=0, ur=0, all_s=0, all_r=0)
)


class Plan:
    def __init__(self, partial, whole, turns, lead, hop):
        self.partial, self.whole, self.turns, self.lead, self.hop = partial, whole, turns, lead, hop
        self.alone = partial - turns
        self.second = partial + whole
        self.near_whole = self.second + partial + 1
        self.n = self.near_whole + whole
        self.partials = 2 * partial + 1

    def far_whole_at(self, i):
        return self.alone + 2 * i if i < self.turns else self.partial + i

    def is_partial(self, j):
        turn = (j >= self.alone) & (j < self.alone + 2 * self.turns) & (lax.rem(j - self.alone, 2) == 1)
        return (j < self.alone) | turn | ((j >= self.second) & (j < self.near_whole))

    def order(self, j):
        turn = self.alone + lax.div(j - self.alone, 2)
        far = jnp.where(j < self.alone, j, turn)
        return jnp.where(j < self.second, far, j - self.second + self.partial)

    def place(self, f):
        far = jnp.where(f < self.alone, f, self.alone + 2 * (f - self.alone) + 1)
        return jnp.where(f < self.partial, far, f - self.partial + self.second)

    def starting(self, t):
        shift = self.second - self.partial - self.lead
        far = (t >= 0) & (t < self.partial)
        near = (t >= self.partial + shift) & (t < self.partials + shift)
        return far | near, jnp.where(far, t, t - shift)


class Exchange:
    def __init__(self, place, plan, unit, refs):
        self.p, self.plan, self.unit, self.hop = place, plan, unit, plan.hop
        for name in EXCHANGE_REFS:
            setattr(self, name, getattr(refs, name))
        line, hop = place.line, plan.hop
        self.roots = (line // 2 - 1, line // 2)
        self.reach = line // 2
        self.at_y = 3 * hop
        self.at_final = self.at_y + (self.reach + 1) * hop
        self.ticks = plan.n + self.at_final + self.reach * hop + 1
        y = place.y
        self.own = pl.ds(pl.multiple_of(y * (3 * unit // 8), 8), unit // 8)
        self.others = pl.ds(pl.multiple_of((1 - y) * (3 * unit // 8), 8), unit // 8)
        self.mid = pl.ds(unit // 8, unit // 4)
        self.message = pl.ds(pl.multiple_of(y * (unit // 8), 8), 3 * unit // 8)

    def slot(self, f):
        return jnp.where(f < self.plan.partial, f, f - self.plan.partial)

    def c_copy(self, f):
        src = self.parts.at[self.slot(f), :, 1 - self.p.c]
        return remote(src, self.c_got.at[lax.rem(f, FEW)], self.fs.at[f, 0], self.fr.at[f, 0], self.p.sib)

    def x_copy(self, f):
        src = self.parts.at[self.slot(f), 1 - self.p.x, self.p.c]
        return remote(src, self.x_got.at[self.slot(f)], self.fs.at[f, 1], self.fr.at[f, 1], self.p.across)

    def y_copy(self, j):
        dst = self.y_got.at[lax.rem(j, RING)]
        return remote(self.acc.at[j, :, self.others], dst, self.all_s.at[0], self.ur.at[j, 0], self.p.pair)

    def r_copy(self, j, a, to_up, index):
        dst = self.r_got.at[lax.rem(j, RING), index]
        device = self.p.up if to_up else self.p.down
        return remote(self.acc.at[j, a, self.message], dst, self.all_s.at[1 + a], self.ur.at[j, 1 + index], device)

    def yz_copy(self, j, a):
        dst = self.yz_got.at[lax.rem(j, RING)]
        return remote(self.acc.at[j, a, self.mid], dst, self.us.at[j], self.ur.at[j, 4], self.p.pair)

    def b_copy(self, j, a, to_up, from_acc):
        src = self.acc if from_acc else self.final
        device = self.p.up if to_up else self.p.down
        send = self.all_s.at[3 + 2 * a + (1 if to_up else 0)]
        return remote(src.at[j, a, self.message], self.final.at[j, a, self.message], send, self.ur.at[j, 5 + a], device)

    def keep_copy(self, j, a):
        return pltpu.make_async_copy(
            self.acc.at[j, a, self.message], self.final.at[j, a, self.message], self.ur.at[j, 5 + a]
        )

    def last_copy(self, j):
        rows = self.final.at[j, :, self.own]
        return remote(rows, rows, self.all_s.at[7], self.all_r.at[0], self.p.pair)

    def tick(self, t):
        p, n, hop = self.p, self.plan.n, self.hop

        def stage(offset, body, cond=None):
            j = t - offset
            ok = (j >= 0) & (j < n)
            if cond is not None:
                ok = ok & cond
            pl.when(ok)(lambda: body(j))

        far = [jnp.abs(p.z - root) for root in self.roots]
        ok, f0 = self.plan.starting(t)
        pl.when(ok)(lambda: self.c_copy(f0).start())

        ok, f1 = self.plan.starting(t - hop)

        @pl.when(ok)
        def _():
            self.c_copy(f1).wait()
            at, slot, j = lax.rem(f1, FEW), self.slot(f1), self.plan.place(f1)
            self.parts[slot, 1 - p.x, p.c, :, :] += self.c_got[at, 1 - p.x]
            self.x_copy(f1).start()
            for a in (0, 1):
                rows = pl.ds(a * (self.unit // 2), self.unit // 2)
                self.acc[j, a] = self.parts[slot, p.x, p.c, rows, :] + self.c_got[at, p.x, rows, :]

        def gather(j):
            @pl.when(self.plan.is_partial(j))
            def _():
                f = self.plan.order(j)
                self.x_copy(f).wait()
                for a in (0, 1):
                    rows = pl.ds(a * (self.unit // 2), self.unit // 2)
                    self.acc[j, a] += self.x_got[self.slot(f), rows, :]

            self.y_copy(j).start()

        stage(2 * hop, gather)

        def own_half(j):
            self.y_copy(j).wait_recv()
            self.acc[j, :, self.own, :] += self.y_got[lax.rem(j, RING)]

        stage(self.at_y, own_half)

        for a in (0, 1):
            root = self.roots[a]
            above, below, here = p.z > root, p.z < root, p.z == root

            def reduce(j, a=a, root=root, above=above, below=below, here=here):
                def take(index):
                    self.r_copy(j, a, True, index).wait_recv()
                    self.acc[j, a, self.message, :] += self.r_got[lax.rem(j, RING), index]

                pl.when(((p.z >= root) & p.has_up) | (below & p.has_down))(lambda: take(a))
                pl.when(here & p.has_down)(lambda: take(2))
                pl.when(above)(lambda: self.r_copy(j, a, False, a).start())
                pl.when(p.z < root - 1)(lambda: self.r_copy(j, a, True, a).start())
                pl.when(p.z == root - 1)(lambda: self.r_copy(j, a, True, 2).start())
                pl.when(here)(lambda: self.yz_copy(j, a).start())

            stage(self.at_y + (self.reach - far[a]) * hop, reduce)

        for a in (0, 1):
            root = self.roots[a]
            above, below = p.z > root, p.z < root

            def forward(j, a=a, above=above, below=below):
                self.b_copy(j, a, True, False).wait_recv()
                pl.when(above & p.has_up)(lambda: self.b_copy(j, a, True, False).start())
                pl.when(below & p.has_down)(lambda: self.b_copy(j, a, False, False).start())

            stage(self.at_final + far[a] * hop, forward, above | below)

            def settle(j, a=a):
                self.yz_copy(j, a).wait()
                self.acc[j, a, self.mid, :] += self.yz_got[lax.rem(j, RING)]
                pl.when(p.has_up)(lambda: self.b_copy(j, a, True, True).start())
                pl.when(p.has_down)(lambda: self.b_copy(j, a, False, True).start())
                self.keep_copy(j, a).start()

            stage(self.at_final, settle, p.z == root)

        def last(j):
            for a in (0, 1):
                pl.when(p.z == self.roots[a])(lambda a=a: self.keep_copy(j, a).wait())
            self.last_copy(j).start()

        stage(self.at_final + jnp.maximum(far[0], far[1]) * hop, last)

    def drain(self):
        p = self.p
        message, own, others = self.final.at[:, 0, self.message], self.final.at[:, :, self.own], self.final.at[:, :, self.others]

        def sent(index, ref):
            remote(ref, ref, self.all_s.at[index], self.all_r.at[0], p.pair).wait_send()

        sent(0, others)
        for a in (0, 1):
            root = self.roots[a]
            pl.when(p.z != root)(lambda a=a: sent(1 + a, message))
            pl.when((p.z >= root) & p.has_up)(lambda a=a: sent(4 + 2 * a, message))
            pl.when((p.z <= root) & p.has_down)(lambda a=a: sent(3 + 2 * a, message))
        sent(7, own)
        remote(own, others, self.all_s.at[7], self.all_r.at[0], p.pair).wait_recv()


def exchange_scratch(plan, unit, lanes):
    slots = plan.partial + 1
    return dict(
        parts=pltpu.VMEM((slots, 2, 2, unit, lanes), f32),
        c_got=pltpu.VMEM((FEW, 2, unit, lanes), f32),
        x_got=pltpu.VMEM((slots, unit, lanes), f32),
        y_got=pltpu.VMEM((RING, 2, unit // 8, lanes), f32),
        r_got=pltpu.VMEM((RING, 3, 3 * unit // 8, lanes), f32),
        yz_got=pltpu.VMEM((RING, unit // 4, lanes), f32),
        acc=pltpu.VMEM((plan.n, 2, unit // 2, lanes), f32),
        fs=pltpu.SemaphoreType.DMA((plan.partials, 2)),
        fr=pltpu.SemaphoreType.DMA((plan.partials, 2)),
        us=pltpu.SemaphoreType.DMA((plan.n,)),
        ur=pltpu.SemaphoreType.DMA((plan.n, 7)),
        all_s=pltpu.SemaphoreType.DMA((8,)),
        all_r=pltpu.SemaphoreType.DMA((1,)),
    )


SMALL = ("cb", "g1", "s1", "vb", "g2", "s2", "ub")
SMALL_ROWS = 40
NEAR_AT, FAR_AT, TABLE_AT = 0, 16, 32
CW = 4
BUBBLE = 2
FIRST_TICK = 1
TURNS, LEAD = 4, 8


def backward_kernel(dims, names, plan, *refs):
    windows, base, d, ff, taps, line, unit = dims
    rows = windows * base
    blocks = ff // d
    lanes = d // SEQ
    half = taps // 2
    r = Refs(names, refs)
    p = Place(line)
    per = d // unit
    smalls = 2 * per * blocks

    def loop(n, body):
        def run(i, carry):
            body(i)
            return carry

        lax.fori_loop(0, n, run, 0)

    def live(w):
        where = p.s * base + lax.broadcasted_iota(jnp.int32, (base, 1), 0)
        return where < r.lengths[w]

    def window(w):
        return pl.ds(pl.multiple_of(w * base, base), base)

    which = {name: i for i, name in enumerate(SAVED)}

    def load(name, side):
        return pltpu.make_async_copy(r.of(side, name), getattr(r, name), r.lsem.at[which[name]])

    def load_h(side):
        return pltpu.make_async_copy(r.of(side, "full"), r.h, r.lsem.at[len(SAVED)])

    def load_conv(side, k, i):
        at = lax.rem(i, CW)
        return pltpu.make_async_copy(r.of(side, "conv").at[k], r.cw.at[at], r.csem.at[at])

    def wide_loads(side, b, slot):
        wide = ff // SEQ
        got = []
        for q in range(SEQ):
            at = pl.ds(pl.multiple_of(q * wide + b * lanes, lanes), lanes)
            put = pl.ds(q * lanes, lanes)
            got.append(pltpu.make_async_copy(r.of(side, "up").at[:, at], r.uw.at[slot, :, put], r.wsem.at[slot, q]))
            got.append(
                pltpu.make_async_copy(r.of(side, "down").at[at, :], r.vw.at[slot, put, :], r.wsem.at[slot, SEQ + q])
            )
        return got

    def start(side, *which_names):
        for name in which_names:
            load(name, side).start()

    def wait(side, *which_names):
        for name in which_names:
            load(name, side).wait()

    cot = pltpu.make_async_copy(r.cotangent, r.dy, r.lsem.at[len(SAVED) + 1])
    cot.start()
    start("far", "n2", "rs2", "mid")
    for b in (0, 1):
        for copy in wide_loads("far", b, b):
            copy.start()
    start("far", "gp", "hid_h", "hid_l", "n1", "gr1")
    load_h("far").start()
    for i in range(CW):
        load_conv("far", i, i).start()

    ex = Exchange(p, plan, unit, r)
    r.sums[...] = jnp.zeros(r.sums.shape, f32)
    r.parts[smalls, :, :, SMALL_ROWS:, :] = jnp.zeros((2, 2, unit - SMALL_ROWS, lanes), f32)

    @pl.when(p.s == 0)
    def _():
        r.dp[:, 0:HALO, :] = jnp.zeros((windows, HALO, d), f32)
        r.dw[:, 0:base, :] = jnp.zeros((windows, base, d), f32)

    @pl.when(p.s == SEQ - 1)
    def _():
        r.dp[:, HALO + base :, :] = jnp.zeros((windows, HALO, d), f32)
        r.dw[:, 2 * base :, :] = jnp.zeros((windows, base, d), f32)

    far_pad = half * SECOND_DILATION
    for ref, pad in ((r.dq_near, HALO), (r.dq_far, far_pad)):
        ref[:, 0:pad, :] = jnp.zeros((windows, pad, lanes), f32)
        ref[:, pad + SEQ * base :, :] = jnp.zeros((windows, pad, lanes), f32)

    p.greet(True)

    def add(kind, v):
        r.sums[kind] += jnp.sum(v.reshape(v.shape[0] // 8, 8, d), axis=0)

    def ffn_norm_back(side, at0):
        def body(w):
            at = window(w)
            dy = r.dy[at, :]
            if side == "far":
                dy = jnp.where(live(w), dy, 0.0)
            n = r.n2[at, :]
            add(at0 + 4, dy * n)
            add(at0 + 5, dy)
            dn = dy * r.of(side, "g2")[...]
            rs = r.rs2[at, 0:1]
            df = rs * (dn - row_mean(dn) - n * row_mean(dn * n))
            add(at0 + 3, df)
            h, l = split(df)
            r.df_h[at, :] = h
            r.df_l[at, :] = l
            r.dmid[at, :] = dy
            mh, ml = split(r.mid[at, :])
            r.mid_h[at, :] = mh
            r.mid_l[at, :] = ml

        loop(windows, body)

    def put_units(j, v):
        for i in range(per):
            for q in range(SEQ):
                r.parts[j + i, q // 2, q % 2, :, :] = v[i * unit : (i + 1) * unit, q * lanes : (q + 1) * lanes]

    def ffn_back(b, at0):
        slot = lax.rem(b, 2)
        for copy in wide_loads("far", b, slot):
            copy.wait()
        r.tmp[...] = dot3((r.df_h[...], r.df_l[...]), split(r.vw[slot]), NT)

        def act(i):
            at = pl.ds(pl.multiple_of(i * ROWS, ROWS), ROWS)
            dz = r.tmp[at, :] * r.gp[b, at, :]
            add(at0 + 6 + b, dz)
            h, l = split(dz)
            r.dz_h[at, :] = h
            r.dz_l[at, :] = l

        loop(rows // ROWS, act)
        r.dmid[...] += dot3((r.dz_h[...], r.dz_l[...]), split(r.uw[slot]), NT)

    def ffn_weights(b):
        put_units(2 * per * b, dot3((r.hid_h[b], r.hid_l[b]), (r.df_h[...], r.df_l[...]), TN))
        put_units(2 * per * b + per, dot3((r.mid_h[...], r.mid_l[...]), (r.dz_h[...], r.dz_l[...]), TN))

    def conv_norm_back(side, at0, put):
        def body(w):
            at = window(w)
            dmid, n = r.dmid[at, :], r.n1[at, :]
            add(at0 + 1, dmid * n)
            add(at0 + 2, dmid)
            dn = dmid * r.of(side, "g1")[...]
            dconv = r.gr1[at, :] * (dn - row_mean(dn) - n * row_mean(dn * n))
            add(at0, dconv)
            put(w, dconv)

        loop(windows, body)

    xs, xr = r.ssem, r.rsem

    def quarter_copies(src, at, pad, dq, sem):
        put = pl.ds(pl.multiple_of(pad + p.s * base, 8), base)
        got = []
        for i, s in enumerate((p.across_s, p.diag_s, p.sib_s)):
            cols = pl.ds(pl.multiple_of(s * lanes, lanes), lanes)
            mine = src.at[:, pl.ds(at, base), cols]
            got.append(remote(mine, dq.at[:, put, :], xs.at[sem + i], xr.at[sem + i], (p.w, s)))
        return got

    def keep_quarter(src, at, pad, dq):
        cols = pl.ds(pl.multiple_of(p.s * lanes, lanes), lanes)
        dq[:, pl.ds(pl.multiple_of(pad + p.s * base, 8), base), :] = src[:, at : at + base, cols]

    def weight_back(dq, pad, dilation, at, w, lo, hi):
        left = split(r.h[:, pl.ds(w, 1), :, :].reshape(SEQ * base, d))
        right = [
            dq[w, pad - (k - half) * dilation : pad - (k - half) * dilation + SEQ * base, :] for k in range(lo, hi)
        ]
        v = dot3(left, split(jnp.concatenate(right, axis=1)), TN)

        def put(first):
            for k in range(lo, hi):
                for i in range(2 * per):
                    piece = v[i * (unit // 2) : (i + 1) * (unit // 2), (k - lo) * lanes : (k - lo + 1) * lanes]
                    j = at(k * per + i // 2)
                    if first:
                        r.acc[j, i % 2] = piece
                    else:
                        r.acc[j, i % 2] += piece

        pl.when(w == 0)(lambda: put(True))
        pl.when(w > 0)(lambda: put(False))

    groups = ((0, half + 1), (half + 1, taps))
    own_rows = pl.ds(base, base)

    def block_next():
        return remote(r.dw.at[:, own_rows], r.dw.at[:, pl.ds(0, base)], xs.at[0], xr.at[0], p.next)

    def block_prev():
        return remote(r.dw.at[:, own_rows], r.dw.at[:, pl.ds(2 * base, base)], xs.at[1], xr.at[1], p.prev)

    def far_quarters():
        return quarter_copies(r.dw, base, far_pad, r.dq_far, 2)

    def halo_next():
        return remote(r.dp.at[:, pl.ds(base, HALO)], r.dp.at[:, pl.ds(0, HALO)], xs.at[5], xr.at[5], p.next)

    def halo_prev():
        return remote(r.dp.at[:, pl.ds(HALO, HALO)], r.dp.at[:, pl.ds(HALO + base, HALO)], xs.at[6], xr.at[6], p.prev)

    def near_quarters():
        return quarter_copies(r.dp, HALO, HALO, r.dq_near, 7)

    def far_norm():
        wait("far", "n1", "gr1")

        def put(w, dconv):
            r.dw[w, base : 2 * base, :] = dconv
            h, l = split(dconv)
            r.dw_h[w, base : 2 * base, :] = h
            r.dw_l[w, base : 2 * base, :] = l

        conv_norm_back("far", FAR_AT, put)
        for copy in far_quarters():
            copy.start()
        pl.when(p.has_next)(lambda: block_next().start())
        pl.when(p.has_prev)(lambda: block_prev().start())
        start("near", "n2", "rs2", "mid", "gp", "hid_h", "hid_l", "n1", "gr1")
        keep_quarter(r.dw, base, far_pad, r.dq_far)
        r.tmp[...] = jnp.zeros((rows, d), f32)

    def far_tap(k):
        at = pl.ds(pl.multiple_of(base - (k - half) * SECOND_DILATION, SECOND_DILATION), base)
        lhs = (r.dw_h[:, at, :].reshape(rows, d), r.dw_l[:, at, :].reshape(rows, d))
        load_conv("far", k, k).wait()
        r.tmp[...] += dot3(lhs, split(r.cw[lax.rem(k, CW)]), NT)
        pl.when(k + CW < taps)(lambda: load_conv("far", k + CW, k + CW).start())
        pl.when(k + CW >= taps)(lambda: load_conv("near", k + CW - taps, k + CW).start())

    def far_halo():
        pl.when(p.has_prev)(lambda: block_next().wait_recv())
        pl.when(p.has_next)(lambda: block_prev().wait_recv())

        def halves(w):
            for at in (0, 2 * base):
                h, l = split(r.dw[w, at : at + base, :])
                r.dw_h[w, at : at + base, :] = h
                r.dw_l[w, at : at + base, :] = l

        loop(windows, halves)

    def far_end():
        def dx(w):
            at = window(w)
            r.dy[at, :] = r.dmid[at, :] + jnp.where(live(w), r.tmp[at, :], 0.0)

        loop(windows, dx)
        wait("near", "n2", "rs2", "mid", "gp", "hid_h", "hid_l")
        ffn_norm_back("near", NEAR_AT)

    def near_norm():
        wait("near", "n1", "gr1")

        def put(w, dconv):
            r.dp[w, HALO : HALO + base, :] = dconv

        conv_norm_back("near", NEAR_AT, put)
        pl.when(p.has_next)(lambda: halo_next().start())
        pl.when(p.has_prev)(lambda: halo_prev().start())
        for copy in near_quarters():
            copy.start()
        keep_quarter(r.dp, HALO, HALO, r.dq_near)

    def near_halo():
        pl.when(p.has_prev)(lambda: halo_next().wait_recv())
        pl.when(p.has_next)(lambda: halo_prev().wait_recv())

    def near_tap(k):
        at = HALO - (k - half) * FIRST_DILATION
        lhs = split(r.dp[:, at : at + base, :].reshape(rows, d))
        load_conv("near", k, taps + k).wait()
        v = dot3(lhs, split(r.cw[(taps + k) % CW]), NT)
        if k == 0:
            r.tmp[...] = v
        else:
            r.tmp[...] += v
        if k + CW < taps:
            load_conv("near", k + CW, taps + k + CW).start()

    def input_grad():
        return pltpu.make_async_copy(r.dy, r.input_grad, r.lsem.at[len(SAVED) + 1])

    def near_end():
        def dx(w):
            at = window(w)
            v = r.dmid[at, :] + jnp.where(live(w), r.tmp[at, :], 0.0)
            r.dy[at, :] = v
            v = jnp.sum(v.reshape(base // 8, 8, d), axis=0)
            species = r.species[w]
            for kind in range(SMALL_ROWS - TABLE_AT):
                r.sums[TABLE_AT + kind] += jnp.where(species == kind, v, 0.0)

        loop(windows, dx)
        input_grad().start()
        small = jnp.sum(r.sums[...], axis=1)
        for q in range(SEQ):
            r.parts[smalls, q // 2, q % 2, 0:SMALL_ROWS, :] = small[:, q * lanes : (q + 1) * lanes]

    cot.wait()
    wait("far", "n2", "rs2", "mid")
    ffn_norm_back("far", FAR_AT)
    wait("far", "gp", "hid_h", "hid_l")

    at = 0

    def take(n):
        nonlocal at
        at += n
        return at - n

    far_ffn = take(2 * blocks)
    far_norm_at = take(1)
    take(BUBBLE)
    far_weights = take(len(groups) * windows)
    far_taps = take(-(-taps // 2))
    far_end_at = take(1)
    near_ffn = take(2 * blocks)
    near_norm_at = take(1)
    take(1)
    near_taps = take(-(-taps // 2))
    near_end_at = take(1)
    near_weights = take(len(groups) * windows)

    def step(i, carry):
        def when(first, n, body, every=1, part=0):
            on = (i >= first) & (i < first + n)
            if every > 1:
                on = on & (lax.rem(i - first, every) == part)
            pl.when(on)(lambda: body(lax.div(i - first, every)))

        def either(first, second, n, part, body):
            far = (i >= first) & (i < first + n)
            near = (i >= second) & (i < second + n)
            m = jnp.where(near, i - second, i - first)
            pl.when((far | near) & (lax.rem(m, 2) == part))(lambda: body(near, lax.div(m, 2)))

        def ffn_step(near, b):
            ffn_back(b, jnp.where(near, NEAR_AT, FAR_AT))

            @pl.when((b < blocks - 2) & near)
            def _():
                for copy in wide_loads("near", b + 2, lax.rem(b, 2)):
                    copy.start()

            @pl.when((b < blocks - 2) & jnp.logical_not(near))
            def _():
                for copy in wide_loads("far", b + 2, lax.rem(b, 2)):
                    copy.start()

            @pl.when((b >= blocks - 2) & jnp.logical_not(near))
            def _():
                for copy in wide_loads("near", b - (blocks - 2), lax.rem(b, 2)):
                    copy.start()

        either(far_ffn, near_ffn, 2 * blocks, 0, ffn_step)
        either(far_ffn, near_ffn, 2 * blocks, 1, lambda near, b: ffn_weights(b))
        when(far_norm_at, 1, lambda _: far_norm())

        @pl.when(i == far_weights)
        def _():
            for copy in far_quarters():
                copy.wait()
            load_h("far").wait()

        for g, (lo, hi) in enumerate(groups):
            when(
                far_weights,
                len(groups) * windows,
                lambda w, lo=lo, hi=hi: weight_back(r.dq_far, far_pad, SECOND_DILATION, plan.far_whole_at, w, lo, hi),
                len(groups),
                g,
            )

        @pl.when(i == far_taps)
        def _():
            load_h("near").start()
            far_halo()

        def two_taps(m):
            far_tap(2 * m)
            pl.when(2 * m + 1 < taps)(lambda: far_tap(2 * m + 1))

        when(far_taps, -(-taps // 2), two_taps)
        when(far_end_at, 1, lambda _: far_end())
        when(near_norm_at, 1, lambda _: near_norm())
        pl.when(i == near_taps)(near_halo)
        for k in range(taps):
            when(near_taps + k // 2, 1, lambda _, k=k: near_tap(k))
        when(near_end_at, 1, lambda _: near_end())

        @pl.when(i == near_weights)
        def _():
            for copy in near_quarters():
                copy.wait()
            load_h("near").wait()

        for g, (lo, hi) in enumerate(groups):
            when(
                near_weights,
                len(groups) * windows,
                lambda w, lo=lo, hi=hi: weight_back(
                    r.dq_near, HALO, FIRST_DILATION, lambda m: plan.near_whole + m, w, lo, hi
                ),
                len(groups),
                g,
            )
        ex.tick(i - FIRST_TICK)
        return carry

    lax.fori_loop(0, max(at, ex.ticks + FIRST_TICK), step, 0)
    ex.drain()

    @pl.when(p.has_next)
    def _():
        halo_next().wait_send()
        block_next().wait_send()

    @pl.when(p.has_prev)
    def _():
        halo_prev().wait_send()
        block_prev().wait_send()

    input_grad().wait()


def backward(line, lengths, species, table, cotangent, fulls, saved, near, far):
    windows, base, d = cotangent.shape
    taps, ff = near[0].shape[0], near[4].shape[1]
    rows, blocks, lanes = windows * base, ff // d, d // SEQ
    unit, hop = 256, (2 if line <= 4 else 1)
    per = d // unit
    plan = Plan(2 * per * blocks, taps * per, TURNS, LEAD, hop)
    n = plan.n
    smem = pl.BlockSpec(memory_space=pltpu.SMEM)
    vmem = pl.BlockSpec(memory_space=pltpu.VMEM)
    hbm = pl.BlockSpec(memory_space=pl.ANY)
    names, args, specs = ["lengths", "species", "cotangent"], [lengths, species, cotangent.reshape(rows, d)], [smem, smem, hbm]
    for side, block, full, kept in zip(("near", "far"), (near, far), fulls, saved, strict=True):
        names += [side + "_" + v for v in ("full", "conv", "up", "down") + SAVED + ("g1", "g2")]
        args += [full, block[0], block[4], block[6], *kept, block[2].reshape(1, -1), block[8].reshape(1, -1)]
        specs += [hbm] * (4 + len(SAVED)) + [vmem] * 2
    names += ["input_grad", "final"]
    scratch = {name: pltpu.VMEM(*v) for name, v in saved_shapes(rows, d, ff).items()}
    for name in ("dy", "dmid", "tmp"):
        scratch[name] = pltpu.VMEM((rows, d), f32)
    for name in ("mid_h", "mid_l", "df_h", "df_l", "dz_h", "dz_l"):
        scratch[name] = pltpu.VMEM((rows, d), bf16)
    scratch.update(
        h=pltpu.VMEM((SEQ, windows, base, d), f32),
        cw=pltpu.VMEM((CW, d, d), f32),
        uw=pltpu.VMEM((2, d, d), f32),
        vw=pltpu.VMEM((2, d, d), f32),
        dp=pltpu.VMEM((windows, base + 2 * HALO, d), f32),
        dw=pltpu.VMEM((windows, 3 * base, d), f32),
        dw_h=pltpu.VMEM((windows, 3 * base, d), bf16),
        dw_l=pltpu.VMEM((windows, 3 * base, d), bf16),
        dq_near=pltpu.VMEM((windows, SEQ * base + 2 * HALO, lanes), f32),
        dq_far=pltpu.VMEM((windows, SEQ * base + taps // 2 * 2 * SECOND_DILATION, lanes), f32),
        sums=pltpu.VMEM((SMALL_ROWS, 8, d), f32),
        lsem=pltpu.SemaphoreType.DMA((len(SAVED) + 2,)),
        csem=pltpu.SemaphoreType.DMA((CW,)),
        wsem=pltpu.SemaphoreType.DMA((2, 2 * SEQ)),
        ssem=pltpu.SemaphoreType.DMA((10,)),
        rsem=pltpu.SemaphoreType.DMA((10,)),
    )
    scratch.update(exchange_scratch(plan, unit, lanes))
    names += list(scratch)
    input_grad, final = pl.pallas_call(
        functools.partial(backward_kernel, (windows, base, d, ff, taps, line, unit), names, plan),
        out_shape=[jax.ShapeDtypeStruct((rows, d), f32), jax.ShapeDtypeStruct((n, 2, unit // 2, lanes), f32)],
        in_specs=specs,
        out_specs=[hbm, hbm],
        scratch_shapes=list(scratch.values()),
        compiler_params=pltpu.CompilerParams(
            collective_id=1, has_side_effects=True, vmem_limit_bytes=64 * 1024 * 1024 - 65536
        ),
        name="backward",
    )(*args)

    final = final.reshape(n, unit, lanes)

    def grads(v, conv, small):
        v = v.reshape(blocks, 2, d, lanes)
        down = jnp.transpose(v[:, 0].reshape(blocks, SEQ, lanes, lanes), (1, 0, 2, 3)).reshape(ff, lanes)
        up = jnp.transpose(v[:, 1], (1, 0, 2)).reshape(d, ff // SEQ)
        one = dict(zip(SMALL, small, strict=False))
        ub = small[len(SMALL) - 1 : len(SMALL) - 1 + blocks].reshape(-1)
        return (conv.reshape(taps, d, lanes), one["cb"], one["g1"], one["s1"], up, ub, down, one["vb"], one["g2"], one["s2"])

    small = final[plan.near_whole - 1]
    partial = [f if f < plan.alone else plan.alone + 2 * (f - plan.alone) + 1 for f in range(plan.partial)]
    whole = [plan.far_whole_at(i) for i in range(plan.whole)]
    far_grads = grads(
        jnp.stack([final[j] for j in partial]), jnp.stack([final[j] for j in whole]), small[FAR_AT:TABLE_AT]
    )
    near_grads = grads(final[plan.second : plan.near_whole - 1], final[plan.near_whole :], small[NEAR_AT:FAR_AT])
    table_grad = small[TABLE_AT : TABLE_AT + table.shape[0]]
    return input_grad.reshape(cotangent.shape), table_grad, near_grads, far_grads


def on_device(inputs, species, lengths, species_table, *rest):
    near, far, cotangent = rest[:10], rest[10:20], rest[20]
    line = lax.axis_size("win") // 2
    output, near_full, far_full, near_saved, far_saved = forward(
        line, lengths, species, species_table, inputs, near, far
    )
    input_grad, table_grad, near_grads, far_grads = backward(
        line, lengths, species, species_table, cotangent, (near_full, far_full), (near_saved, far_saved), near, far
    )
    return (output, input_grad, table_grad, *near_grads, *far_grads)


def solution(mesh):
    split_windows = P("win", "seq", None)
    block_grads = (P(None, None, "seq"), P("seq"), P("seq"), P("seq"), P(None, "seq"), P("seq"), P(None, "seq"))
    block_grads += (P("seq"), P("seq"), P("seq"))
    return jax.shard_map(
        on_device,
        mesh=mesh,
        in_specs=(split_windows, P("win"), P("win")) + (P(),) * 21 + (split_windows,),
        out_specs=(split_windows, split_windows, P(None, "seq")) + block_grads + block_grads,
        check_vma=False,
    )
```

```python
import functools

import jax
import jax.numpy as jnp
from jax import lax
from jax.experimental import pallas as pl
from jax.experimental.pallas import tpu as pltpu
from jax.sharding import PartitionSpec as P

FIRST_DILATION = 1
SECOND_DILATION = 32
EPS = 1e-05
ROWS = 32
HALO = 8
SEQ = 4
f32, bf16 = jnp.float32, jnp.bfloat16
MESH_ID = pl.DeviceIdType.MESH


def split(v):
    high = v.astype(bf16)
    return high, (v - high.astype(f32)).astype(bf16)


def dot(left, right, dims):
    return lax.dot_general(left, right, (dims, ((), ())), preferred_element_type=f32)


def dot3(left, right, dims=((1,), (0,))):
    (lh, ll), (rh, rl) = left, right
    return dot(lh, rh, dims) + (dot(lh, rl, dims) + dot(ll, rh, dims))


NT = ((1,), (1,))
TN = ((0,), (0,))


def gauss(z):
    size = jnp.abs(z)
    t = 1.0 / (1.0 + (0.3275911 * 0.7071067811865476) * size)
    e = jnp.exp(-0.5 * z * z)
    poly = 0.5 * 1.061405429
    for term in (-1.453152027, 1.421413741, -0.284496736, 0.254829592):
        poly = poly * t + 0.5 * term
    tail = poly * t * e
    return jnp.where(z >= 0, 1.0 - tail, tail), (z * 0.3989422804014327) * e


def row_mean(v):
    return jnp.mean(v, axis=-1, keepdims=True)


def remote(src, dst, send, recv, device):
    return pltpu.make_async_remote_copy(
        src_ref=src, dst_ref=dst, send_sem=send, recv_sem=recv, device_id=device, device_id_type=MESH_ID
    )


class Refs:
    def __init__(self, names, refs):
        for name, ref in zip(names, refs, strict=True):
            setattr(self, name, ref)

    def of(self, side, name):
        return getattr(self, side + "_" + name)


class Place:
    def __init__(self, line):
        w, s = lax.axis_index("win"), lax.axis_index("seq")
        self.w, self.s, self.line = w, s, line
        self.z, self.y = lax.div(w, 2), lax.rem(w, 2)
        self.x, self.c = lax.div(s, 2), lax.rem(s, 2)
        self.sib_s = 2 * self.x + 1 - self.c
        self.across_s = 2 * (1 - self.x) + self.c
        self.diag_s = SEQ - 1 - s
        self.sib, self.across, self.diag = (w, self.sib_s), (w, self.across_s), (w, self.diag_s)
        self.pair = (2 * self.z + 1 - self.y, s)
        self.up, self.down = (w + 2, s), (w - 2, s)
        self.next, self.prev = (w, s + 1), (w, s - 1)
        self.has_up, self.has_down = self.z < line - 1, self.z > 0
        self.has_next, self.has_prev = s < SEQ - 1, s > 0
        self.inner = self.c != self.x

    def greet(self, whole):
        barrier = pltpu.get_barrier_semaphore()

        def signal(device):
            pl.semaphore_signal(barrier, inc=1, device_id=device, device_id_type=MESH_ID)

        for device in (self.sib, self.across, self.diag):
            signal(device)
        if not whole:
            pl.semaphore_wait(barrier, 3)
            return
        signal(self.pair)
        pl.when(self.has_up)(lambda: signal(self.up))
        pl.when(self.has_down)(lambda: signal(self.down))
        pl.semaphore_wait(barrier, 4 + self.has_up.astype(jnp.int32) + self.has_down.astype(jnp.int32))


AHEAD = 4
LARGE, SMALLER = ("hid_h", "hid_l", "gp"), ("mid", "n1", "gr1", "n2", "rs2")
SAVED = ("mid", "n1", "gr1", "n2", "rs2", "hid_h", "hid_l", "gp")


def saved_shapes(rows, d, ff):
    blocks = ff // d
    return dict(
        mid=((rows, d), f32),
        n1=((rows, d), f32),
        gr1=((rows, d), f32),
        n2=((rows, d), f32),
        rs2=((rows, 128), f32),
        hid_h=((blocks, rows, d), bf16),
        hid_l=((blocks, rows, d), bf16),
        gp=((blocks, rows, d), f32),
    )


def ff_columns(ref, b, d, parts, lanes):
    wide = d * parts // SEQ
    return [ref[:, pl.ds(pl.multiple_of(q * wide + b * lanes, lanes), lanes)] for q in range(SEQ)]


def ff_rows(ref, b, d, parts, lanes):
    wide = d * parts // SEQ
    return [ref[pl.ds(pl.multiple_of(q * wide + b * lanes, lanes), lanes), :] for q in range(SEQ)]


def forward_kernel(dims, *refs):
    windows, base, d, ff, taps, line = dims
    rows = windows * base
    blocks = ff // d
    lanes = d // SEQ
    names = ["lengths", "species", "table", "inputs"]
    weights = ("conv", "up", "down")
    vectors = ("cb", "g1", "s1", "ub", "vb", "g2", "s2")
    for side in ("near", "far"):
        names += [side + "_" + v for v in weights + vectors]
    names += ["output", "near_full", "far_full"]
    for side in ("near", "far"):
        names += [side + "_out_" + v for v in SAVED]
    for side in ("near", "far"):
        names += [side + "_" + v for v in SAVED]
    names += ["cw", "uw", "vw", "x", "acc", "zb", "mid_h", "mid_l", "hp", "hq", "hq_h", "hq_l", "own"]
    names += ["own2", "out_buf", "csem", "wsem", "osem", "bsem", "gsem", "ssem", "rsem"]
    r = Refs(names, refs)
    p = Place(line)

    def conv_weights(side, k):
        return pltpu.make_async_copy(r.of(side, "conv").at[k], r.cw.at[k], r.csem.at[k])

    def wide_weights(side, i):
        src, dst = (("up", r.uw), ("down", r.vw))[i]
        return pltpu.make_async_copy(r.of(side, src), dst, r.wsem.at[i])

    order = [taps // 2] + [k for k in range(taps) if k != taps // 2]
    for k in order[:AHEAD]:
        conv_weights("near", k).start()

    def live(w):
        where = p.s * base + lax.broadcasted_iota(jnp.int32, (base, 1), 0)
        return where < r.lengths[w]

    def window(w):
        return pl.ds(pl.multiple_of(w * base, base), base)

    def step_rows(i):
        return pl.ds(pl.multiple_of(i * ROWS, ROWS), ROWS)

    def loop(n, body):
        def run(i, carry):
            body(i)
            return carry

        lax.fori_loop(0, n, run, 0)

    def begin(w):
        v = r.inputs[w] + r.table[pl.ds(r.species[w], 1), :]
        r.x[window(w), :] = v
        h = jnp.where(live(w), v, 0.0)
        r.hp[w, HALO : HALO + base, :] = h
        r.own[w] = h

    loop(windows, begin)

    @pl.when(p.s == 0)
    def _():
        r.hp[:, 0:HALO, :] = jnp.zeros((windows, HALO, d), f32)
        r.hq[:, 0:base, :] = jnp.zeros((windows, base, d), f32)

    @pl.when(p.s == SEQ - 1)
    def _():
        r.hp[:, HALO + base :, :] = jnp.zeros((windows, HALO, d), f32)
        r.hq[:, 2 * base :, :] = jnp.zeros((windows, base, d), f32)

    p.greet(False)
    ssem, rsem = r.ssem, r.rsem

    def halo_next():
        return remote(
            r.hp.at[:, pl.ds(base, HALO)], r.hp.at[:, pl.ds(0, HALO)], ssem.at[0], rsem.at[0], p.next
        )

    def halo_prev():
        return remote(
            r.hp.at[:, pl.ds(HALO, HALO)], r.hp.at[:, pl.ds(HALO + base, HALO)], ssem.at[1], rsem.at[1], p.prev
        )

    pl.when(p.has_next)(lambda: halo_next().start())
    pl.when(p.has_prev)(lambda: halo_prev().start())

    other_inner = (p.w, jnp.where(p.x == 0, 2, 1))
    first_other = 2 * (1 - p.x)
    other_outer = jnp.where(p.x == 0, 3, 0)

    def bulk_own(full):
        return r.own if full == "near" else r.own2

    def bulk_keep(full, at):
        return pltpu.make_async_copy(bulk_own(full), r.of(full, "full").at[p.s], ssem.at[at])

    def bulk_sib(full, at, block, src=None):
        return remote(
            bulk_own(full) if src is None else src, r.of(full, "full").at[block], ssem.at[at + 1], rsem.at[at + 1], p.sib
        )

    def bulk_across(full, at):
        return remote(bulk_own(full), r.of(full, "full").at[p.s], ssem.at[at + 2], rsem.at[at + 2 + lax.rem(p.s, 2)], other_inner)

    def bulk_relay(full, at, block, i, src=None):
        src = r.of(full, "full").at[block] if src is None else src
        return remote(src, r.of(full, "full").at[block], ssem.at[at + 3 + i], rsem.at[at + 4 + i], p.sib)

    NEAR, FAR = 4, 12
    bulk_keep("near", NEAR).start()
    bulk_sib("near", NEAR, p.s).start()
    bulk_across("near", NEAR).start()

    def near_tap(k, lo, hi):
        at = HALO + (k - taps // 2) * FIRST_DILATION
        return dot3(split(r.hp[lo:hi, at : at + base, :].reshape((hi - lo) * base, d)), split(r.cw[k]))

    def conv_tail(side, lo, hi):
        def body(w):
            at = window(w)
            v = r.acc[at, :] + r.of(side, "cb")[...]
            cdf, zd = gauss(v)
            a = v * cdf
            center = a - row_mean(a)
            rs = lax.rsqrt(row_mean(center * center) + EPS)
            n = center * rs
            mid = r.x[at, :] + (n * r.of(side, "g1")[...] + r.of(side, "s1")[...])
            r.of(side, "n1")[at, :] = n
            r.of(side, "gr1")[at, :] = (cdf + zd) * rs
            r.of(side, "mid")[at, :] = mid
            h, l = split(mid)
            r.mid_h[at, :] = h
            r.mid_l[at, :] = l

        loop(hi - lo, lambda i: body(i + lo))

    def ffn(side, lo, hi):
        part = pl.ds(lo * base, (hi - lo) * base)

        def body(b):
            up = jnp.concatenate(ff_columns(r.uw, b, d, blocks, lanes), axis=1)
            r.zb[part, :] = dot3((r.mid_h[part, :], r.mid_l[part, :]), split(up))
            bias = jnp.concatenate(ff_columns(r.of(side, "ub"), b, d, blocks, lanes), axis=1)

            def act(i):
                at = pl.ds(pl.multiple_of(lo * base + i * ROWS, ROWS), ROWS)
                z = r.zb[at, :] + bias
                cdf, zd = gauss(z)
                h, l = split(z * cdf)
                r.of(side, "hid_h")[b, at, :] = h
                r.of(side, "hid_l")[b, at, :] = l
                r.of(side, "gp")[b, at, :] = cdf + zd

            loop((hi - lo) * base // ROWS, act)
            if hi == windows:
                for name in LARGE:
                    save_part(side, name, b).start()
            down = jnp.concatenate(ff_rows(r.vw, b, d, blocks, lanes), axis=0)
            f = dot3((r.of(side, "hid_h")[b, part, :], r.of(side, "hid_l")[b, part, :]), split(down))

            @pl.when(b == 0)
            def _():
                r.acc[part, :] = f

            @pl.when(b > 0)
            def _():
                r.acc[part, :] += f

        loop(blocks, body)

    def ffn_tail(side, keep, lo, hi):
        def body(w):
            at = window(w)
            f = r.acc[at, :] + r.of(side, "vb")[...]
            center = f - row_mean(f)
            rs = lax.rsqrt(row_mean(center * center) + EPS)
            n = center * rs
            r.of(side, "n2")[at, :] = n
            r.of(side, "rs2")[at, :] = jnp.broadcast_to(rs, (base, 128))
            keep(w, at, r.of(side, "mid")[at, :] + (n * r.of(side, "g2")[...] + r.of(side, "s2")[...]))

        loop(hi - lo, lambda i: body(i + lo))

    which = {name: i for i, name in enumerate(SAVED)}

    def save_sem(side, name):
        return r.osem.at[(0 if side == "near" else len(SAVED)) + which[name]]

    def save(side, name):
        return pltpu.make_async_copy(r.of(side, name), r.of(side, "out_" + name), save_sem(side, name))

    def save_part(side, name, b):
        return pltpu.make_async_copy(
            r.of(side, name).at[b], r.of(side, "out_" + name).at[b], r.bsem.at[0 if side == "near" else 1, which[name], b]
        )

    def block_next(g):
        lo, hi = groups[g]
        at = pl.ds(lo, hi - lo)
        return remote(r.own2.at[at], r.hq.at[at, pl.ds(0, base)], r.gsem.at[0, g, 0], r.gsem.at[1, g, 0], p.next)

    def block_prev(g):
        lo, hi = groups[g]
        at = pl.ds(lo, hi - lo)
        return remote(r.own2.at[at], r.hq.at[at, pl.ds(2 * base, base)], r.gsem.at[0, g, 1], r.gsem.at[1, g, 1], p.prev)

    def middle(w, at, v):
        r.x[at, :] = v
        h = jnp.where(live(w), v, 0.0)
        r.hq[w, base : 2 * base, :] = h
        r.own2[w] = h
        hh, hl = split(h)
        r.hq_h[w, base : 2 * base, :] = hh
        r.hq_l[w, base : 2 * base, :] = hl

    groups = ((0, windows - 1), (windows - 1, windows))
    for g, (lo, hi) in enumerate(groups):
        part = pl.ds(lo * base, (hi - lo) * base)
        for n, k in enumerate(order):
            if g == 0:
                conv_weights("near", k).wait()
                if n + AHEAD < taps:
                    conv_weights("near", order[n + AHEAD]).start()
                if n == taps - AHEAD:
                    for i in (0, 1):
                        wide_weights("near", i).start()
            if g == 0 and n == 1:
                pl.when(p.has_prev)(lambda: halo_next().wait_recv())
                pl.when(p.has_next)(lambda: halo_prev().wait_recv())
            v = near_tap(k, lo, hi)
            if n == 0:
                r.acc[part, :] = v
            else:
                r.acc[part, :] += v
        if hi == windows:
            for k in order:
                conv_weights("far", k).start()
        conv_tail("near", lo, hi)
        if g == 0:
            for i in (0, 1):
                wide_weights("near", i).wait()
        ffn("near", lo, hi)
        if hi == windows:
            for i in (0, 1):
                wide_weights("far", i).start()
        ffn_tail("near", middle, lo, hi)
        pl.when(p.has_next)(lambda g=g: block_next(g).start())
        pl.when(p.has_prev)(lambda g=g: block_prev(g).start())

    bulk_keep("far", FAR).start()
    bulk_sib("far", FAR, p.s).start()
    for name in SMALLER:
        save("near", name).start()

    @pl.when(p.inner)
    def _():
        for i in (0, 1):
            remote(
                r.own, r.near_full.at[first_other + i], ssem.at[NEAR + 2], rsem.at[NEAR + 2 + i], other_inner
            ).wait_recv()
            bulk_relay("near", NEAR, first_other + i, i).start()

    def far_tap(k):
        at = pl.ds(pl.multiple_of(base + (k - taps // 2) * SECOND_DILATION, SECOND_DILATION), base)
        lhs = (r.hq_h[:, at, :].reshape(rows, d), r.hq_l[:, at, :].reshape(rows, d))
        conv_weights("far", k).wait()
        r.acc[...] += dot3(lhs, split(r.cw[k]))

    r.acc[...] = jnp.zeros((rows, d), f32)
    far_tap(taps // 2)
    for g in range(len(groups)):
        pl.when(p.has_prev)(lambda g=g: block_next(g).wait_recv())
        pl.when(p.has_next)(lambda g=g: block_prev(g).wait_recv())

    @pl.when(jnp.logical_not(p.inner))
    def _():
        bulk_across("far", FAR).start()

    def halves(w):
        for at in (0, 2 * base):
            h, l = split(r.hq[w, at : at + base, :])
            r.hq_h[w, at : at + base, :] = h
            r.hq_l[w, at : at + base, :] = l

    loop(windows, halves)

    def keep_inner(at):
        return pltpu.make_async_copy(
            r.hq.at[:, pl.ds(at, base)], r.far_full.at[other_inner[1]], ssem.at[FAR + 2]
        )

    def relay_inner(at):
        return bulk_relay("far", FAR, other_inner[1], 0, r.hq.at[:, pl.ds(at, base)])

    inner_at = pl.multiple_of(jnp.where(p.x == 0, 2 * base, 0), base)

    @pl.when(p.inner)
    def _():
        keep_inner(inner_at).start()
        relay_inner(inner_at).start()

    loop(taps // 2, far_tap)
    loop(taps // 2, lambda i: far_tap(i + taps // 2 + 1))
    conv_tail("far", 0, windows)
    for name in ("mid", "n1", "gr1"):
        save("far", name).start()
    for i in (0, 1):
        wide_weights("far", i).wait()
    ffn("far", 0, windows)

    def finish(w, at, v):
        r.out_buf[at, :] = jnp.where(live(w), v, 0.0)

    ffn_tail("far", finish, 0, windows)
    for name in ("n2", "rs2"):
        save("far", name).start()
    result = pltpu.make_async_copy(r.out_buf, r.output, r.osem.at[2 * len(SAVED)])
    result.start()

    @pl.when(p.inner)
    def _():
        remote(
            r.own, r.far_full.at[other_outer], ssem.at[FAR + 2], rsem.at[FAR + 2 + lax.rem(other_outer, 2)], other_inner
        ).wait_recv()
        bulk_relay("far", FAR, other_outer, 1).start()
        keep_inner(inner_at).wait()
        relay_inner(inner_at).wait_send()
        bulk_relay("far", FAR, other_outer, 1).wait_send()
        for i in (0, 1):
            bulk_relay("near", NEAR, first_other + i, i).wait_send()

    @pl.when(jnp.logical_not(p.inner))
    def _():
        bulk_across("far", FAR).wait_send()
        for full, at in (("near", NEAR), ("far", FAR)):
            for i in (0, 1):
                bulk_relay(full, at, first_other + i, i).wait_recv()

    for full, at in (("near", NEAR), ("far", FAR)):
        bulk_sib(full, at, p.sib_s).wait_recv()
    for full, at in (("near", NEAR), ("far", FAR)):
        bulk_sib(full, at, p.s).wait_send()
        bulk_keep(full, at).wait()
    bulk_across("near", NEAR).wait_send()

    @pl.when(p.has_next)
    def _():
        halo_next().wait_send()
        for g in range(len(groups)):
            block_next(g).wait_send()

    @pl.when(p.has_prev)
    def _():
        halo_prev().wait_send()
        for g in range(len(groups)):
            block_prev(g).wait_send()

    result.wait()
    for side in ("near", "far"):
        for name in SMALLER:
            save(side, name).wait()
        for name in LARGE:
            for b in range(blocks):
                save_part(side, name, b).wait()


def forward(line, lengths, species, table, inputs, near, far):
    windows, base, d = inputs.shape
    taps, ff = near[0].shape[0], near[4].shape[1]
    rows, blocks = windows * base, ff // d
    smem = pl.BlockSpec(memory_space=pltpu.SMEM)
    vmem = pl.BlockSpec(memory_space=pltpu.VMEM)
    hbm = pl.BlockSpec(memory_space=pl.ANY)
    args, specs = [lengths, species, table, inputs], [smem, smem, vmem, vmem]
    for cw, cb, g1, s1, uw, ub, vw, vb, g2, s2 in (near, far):
        args += [cw, uw, vw] + [v.reshape(1, -1) for v in (cb, g1, s1, ub, vb, g2, s2)]
        specs += [hbm] * 3 + [vmem] * 7
    kept = saved_shapes(rows, d, ff)
    full = ((SEQ, windows, base, d), f32)
    outs = [((rows, d), f32), full, full] + 2 * [kept[v] for v in SAVED]
    scratch = 2 * [pltpu.VMEM(*kept[v]) for v in SAVED]
    scratch += [
        pltpu.VMEM((taps, d, d), f32),
        pltpu.VMEM((d, ff), f32),
        pltpu.VMEM((ff, d), f32),
        pltpu.VMEM((rows, d), f32),
        pltpu.VMEM((rows, d), f32),
        pltpu.VMEM((rows, d), f32),
        pltpu.VMEM((rows, d), bf16),
        pltpu.VMEM((rows, d), bf16),
        pltpu.VMEM((windows, base + 2 * HALO, d), f32),
        pltpu.VMEM((windows, 3 * base, d), f32),
        pltpu.VMEM((windows, 3 * base, d), bf16),
        pltpu.VMEM((windows, 3 * base, d), bf16),
        pltpu.VMEM((windows, base, d), f32),
        pltpu.VMEM((windows, base, d), f32),
        pltpu.VMEM((rows, d), f32),
        pltpu.SemaphoreType.DMA((taps,)),
        pltpu.SemaphoreType.DMA((2,)),
        pltpu.SemaphoreType.DMA((2 * len(SAVED) + 1,)),
        pltpu.SemaphoreType.DMA((2, len(SAVED), blocks)),
        pltpu.SemaphoreType.DMA((2, 2, 2)),
        pltpu.SemaphoreType.DMA((20,)),
        pltpu.SemaphoreType.DMA((20,)),
    ]
    got = pl.pallas_call(
        functools.partial(forward_kernel, (windows, base, d, ff, taps, line)),
        out_shape=[jax.ShapeDtypeStruct(*v) for v in outs],
        in_specs=specs,
        out_specs=[hbm] * len(outs),
        scratch_shapes=scratch,
        compiler_params=pltpu.CompilerParams(
            collective_id=0, has_side_effects=True, vmem_limit_bytes=60 * 1024 * 1024
        ),
        name="forward",
    )(*args)
    n = len(SAVED)
    return got[0].reshape(inputs.shape), got[1], got[2], got[3 : 3 + n], got[3 + n :]


RING = 12
FEW = 6
EXCHANGE_REFS = tuple(
    dict(parts=0, c_got=0, x_got=0, y_got=0, r_got=0, yz_got=0, acc=0, final=0, fs=0, fr=0, us=0, ur=0, all_s=0, all_r=0)
)


def line_ring(line, hop):
    return max(RING, hop * (1 + 2 * (line // 2)) + 1)


class Plan:
    def __init__(self, partial, whole, hop, early, whole_tick, later, second_early, second_start, held):
        gap = whole_tick - 2 * hop - early
        self.partial, self.whole, self.hop, self.early, self.gap = partial, whole, hop, early, gap
        self.later, self.second_start, self.held = later, second_start, held
        self.partials = 2 * partial + 1
        self.far_whole = early + gap
        self.shift = gap + whole
        self.before = partial + second_early
        self.near_whole = self.shift + self.before
        self.n = gap + self.partials + 2 * whole
        self.units = self.n - gap

    def at(self, j):
        if isinstance(j, int):
            return j if j < self.early else j - self.gap
        return jnp.where(j < self.early, j, j - self.gap)

    def real(self, j):
        return (j < self.early) | (j >= self.far_whole)

    def is_partial(self, j):
        far_or_first = (j >= self.early + self.shift) & (j < self.near_whole)
        return (j < self.early) | far_or_first | (j >= self.near_whole + self.whole)

    def number(self, j):
        return jnp.where(
            j < self.early, j, jnp.where(j < self.near_whole, j - self.shift, j - self.shift - self.whole)
        )

    def place(self, f):
        if isinstance(f, int):
            return f if f < self.early else f + self.shift + (self.whole if f >= self.before else 0)
        return jnp.where(f < self.early, f, jnp.where(f < self.before, f, f + self.whole) + self.shift)

    def starting(self, t):
        first = (t >= 0) & (t < self.early)
        far = (t >= self.early + self.later) & (t < self.partial + self.later)
        near = (t >= self.second_start) & (t < self.second_start + self.partial + 1)
        return first | far | near, jnp.where(
            first, t, jnp.where(far, t - self.later, t - self.second_start + self.partial)
        )


class Exchange:
    def __init__(self, place, plan, unit, refs):
        self.p, self.plan, self.unit, self.hop = place, plan, unit, plan.hop
        for name in EXCHANGE_REFS:
            setattr(self, name, getattr(refs, name))
        line, hop = place.line, plan.hop
        self.roots = (line // 2 - 1, line // 2)
        self.reach = line // 2
        self.ring = line_ring(line, hop)
        self.at_y = 3 * hop
        self.at_final = self.at_y + (self.reach + 1) * hop
        self.ticks = plan.n + self.at_final + self.reach * hop + 1
        y = place.y
        self.own = pl.ds(pl.multiple_of(y * (3 * unit // 8), 8), unit // 8)
        self.others = pl.ds(pl.multiple_of((1 - y) * (3 * unit // 8), 8), unit // 8)
        self.mid = pl.ds(unit // 8, unit // 4)
        self.message = pl.ds(pl.multiple_of(y * (unit // 8), 8), 3 * unit // 8)

    def slot(self, f):
        return jnp.where(f < self.plan.partial, f, f - self.plan.partial)

    def c_copy(self, f):
        src = self.parts.at[self.slot(f), :, 1 - self.p.c]
        return remote(src, self.c_got.at[lax.rem(f, FEW)], self.fs.at[f, 0], self.fr.at[f, 0], self.p.sib)

    def x_copy(self, f):
        src = self.parts.at[self.slot(f), 1 - self.p.x, self.p.c]
        return remote(src, self.x_got.at[f], self.fs.at[f, 1], self.fr.at[f, 1], self.p.across)

    def y_copy(self, j):
        dst = self.y_got.at[lax.rem(j, RING)]
        return remote(self.acc.at[self.plan.at(j), :, self.others], dst, self.all_s.at[0], self.ur.at[j, 0], self.p.pair)

    def r_copy(self, j, a, to_up, index):
        dst = self.r_got.at[lax.rem(j, self.ring), index]
        device = self.p.up if to_up else self.p.down
        return remote(self.acc.at[self.plan.at(j), a, self.message], dst, self.all_s.at[1 + a], self.ur.at[j, 1 + index], device)

    def yz_copy(self, j, a):
        dst = self.yz_got.at[lax.rem(j, RING)]
        return remote(self.acc.at[self.plan.at(j), a, self.mid], dst, self.us.at[j], self.ur.at[j, 4], self.p.pair)

    def b_copy(self, j, a, to_up, from_acc):
        src = self.acc if from_acc else self.final
        device = self.p.up if to_up else self.p.down
        send = self.all_s.at[3 + 2 * a + (1 if to_up else 0)]
        return remote(src.at[self.plan.at(j), a, self.message], self.final.at[self.plan.at(j), a, self.message], send, self.ur.at[j, 5 + a], device)

    def keep_copy(self, j, a):
        return pltpu.make_async_copy(
            self.acc.at[self.plan.at(j), a, self.message], self.final.at[self.plan.at(j), a, self.message], self.ur.at[j, 5 + a]
        )

    def last_copy(self, j):
        rows = self.final.at[self.plan.at(j), :, self.own]
        return remote(rows, rows, self.all_s.at[7], self.all_r.at[0], self.p.pair)

    def tick(self, t):
        p, n, hop = self.p, self.plan.n, self.hop

        def stage(offset, body, cond=None):
            j = t - offset
            ok = (j >= 0) & (j < n) & self.plan.real(j)
            if cond is not None:
                ok = ok & cond
            pl.when(ok)(lambda: body(j))

        far = [jnp.abs(p.z - root) for root in self.roots]
        ok, f0 = self.plan.starting(t)
        pl.when(ok)(lambda: self.c_copy(f0).start())

        ok, f1 = self.plan.starting(t - hop)

        @pl.when(ok)
        def _():
            self.c_copy(f1).wait()
            at, slot, j = lax.rem(f1, FEW), self.slot(f1), self.plan.place(f1)
            self.parts[slot, 1 - p.x, p.c, :, :] += self.c_got[at, 1 - p.x]
            self.x_copy(f1).start()
            for a in (0, 1):
                rows = pl.ds(a * (self.unit // 2), self.unit // 2)
                self.acc[self.plan.at(j), a] = self.parts[slot, p.x, p.c, rows, :] + self.c_got[at, p.x, rows, :]

        f2 = t - hop - self.plan.later - self.plan.held
        pl.when((f2 >= self.plan.early) & (f2 < self.plan.partial))(lambda: self.x_copy(f2).wait_send())

        def gather(j):
            @pl.when(self.plan.is_partial(j))
            def _():
                f = self.plan.number(j)
                self.x_copy(f).wait_recv()
                pl.when((f < self.plan.early) | (f >= self.plan.partial))(lambda: self.x_copy(f).wait_send())
                for a in (0, 1):
                    rows = pl.ds(a * (self.unit // 2), self.unit // 2)
                    self.acc[self.plan.at(j), a] += self.x_got[f, rows, :]

            self.y_copy(j).start()

        stage(2 * hop, gather)

        def own_half(j):
            self.y_copy(j).wait_recv()
            self.acc[self.plan.at(j), :, self.own, :] += self.y_got[lax.rem(j, RING)]

        stage(self.at_y, own_half)

        for a in (0, 1):
            root = self.roots[a]
            above, below, here = p.z > root, p.z < root, p.z == root

            def reduce(j, a=a, root=root, above=above, below=below, here=here):
                def take(index):
                    self.r_copy(j, a, True, index).wait_recv()
                    self.acc[self.plan.at(j), a, self.message, :] += self.r_got[lax.rem(j, self.ring), index]

                pl.when(((p.z >= root) & p.has_up) | (below & p.has_down))(lambda: take(a))
                pl.when(here & p.has_down)(lambda: take(2))
                pl.when(above)(lambda: self.r_copy(j, a, False, a).start())
                pl.when(p.z < root - 1)(lambda: self.r_copy(j, a, True, a).start())
                pl.when(p.z == root - 1)(lambda: self.r_copy(j, a, True, 2).start())
                pl.when(here)(lambda: self.yz_copy(j, a).start())

            stage(self.at_y + (self.reach - far[a]) * hop, reduce)

        for a in (0, 1):
            root = self.roots[a]
            above, below = p.z > root, p.z < root

            def forward(j, a=a, above=above, below=below):
                self.b_copy(j, a, True, False).wait_recv()
                pl.when(above & p.has_up)(lambda: self.b_copy(j, a, True, False).start())
                pl.when(below & p.has_down)(lambda: self.b_copy(j, a, False, False).start())

            stage(self.at_final + far[a] * hop, forward, above | below)

            def settle(j, a=a):
                self.yz_copy(j, a).wait()
                self.acc[self.plan.at(j), a, self.mid, :] += self.yz_got[lax.rem(j, RING)]
                pl.when(p.has_up)(lambda: self.b_copy(j, a, True, True).start())
                pl.when(p.has_down)(lambda: self.b_copy(j, a, False, True).start())
                self.keep_copy(j, a).start()

            stage(self.at_final, settle, p.z == root)

        def last(j):
            for a in (0, 1):
                pl.when(p.z == self.roots[a])(lambda a=a: self.keep_copy(j, a).wait())
            self.last_copy(j).start()

        stage(self.at_final + jnp.maximum(far[0], far[1]) * hop, last)

    def drain(self):
        p = self.p
        message = self.final.at[:, 0, self.message]
        own, others = self.final.at[:, :, self.own], self.final.at[:, :, self.others]

        def sent(index, ref):
            remote(ref, ref, self.all_s.at[index], self.all_r.at[0], p.pair).wait_send()

        sent(0, others)
        for a in (0, 1):
            root = self.roots[a]
            pl.when(p.z != root)(lambda a=a: sent(1 + a, message))
            pl.when((p.z >= root) & p.has_up)(lambda a=a: sent(4 + 2 * a, message))
            pl.when((p.z <= root) & p.has_down)(lambda a=a: sent(3 + 2 * a, message))
        sent(7, own)
        remote(own, others, self.all_s.at[7], self.all_r.at[0], p.pair).wait_recv()


def exchange_scratch(plan, unit, lanes, line):
    slots = plan.partial + 1
    return dict(
        parts=pltpu.VMEM((slots, 2, 2, unit, lanes), f32),
        c_got=pltpu.VMEM((FEW, 2, unit, lanes), f32),
        x_got=pltpu.VMEM((plan.partials, unit, lanes), f32),
        y_got=pltpu.VMEM((RING, 2, unit // 8, lanes), f32),
        r_got=pltpu.VMEM((line_ring(line, plan.hop), 3, 3 * unit // 8, lanes), f32),
        yz_got=pltpu.VMEM((RING, unit // 4, lanes), f32),
        acc=pltpu.VMEM((plan.units, 2, unit // 2, lanes), f32),
        fs=pltpu.SemaphoreType.DMA((plan.partials, 2)),
        fr=pltpu.SemaphoreType.DMA((plan.partials, 2)),
        us=pltpu.SemaphoreType.DMA((plan.n,)),
        ur=pltpu.SemaphoreType.DMA((plan.n, 7)),
        all_s=pltpu.SemaphoreType.DMA((8,)),
        all_r=pltpu.SemaphoreType.DMA((1,)),
    )


SMALL = ("cb", "g1", "s1", "vb", "g2", "s2", "ub")
SMALL_ROWS = 40
NEAR_AT, FAR_AT, TABLE_AT = 0, 16, 32
CW = 3
FIRST_TICK = 1
ORDER = dict(whole_tick=10, later=3, second_early=7, second_start=32, held=12)


def backward_kernel(dims, names, plan, *refs):
    windows, base, d, ff, taps, line, unit = dims
    rows = windows * base
    blocks = ff // d
    lanes = d // SEQ
    half = taps // 2
    r = Refs(names, refs)
    p = Place(line)
    per = d // unit
    smalls = 2 * per * blocks

    def loop(n, body):
        def run(i, carry):
            body(i)
            return carry

        lax.fori_loop(0, n, run, 0)

    def live(w):
        where = p.s * base + lax.broadcasted_iota(jnp.int32, (base, 1), 0)
        return where < r.lengths[w]

    def window(w):
        return pl.ds(pl.multiple_of(w * base, base), base)

    which = {name: i for i, name in enumerate(SAVED)}

    def load(name, side):
        return pltpu.make_async_copy(r.of(side, name), getattr(r, name), r.lsem.at[which[name]])

    def load_h(side):
        return pltpu.make_async_copy(r.of(side, "full"), r.h, r.lsem.at[len(SAVED)])

    def load_conv(side, k, i):
        at = lax.rem(i, CW)
        return pltpu.make_async_copy(r.of(side, "conv").at[k], r.cw.at[at], r.csem.at[at])

    def wide_loads(side, b, slot):
        wide = ff // SEQ
        got = []
        for q in range(SEQ):
            at = pl.ds(pl.multiple_of(q * wide + b * lanes, lanes), lanes)
            put = pl.ds(q * lanes, lanes)
            got.append(pltpu.make_async_copy(r.of(side, "up").at[:, at], r.uw.at[slot, :, put], r.wsem.at[slot, q]))
            got.append(
                pltpu.make_async_copy(r.of(side, "down").at[at, :], r.vw.at[slot, put, :], r.wsem.at[slot, SEQ + q])
            )
        return got

    def start(side, *which_names):
        for name in which_names:
            load(name, side).start()

    def wait(side, *which_names):
        for name in which_names:
            load(name, side).wait()

    cot = pltpu.make_async_copy(r.cotangent, r.dy, r.lsem.at[len(SAVED) + 1])
    cot.start()
    start("far", "n2", "rs2", "mid")

    ex = Exchange(p, plan, unit, r)
    r.sums[...] = jnp.zeros(r.sums.shape, f32)
    r.parts[smalls, :, :, SMALL_ROWS:, :] = jnp.zeros((2, 2, unit - SMALL_ROWS, lanes), f32)

    @pl.when(p.s == 0)
    def _():
        r.dp[:, 0:HALO, :] = jnp.zeros((windows, HALO, d), f32)
        r.dw[:, 0:base, :] = jnp.zeros((windows, base, d), f32)

    @pl.when(p.s == SEQ - 1)
    def _():
        r.dp[:, HALO + base :, :] = jnp.zeros((windows, HALO, d), f32)
        r.dw[:, 2 * base :, :] = jnp.zeros((windows, base, d), f32)

    far_pad = half * SECOND_DILATION
    for ref, pad in ((r.dq_near, HALO), (r.dq_far, far_pad)):
        ref[:, 0:pad, :] = jnp.zeros((windows, pad, lanes), f32)
        ref[:, pad + SEQ * base :, :] = jnp.zeros((windows, pad, lanes), f32)

    p.greet(True)

    def add(kind, v):
        r.sums[kind] += jnp.sum(v.reshape(v.shape[0] // 8, 8, d), axis=0)

    def ffn_norm_back(side, at0):
        def body(w):
            at = window(w)
            dy = r.dy[at, :]
            if side == "far":
                dy = jnp.where(live(w), dy, 0.0)
            n = r.n2[at, :]
            add(at0 + 4, dy * n)
            add(at0 + 5, dy)
            dn = dy * r.of(side, "g2")[...]
            rs = r.rs2[at, 0:1]
            df = rs * (dn - row_mean(dn) - n * row_mean(dn * n))
            add(at0 + 3, df)
            h, l = split(df)
            r.df_h[at, :] = h
            r.df_l[at, :] = l
            r.dmid[at, :] = dy
            mh, ml = split(r.mid[at, :])
            r.mid_h[at, :] = mh
            r.mid_l[at, :] = ml

        loop(windows, body)

    def put_units(j, v):
        for i in range(per):
            for q in range(SEQ):
                r.parts[j + i, q // 2, q % 2, :, :] = v[i * unit : (i + 1) * unit, q * lanes : (q + 1) * lanes]

    def ffn_back(b, at0):
        slot = lax.rem(b, 2)
        for copy in wide_loads("far", b, slot):
            copy.wait()
        r.tmp[...] = dot3((r.df_h[...], r.df_l[...]), split(r.vw[slot]), NT)

        def act(i):
            at = pl.ds(pl.multiple_of(i * ROWS, ROWS), ROWS)
            dz = r.tmp[at, :] * r.gp[b, at, :]
            add(at0 + 6 + b, dz)
            h, l = split(dz)
            r.dz_h[at, :] = h
            r.dz_l[at, :] = l
            r.gp[b, at, :] = dz

        loop(rows // ROWS, act)

    def ffn_on(b):
        r.dmid[...] += dot3((r.dz_h[...], r.dz_l[...]), split(r.uw[lax.rem(b, 2)]), NT)

    def down_weights(b):
        put_units(2 * per * b, dot3((r.hid_h[b], r.hid_l[b]), (r.df_h[...], r.df_l[...]), TN))

    def up_weights(b):
        put_units(2 * per * b + per, dot3((r.mid_h[...], r.mid_l[...]), split(r.gp[b]), TN))

    def conv_norm_back(side, at0, put):
        def body(w):
            at = window(w)
            dmid, n = r.dmid[at, :], r.n1[at, :]
            add(at0 + 1, dmid * n)
            add(at0 + 2, dmid)
            dn = dmid * r.of(side, "g1")[...]
            dconv = r.gr1[at, :] * (dn - row_mean(dn) - n * row_mean(dn * n))
            add(at0, dconv)
            put(w, dconv)

        loop(windows, body)

    xs, xr = r.ssem, r.rsem

    def quarter_copies(src, at, pad, dq, sem):
        put = pl.ds(pl.multiple_of(pad + p.s * base, 8), base)
        got = []
        for i, s in enumerate((p.across_s, p.diag_s, p.sib_s)):
            cols = pl.ds(pl.multiple_of(s * lanes, lanes), lanes)
            mine = src.at[:, pl.ds(at, base), cols]
            got.append(remote(mine, dq.at[:, put, :], xs.at[sem + i], xr.at[sem + i], (p.w, s)))
        return got

    def keep_quarter(src, at, pad, dq):
        cols = pl.ds(pl.multiple_of(p.s * lanes, lanes), lanes)
        dq[:, pl.ds(pl.multiple_of(pad + p.s * base, 8), base), :] = src[:, at : at + base, cols]

    def weight_back(dq, pad, dilation, at, w, lo, hi):
        left = split(r.h[:, pl.ds(w, 1), :, :].reshape(SEQ * base, d))
        right = [
            dq[w, pad - (k - half) * dilation : pad - (k - half) * dilation + SEQ * base, :] for k in range(lo, hi)
        ]
        v = dot3(left, split(jnp.concatenate(right, axis=1)), TN)

        def put(first):
            for k in range(lo, hi):
                for i in range(2 * per):
                    piece = v[i * (unit // 2) : (i + 1) * (unit // 2), (k - lo) * lanes : (k - lo + 1) * lanes]
                    j = at + k * per + i // 2
                    if first:
                        r.acc[j, i % 2] = piece
                    else:
                        r.acc[j, i % 2] += piece

        pl.when(w == 0)(lambda: put(True))
        pl.when(w > 0)(lambda: put(False))

    groups = ((0, half + 1), (half + 1, taps))
    own_rows = pl.ds(base, base)

    def block_next():
        return remote(r.dw.at[:, own_rows], r.dw.at[:, pl.ds(0, base)], xs.at[0], xr.at[0], p.next)

    def block_prev():
        return remote(r.dw.at[:, own_rows], r.dw.at[:, pl.ds(2 * base, base)], xs.at[1], xr.at[1], p.prev)

    def far_quarters():
        return quarter_copies(r.dw, base, far_pad, r.dq_far, 2)

    def halo_next():
        return remote(r.dp.at[:, pl.ds(base, HALO)], r.dp.at[:, pl.ds(0, HALO)], xs.at[5], xr.at[5], p.next)

    def halo_prev():
        return remote(r.dp.at[:, pl.ds(HALO, HALO)], r.dp.at[:, pl.ds(HALO + base, HALO)], xs.at[6], xr.at[6], p.prev)

    def near_quarters():
        return quarter_copies(r.dp, HALO, HALO, r.dq_near, 7)

    def far_norm():
        wait("far", "n1", "gr1")

        def put(w, dconv):
            r.dw[w, base : 2 * base, :] = dconv
            h, l = split(dconv)
            r.dw_h[w, base : 2 * base, :] = h
            r.dw_l[w, base : 2 * base, :] = l

        conv_norm_back("far", FAR_AT, put)
        for copy in far_quarters():
            copy.start()
        start("near", "n2", "rs2", "n1", "gr1")
        keep_quarter(r.dw, base, far_pad, r.dq_far)
        r.tmp[...] = jnp.zeros((rows, d), f32)

    def far_tap(k):
        at = pl.ds(pl.multiple_of(base - (k - half) * SECOND_DILATION, SECOND_DILATION), base)
        lhs = (r.dw_h[:, at, :].reshape(rows, d), r.dw_l[:, at, :].reshape(rows, d))
        load_conv("far", k, k).wait()
        r.tmp[...] += dot3(lhs, split(r.cw[lax.rem(k, CW)]), NT)
        pl.when(k + CW < taps)(lambda: load_conv("far", k + CW, k + CW).start())
        pl.when(k + CW >= taps)(lambda: load_conv("near", k + CW - taps, k + CW).start())

    def far_halo():
        pl.when(p.has_prev)(lambda: block_next().wait_recv())
        pl.when(p.has_next)(lambda: block_prev().wait_recv())

        def halves(w):
            for at in (0, 2 * base):
                h, l = split(r.dw[w, at : at + base, :])
                r.dw_h[w, at : at + base, :] = h
                r.dw_l[w, at : at + base, :] = l

        loop(windows, halves)

    def far_end():
        def dx(w):
            at = window(w)
            r.dy[at, :] = r.dmid[at, :] + jnp.where(live(w), r.tmp[at, :], 0.0)

        loop(windows, dx)

    def near_begin():
        wait("near", "n2", "rs2", "mid", "gp", "hid_h", "hid_l")
        ffn_norm_back("near", NEAR_AT)

    def near_norm():
        wait("near", "n1", "gr1")

        def put(w, dconv):
            r.dp[w, HALO : HALO + base, :] = dconv

        conv_norm_back("near", NEAR_AT, put)
        pl.when(p.has_next)(lambda: halo_next().start())
        pl.when(p.has_prev)(lambda: halo_prev().start())
        for copy in near_quarters():
            copy.start()
        keep_quarter(r.dp, HALO, HALO, r.dq_near)

    def near_halo():
        pl.when(p.has_prev)(lambda: halo_next().wait_recv())
        pl.when(p.has_next)(lambda: halo_prev().wait_recv())

    def near_tap(k):
        at = HALO - (k - half) * FIRST_DILATION
        lhs = split(r.dp[:, at : at + base, :].reshape(rows, d))
        load_conv("near", k, taps + k).wait()
        v = dot3(lhs, split(r.cw[(taps + k) % CW]), NT)
        if k == 0:
            r.tmp[...] = v
        else:
            r.tmp[...] += v
        if k + CW < taps:
            load_conv("near", k + CW, taps + k + CW).start()

    def input_grad():
        return pltpu.make_async_copy(r.dy, r.input_grad, r.lsem.at[len(SAVED) + 1])

    def near_end():
        def dx(w):
            at = window(w)
            v = r.dmid[at, :] + jnp.where(live(w), r.tmp[at, :], 0.0)
            r.dy[at, :] = v
            v = jnp.sum(v.reshape(base // 8, 8, d), axis=0)
            species = r.species[w]
            for kind in range(SMALL_ROWS - TABLE_AT):
                r.sums[TABLE_AT + kind] += jnp.where(species == kind, v, 0.0)

        loop(windows, dx)
        input_grad().start()
        small = jnp.sum(r.sums[...], axis=1)
        for q in range(SEQ):
            r.parts[smalls, q // 2, q % 2, 0:SMALL_ROWS, :] = small[:, q * lanes : (q + 1) * lanes]

    cot.wait()
    wait("far", "n2", "rs2", "mid")
    for copy in wide_loads("far", 0, 0):
        copy.start()
    start("far", "gp")
    ffn_norm_back("far", FAR_AT)
    start("far", "hid_h", "hid_l")
    for copy in wide_loads("far", 1, 1):
        copy.start()
    start("far", "n1", "gr1")
    wait("far", "gp")

    at = 0

    def take(n):
        nonlocal at
        at += n
        return at - n

    first_ffn = take(1)
    first_ffn_weights = take(1)
    far_ffn = take(blocks - 1)
    far_norm_at = take(1)
    far_ffn_weights = take(blocks - 1)
    far_weights = take(len(groups) * windows)
    far_taps = take(-(-taps // 2))
    far_end_at = take(1)
    near_begin_at = take(1)
    near_ffn = take(2 * blocks)
    near_norm_at = take(1)
    near_ffn_weights = take(2 * blocks)
    near_taps = take(-(-taps // 2))
    near_end_at = take(1)
    near_weights = take(len(groups) * windows)

    def step(i, carry):
        def when(first, n, body):
            pl.when((i >= first) & (i < first + n))(lambda: body(i - first))

        first = i == first_ffn
        far = first | ((i >= far_ffn) & (i < far_ffn + blocks - 1))
        near = (i >= near_ffn) & (i < near_ffn + 2 * blocks)
        b = jnp.where(first, 0, jnp.where(far, i - far_ffn + 1, lax.div(i - near_ffn, 2)))
        odd = lax.rem(i - near_ffn, 2) == 1
        pl.when(far | (near & jnp.logical_not(odd)))(lambda: ffn_back(b, jnp.where(near, NEAR_AT, FAR_AT)))

        @pl.when(far | (near & odd))
        def _():
            ffn_on(b)

            def fetch(side, b):
                for copy in wide_loads(side, b, lax.rem(b, 2)):
                    copy.start()

            pl.when(near & (b < blocks - 2))(lambda: fetch("near", b + 2))
            pl.when(far & (b < blocks - 2))(lambda: fetch("far", b + 2))
            pl.when(far & (b >= blocks - 2))(lambda: fetch("near", b - (blocks - 2)))

        pl.when(i == first_ffn_weights)(lambda: wait("far", "hid_h", "hid_l"))

        @pl.when(i == far_ffn)
        def _():
            load_h("far").start()
            for k in range(CW):
                load_conv("far", k, k).start()

        first = i == first_ffn_weights
        far = first | ((i >= far_ffn_weights) & (i < far_ffn_weights + blocks - 1))
        near = (i >= near_ffn_weights) & (i < near_ffn_weights + 2 * blocks)
        b = jnp.where(first, 0, jnp.where(far, i - far_ffn_weights + 1, lax.div(i - near_ffn_weights, 2)))
        odd = lax.rem(i - near_ffn_weights, 2) == 1
        pl.when(far | (near & jnp.logical_not(odd)))(lambda: down_weights(b))
        pl.when(far | (near & odd))(lambda: up_weights(b))
        when(far_norm_at, 1, lambda _: far_norm())

        @pl.when(i == far_weights)
        def _():
            start("near", "mid", "gp", "hid_h", "hid_l")
            for copy in far_quarters():
                copy.wait()
            pl.when(p.has_next)(lambda: block_next().start())
            pl.when(p.has_prev)(lambda: block_prev().start())
            load_h("far").wait()

        for g, (lo, hi) in enumerate(groups):
            when(
                far_weights + g * windows,
                windows,
                lambda w, lo=lo, hi=hi: weight_back(
                    r.dq_far, far_pad, SECOND_DILATION, plan.far_whole - plan.gap, w, lo, hi
                ),
            )

        @pl.when(i == far_taps)
        def _():
            load_h("near").start()
            far_halo()

        def two_taps(m):
            far_tap(2 * m)
            pl.when(2 * m + 1 < taps)(lambda: far_tap(2 * m + 1))

        when(far_taps, -(-taps // 2), two_taps)
        when(far_end_at, 1, lambda _: far_end())
        when(near_begin_at, 1, lambda _: near_begin())
        when(near_norm_at, 1, lambda _: near_norm())
        pl.when(i == near_taps)(near_halo)
        for k in range(taps):
            when(near_taps + k // 2, 1, lambda _, k=k: near_tap(k))
        when(near_end_at, 1, lambda _: near_end())

        @pl.when(i == near_weights)
        def _():
            for copy in near_quarters():
                copy.wait()
            load_h("near").wait()

        for g, (lo, hi) in enumerate(groups):
            when(
                near_weights + g * windows,
                windows,
                lambda w, lo=lo, hi=hi: weight_back(r.dq_near, HALO, FIRST_DILATION, plan.near_whole - plan.gap, w, lo, hi),
            )
        ex.tick(i - FIRST_TICK)
        return carry

    lax.fori_loop(0, max(at, ex.ticks + FIRST_TICK), step, 0)
    ex.drain()

    @pl.when(p.has_next)
    def _():
        halo_next().wait_send()
        block_next().wait_send()

    @pl.when(p.has_prev)
    def _():
        halo_prev().wait_send()
        block_prev().wait_send()

    input_grad().wait()


def backward(line, lengths, species, table, cotangent, fulls, saved, near, far):
    windows, base, d = cotangent.shape
    taps, ff = near[0].shape[0], near[4].shape[1]
    rows, blocks, lanes = windows * base, ff // d, d // SEQ
    unit, hop = 256, (2 if line <= 4 else 1)
    per = d // unit
    plan = Plan(2 * per * blocks, taps * per, hop, 2 * per, **ORDER)
    n = plan.units
    smem = pl.BlockSpec(memory_space=pltpu.SMEM)
    vmem = pl.BlockSpec(memory_space=pltpu.VMEM)
    hbm = pl.BlockSpec(memory_space=pl.ANY)
    names, args, specs = ["lengths", "species", "cotangent"], [lengths, species, cotangent.reshape(rows, d)], [smem, smem, hbm]
    for side, block, full, kept in zip(("near", "far"), (near, far), fulls, saved, strict=True):
        names += [side + "_" + v for v in ("full", "conv", "up", "down") + SAVED + ("g1", "g2")]
        args += [full, block[0], block[4], block[6], *kept, block[2].reshape(1, -1), block[8].reshape(1, -1)]
        specs += [hbm] * (4 + len(SAVED)) + [vmem] * 2
    names += ["input_grad", "final"]
    scratch = {name: pltpu.VMEM(*v) for name, v in saved_shapes(rows, d, ff).items()}
    for name in ("dy", "dmid", "tmp"):
        scratch[name] = pltpu.VMEM((rows, d), f32)
    for name in ("mid_h", "mid_l", "df_h", "df_l", "dz_h", "dz_l"):
        scratch[name] = pltpu.VMEM((rows, d), bf16)
    scratch.update(
        h=pltpu.VMEM((SEQ, windows, base, d), f32),
        cw=pltpu.VMEM((CW, d, d), f32),
        uw=pltpu.VMEM((2, d, d), f32),
        vw=pltpu.VMEM((2, d, d), f32),
        dp=pltpu.VMEM((windows, base + 2 * HALO, d), f32),
        dw=pltpu.VMEM((windows, 3 * base, d), f32),
        dw_h=pltpu.VMEM((windows, 3 * base, d), bf16),
        dw_l=pltpu.VMEM((windows, 3 * base, d), bf16),
        dq_near=pltpu.VMEM((windows, SEQ * base + 2 * HALO, lanes), f32),
        dq_far=pltpu.VMEM((windows, SEQ * base + taps // 2 * 2 * SECOND_DILATION, lanes), f32),
        sums=pltpu.VMEM((SMALL_ROWS, 8, d), f32),
        lsem=pltpu.SemaphoreType.DMA((len(SAVED) + 2,)),
        csem=pltpu.SemaphoreType.DMA((CW,)),
        wsem=pltpu.SemaphoreType.DMA((2, 2 * SEQ)),
        ssem=pltpu.SemaphoreType.DMA((10,)),
        rsem=pltpu.SemaphoreType.DMA((10,)),
    )
    scratch.update(exchange_scratch(plan, unit, lanes, line))
    names += list(scratch)
    input_grad, final = pl.pallas_call(
        functools.partial(backward_kernel, (windows, base, d, ff, taps, line, unit), names, plan),
        out_shape=[jax.ShapeDtypeStruct((rows, d), f32), jax.ShapeDtypeStruct((n, 2, unit // 2, lanes), f32)],
        in_specs=specs,
        out_specs=[hbm, hbm],
        scratch_shapes=list(scratch.values()),
        compiler_params=pltpu.CompilerParams(
            collective_id=1, has_side_effects=True, vmem_limit_bytes=64 * 1024 * 1024 - 65536
        ),
        name="backward",
    )(*args)

    grads = unpack(plan, windows, rows, blocks, taps, d, ff, unit, final.reshape(n, unit, lanes))
    table_grad, near_grads, far_grads = grads[0], grads[1:11], grads[11:]
    shapes = [(taps, d, lanes), (lanes,), (lanes,), (lanes,), (d, ff // SEQ), (ff // SEQ,), (ff, lanes)] + 3 * [(lanes,)]
    near_grads = [v.reshape(shape) for v, shape in zip(near_grads, shapes, strict=True)]
    far_grads = [v.reshape(shape) for v, shape in zip(far_grads, shapes, strict=True)]
    return input_grad.reshape(cotangent.shape), table_grad, near_grads, far_grads


def unpack_kernel(plan, dims, final, table, *refs):
    blocks, taps, d, ff, unit = dims
    lanes = d // SEQ
    per = d // unit
    outs, out_sem = refs[:20], refs[20]

    def copy(src, dst):
        pltpu.make_async_copy(src, dst, out_sem.at[0]).start()

    def unit_at(j):
        return final.at[plan.at(j)]

    small = unit_at(plan.place(plan.partials - 1))
    copy(small.at[pl.ds(TABLE_AT, SMALL_ROWS - TABLE_AT)], table)
    for side, at, first, whole in (
        (outs[:10], NEAR_AT, plan.partial, plan.near_whole),
        (outs[10:], FAR_AT, 0, plan.far_whole),
    ):
        cw, cb, g1, s1, uw, ub, vw, vb, g2, s2 = side
        for i in range(taps * per):
            copy(unit_at(whole + i), cw.at[i // per, pl.ds(i % per * unit, unit)])
        for b in range(blocks):
            cols = pl.ds(b * lanes, lanes)
            for i in range(per):
                f = first + 2 * per * b + i
                for q in range(unit // lanes):
                    row = (i * (unit // lanes) + q) * (ff // SEQ) + b * lanes
                    copy(unit_at(plan.place(f)).at[pl.ds(q * lanes, lanes)], vw.at[pl.ds(row, lanes)])
                copy(unit_at(plan.place(f + per)), uw.at[pl.ds(i * unit, unit), cols])
            copy(small.at[pl.ds(at + 6 + b, 1)], ub.at[:, cols])
        for i, ref in enumerate((cb, g1, s1, vb, g2, s2)):
            copy(small.at[pl.ds(at + i, 1)], ref)
    for ref in (table, *outs):
        pltpu.make_async_copy(ref, ref, out_sem.at[0]).wait()


def unpack(plan, windows, rows, blocks, taps, d, ff, unit, final):
    lanes = d // SEQ
    one = (1, lanes)
    block = [(taps, d, lanes), one, one, one, (d, ff // SEQ), (1, ff // SEQ), (ff, lanes), one, one, one]
    hbm = pl.BlockSpec(memory_space=pl.ANY)
    outs = [(SMALL_ROWS - TABLE_AT, lanes)] + block + block
    return pl.pallas_call(
        functools.partial(unpack_kernel, plan, (blocks, taps, d, ff, unit)),
        out_shape=[jax.ShapeDtypeStruct(v, f32) for v in outs],
        in_specs=[pl.BlockSpec(memory_space=pltpu.VMEM)],
        out_specs=[hbm] * len(outs),
        scratch_shapes=[
            pltpu.SemaphoreType.DMA((1,)),
        ],
        compiler_params=pltpu.CompilerParams(vmem_limit_bytes=32 * 1024 * 1024),
        name="unpack",
    )(final)


def on_device(inputs, species, lengths, species_table, *rest):
    near, far, cotangent = rest[:10], rest[10:20], rest[20]
    line = lax.axis_size("win") // 2
    output, near_full, far_full, near_saved, far_saved = forward(
        line, lengths, species, species_table, inputs, near, far
    )
    input_grad, table_grad, near_grads, far_grads = backward(
        line, lengths, species, species_table, cotangent, (near_full, far_full), (near_saved, far_saved), near, far
    )
    return (output, input_grad, table_grad, *near_grads, *far_grads)


def solution(mesh):
    split_windows = P("win", "seq", None)
    block_grads = (P(None, None, "seq"), P("seq"), P("seq"), P("seq"), P(None, "seq"), P("seq"), P(None, "seq"))
    block_grads += (P("seq"), P("seq"), P("seq"))
    return jax.shard_map(
        on_device,
        mesh=mesh,
        in_specs=(split_windows, P("win"), P("win")) + (P(),) * 21 + (split_windows,),
        out_specs=(split_windows, split_windows, P(None, "seq")) + block_grads + block_grads,
        check_vma=False,
    )
```

```python
import functools

import jax
import jax.numpy as jnp
from jax import lax
from jax.experimental import pallas as pl
from jax.experimental.pallas import tpu as pltpu
from jax.sharding import PartitionSpec as P

FIRST_DILATION = 1
SECOND_DILATION = 32
EPS = 1e-05
ROWS = 32
HALO = 8
SEQ = 4
f32, bf16 = jnp.float32, jnp.bfloat16
MESH_ID = pl.DeviceIdType.MESH


def split(v):
    high = v.astype(bf16)
    return high, (v - high.astype(f32)).astype(bf16)


def dot(left, right, dims):
    return lax.dot_general(left, right, (dims, ((), ())), preferred_element_type=f32)


def dot3(left, right, dims=((1,), (0,))):
    (lh, ll), (rh, rl) = left, right
    return dot(lh, rh, dims) + (dot(lh, rl, dims) + dot(ll, rh, dims))


NT = ((1,), (1,))
TN = ((0,), (0,))


def gauss(z):
    size = jnp.abs(z)
    t = 1.0 / (1.0 + (0.3275911 * 0.7071067811865476) * size)
    e = jnp.exp(-0.5 * z * z)
    poly = 0.5 * 1.061405429
    for term in (-1.453152027, 1.421413741, -0.284496736, 0.254829592):
        poly = poly * t + 0.5 * term
    tail = poly * t * e
    return jnp.where(z >= 0, 1.0 - tail, tail), (z * 0.3989422804014327) * e


def row_mean(v):
    return jnp.mean(v, axis=-1, keepdims=True)


def remote(src, dst, send, recv, device):
    return pltpu.make_async_remote_copy(
        src_ref=src, dst_ref=dst, send_sem=send, recv_sem=recv, device_id=device, device_id_type=MESH_ID
    )


class Refs:
    def __init__(self, names, refs):
        for name, ref in zip(names, refs, strict=True):
            setattr(self, name, ref)

    def of(self, side, name):
        return getattr(self, side + "_" + name)


class Place:
    def __init__(self, line):
        w, s = lax.axis_index("win"), lax.axis_index("seq")
        self.w, self.s, self.line = w, s, line
        self.z, self.y = lax.div(w, 2), lax.rem(w, 2)
        self.x, self.c = lax.div(s, 2), lax.rem(s, 2)
        self.sib_s = 2 * self.x + 1 - self.c
        self.across_s = 2 * (1 - self.x) + self.c
        self.diag_s = SEQ - 1 - s
        self.sib, self.across, self.diag = (w, self.sib_s), (w, self.across_s), (w, self.diag_s)
        self.pair = (2 * self.z + 1 - self.y, s)
        self.up, self.down = (w + 2, s), (w - 2, s)
        self.next, self.prev = (w, s + 1), (w, s - 1)
        self.has_up, self.has_down = self.z < line - 1, self.z > 0
        self.has_next, self.has_prev = s < SEQ - 1, s > 0
        self.inner = self.c != self.x

    def greet(self, whole):
        barrier = pltpu.get_barrier_semaphore()

        def signal(device):
            pl.semaphore_signal(barrier, inc=1, device_id=device, device_id_type=MESH_ID)

        for device in (self.sib, self.across, self.diag):
            signal(device)
        if not whole:
            pl.semaphore_wait(barrier, 3)
            return
        signal(self.pair)
        pl.when(self.has_up)(lambda: signal(self.up))
        pl.when(self.has_down)(lambda: signal(self.down))
        pl.semaphore_wait(barrier, 4 + self.has_up.astype(jnp.int32) + self.has_down.astype(jnp.int32))


AHEAD = 4
LARGE, SMALLER = ("hid_h", "hid_l", "gp"), ("mid", "n1", "gr1", "n2", "rs2")
SAVED = ("mid", "n1", "gr1", "n2", "rs2", "hid_h", "hid_l", "gp")


def saved_shapes(rows, d, ff):
    blocks = ff // d
    return dict(
        mid=((rows, d), f32),
        n1=((rows, d), f32),
        gr1=((rows, d), f32),
        n2=((rows, d), f32),
        rs2=((rows, 128), f32),
        hid_h=((blocks, rows, d), bf16),
        hid_l=((blocks, rows, d), bf16),
        gp=((blocks, rows, d), f32),
    )


def ff_columns(ref, b, d, parts, lanes):
    wide = d * parts // SEQ
    return [ref[:, pl.ds(pl.multiple_of(q * wide + b * lanes, lanes), lanes)] for q in range(SEQ)]


def ff_rows(ref, b, d, parts, lanes):
    wide = d * parts // SEQ
    return [ref[pl.ds(pl.multiple_of(q * wide + b * lanes, lanes), lanes), :] for q in range(SEQ)]


def forward_kernel(dims, *refs):
    windows, base, d, ff, taps, line = dims
    rows = windows * base
    blocks = ff // d
    lanes = d // SEQ
    names = ["lengths", "species", "table", "inputs"]
    weights = ("conv", "up", "down")
    vectors = ("cb", "g1", "s1", "ub", "vb", "g2", "s2")
    for side in ("near", "far"):
        names += [side + "_" + v for v in weights + vectors]
    names += ["output", "near_full", "far_full"]
    for side in ("near", "far"):
        names += [side + "_out_" + v for v in SAVED]
    for side in ("near", "far"):
        names += [side + "_" + v for v in SAVED]
    names += ["cw", "uw", "vw", "x", "acc", "zb", "mid_h", "mid_l", "hp", "hq", "hq_h", "hq_l", "own"]
    names += ["own2", "out_buf", "csem", "wsem", "osem", "bsem", "gsem", "ssem", "rsem"]
    r = Refs(names, refs)
    p = Place(line)

    def conv_weights(side, k):
        return pltpu.make_async_copy(r.of(side, "conv").at[k], r.cw.at[k], r.csem.at[k])

    def wide_weights(side, i):
        src, dst = (("up", r.uw), ("down", r.vw))[i]
        return pltpu.make_async_copy(r.of(side, src), dst, r.wsem.at[i])

    order = [taps // 2] + [k for k in range(taps) if k != taps // 2]
    for k in order[:AHEAD]:
        conv_weights("near", k).start()

    def live(w):
        where = p.s * base + lax.broadcasted_iota(jnp.int32, (base, 1), 0)
        return where < r.lengths[w]

    def window(w):
        return pl.ds(pl.multiple_of(w * base, base), base)

    def step_rows(i):
        return pl.ds(pl.multiple_of(i * ROWS, ROWS), ROWS)

    def loop(n, body):
        def run(i, carry):
            body(i)
            return carry

        lax.fori_loop(0, n, run, 0)

    def begin(w):
        v = r.inputs[w] + r.table[pl.ds(r.species[w], 1), :]
        r.x[window(w), :] = v
        h = jnp.where(live(w), v, 0.0)
        r.hp[w, HALO : HALO + base, :] = h
        r.own[w] = h

    loop(windows, begin)

    @pl.when(p.s == 0)
    def _():
        r.hp[:, 0:HALO, :] = jnp.zeros((windows, HALO, d), f32)
        r.hq[:, 0:base, :] = jnp.zeros((windows, base, d), f32)

    @pl.when(p.s == SEQ - 1)
    def _():
        r.hp[:, HALO + base :, :] = jnp.zeros((windows, HALO, d), f32)
        r.hq[:, 2 * base :, :] = jnp.zeros((windows, base, d), f32)

    p.greet(False)
    ssem, rsem = r.ssem, r.rsem

    def halo_next():
        return remote(
            r.hp.at[:, pl.ds(base, HALO)], r.hp.at[:, pl.ds(0, HALO)], ssem.at[0], rsem.at[0], p.next
        )

    def halo_prev():
        return remote(
            r.hp.at[:, pl.ds(HALO, HALO)], r.hp.at[:, pl.ds(HALO + base, HALO)], ssem.at[1], rsem.at[1], p.prev
        )

    pl.when(p.has_next)(lambda: halo_next().start())
    pl.when(p.has_prev)(lambda: halo_prev().start())

    other_inner = (p.w, jnp.where(p.x == 0, 2, 1))
    first_other = 2 * (1 - p.x)
    other_outer = jnp.where(p.x == 0, 3, 0)

    def bulk_own(full):
        return r.own if full == "near" else r.own2

    def bulk_keep(full, at):
        return pltpu.make_async_copy(bulk_own(full), r.of(full, "full").at[p.s], ssem.at[at])

    def bulk_sib(full, at, block, src=None):
        return remote(
            bulk_own(full) if src is None else src, r.of(full, "full").at[block], ssem.at[at + 1], rsem.at[at + 1], p.sib
        )

    def bulk_across(full, at):
        return remote(bulk_own(full), r.of(full, "full").at[p.s], ssem.at[at + 2], rsem.at[at + 2 + lax.rem(p.s, 2)], other_inner)

    def bulk_relay(full, at, block, i, src=None):
        src = r.of(full, "full").at[block] if src is None else src
        return remote(src, r.of(full, "full").at[block], ssem.at[at + 3 + i], rsem.at[at + 4 + i], p.sib)

    NEAR, FAR = 4, 12
    bulk_keep("near", NEAR).start()
    bulk_sib("near", NEAR, p.s).start()
    bulk_across("near", NEAR).start()

    def near_tap(k, lo, hi):
        at = HALO + (k - taps // 2) * FIRST_DILATION
        return dot3(split(r.hp[lo:hi, at : at + base, :].reshape((hi - lo) * base, d)), split(r.cw[k]))

    def conv_tail(side, lo, hi):
        def body(w):
            at = window(w)
            v = r.acc[at, :] + r.of(side, "cb")[...]
            cdf, zd = gauss(v)
            a = v * cdf
            center = a - row_mean(a)
            rs = lax.rsqrt(row_mean(center * center) + EPS)
            n = center * rs
            mid = r.x[at, :] + (n * r.of(side, "g1")[...] + r.of(side, "s1")[...])
            r.of(side, "n1")[at, :] = n
            r.of(side, "gr1")[at, :] = (cdf + zd) * rs
            r.of(side, "mid")[at, :] = mid
            h, l = split(mid)
            r.mid_h[at, :] = h
            r.mid_l[at, :] = l

        loop(hi - lo, lambda i: body(i + lo))

    def ffn(side, lo, hi):
        part = pl.ds(lo * base, (hi - lo) * base)

        def body(b):
            up = jnp.concatenate(ff_columns(r.uw, b, d, blocks, lanes), axis=1)
            r.zb[part, :] = dot3((r.mid_h[part, :], r.mid_l[part, :]), split(up))
            bias = jnp.concatenate(ff_columns(r.of(side, "ub"), b, d, blocks, lanes), axis=1)

            def act(i):
                at = pl.ds(pl.multiple_of(lo * base + i * ROWS, ROWS), ROWS)
                z = r.zb[at, :] + bias
                cdf, zd = gauss(z)
                h, l = split(z * cdf)
                r.of(side, "hid_h")[b, at, :] = h
                r.of(side, "hid_l")[b, at, :] = l
                r.of(side, "gp")[b, at, :] = cdf + zd

            loop((hi - lo) * base // ROWS, act)
            if hi == windows:
                for name in LARGE:
                    save_part(side, name, b).start()
            down = jnp.concatenate(ff_rows(r.vw, b, d, blocks, lanes), axis=0)
            f = dot3((r.of(side, "hid_h")[b, part, :], r.of(side, "hid_l")[b, part, :]), split(down))

            @pl.when(b == 0)
            def _():
                r.acc[part, :] = f

            @pl.when(b > 0)
            def _():
                r.acc[part, :] += f

        loop(blocks, body)

    def ffn_tail(side, keep, lo, hi):
        def body(w):
            at = window(w)
            f = r.acc[at, :] + r.of(side, "vb")[...]
            center = f - row_mean(f)
            rs = lax.rsqrt(row_mean(center * center) + EPS)
            n = center * rs
            r.of(side, "n2")[at, :] = n
            r.of(side, "rs2")[at, :] = jnp.broadcast_to(rs, (base, 128))
            keep(w, at, r.of(side, "mid")[at, :] + (n * r.of(side, "g2")[...] + r.of(side, "s2")[...]))

        loop(hi - lo, lambda i: body(i + lo))

    which = {name: i for i, name in enumerate(SAVED)}

    def save_sem(side, name):
        return r.osem.at[(0 if side == "near" else len(SAVED)) + which[name]]

    def save(side, name):
        return pltpu.make_async_copy(r.of(side, name), r.of(side, "out_" + name), save_sem(side, name))

    def save_part(side, name, b):
        return pltpu.make_async_copy(
            r.of(side, name).at[b], r.of(side, "out_" + name).at[b], r.bsem.at[0 if side == "near" else 1, which[name], b]
        )

    def block_next(g):
        lo, hi = groups[g]
        at = pl.ds(lo, hi - lo)
        return remote(r.own2.at[at], r.hq.at[at, pl.ds(0, base)], r.gsem.at[0, g, 0], r.gsem.at[1, g, 0], p.next)

    def block_prev(g):
        lo, hi = groups[g]
        at = pl.ds(lo, hi - lo)
        return remote(r.own2.at[at], r.hq.at[at, pl.ds(2 * base, base)], r.gsem.at[0, g, 1], r.gsem.at[1, g, 1], p.prev)

    def middle(w, at, v):
        r.x[at, :] = v
        h = jnp.where(live(w), v, 0.0)
        r.hq[w, base : 2 * base, :] = h
        r.own2[w] = h
        hh, hl = split(h)
        r.hq_h[w, base : 2 * base, :] = hh
        r.hq_l[w, base : 2 * base, :] = hl

    groups = ((0, windows - 1), (windows - 1, windows))
    for g, (lo, hi) in enumerate(groups):
        part = pl.ds(lo * base, (hi - lo) * base)
        for n, k in enumerate(order):
            if g == 0:
                conv_weights("near", k).wait()
                if n + AHEAD < taps:
                    conv_weights("near", order[n + AHEAD]).start()
                if n == taps - AHEAD:
                    for i in (0, 1):
                        wide_weights("near", i).start()
            if g == 0 and n == 1:
                pl.when(p.has_prev)(lambda: halo_next().wait_recv())
                pl.when(p.has_next)(lambda: halo_prev().wait_recv())
            v = near_tap(k, lo, hi)
            if n == 0:
                r.acc[part, :] = v
            else:
                r.acc[part, :] += v
        if hi == windows:
            for k in order:
                conv_weights("far", k).start()
        conv_tail("near", lo, hi)
        if g == 0:
            for i in (0, 1):
                wide_weights("near", i).wait()
        ffn("near", lo, hi)
        if hi == windows:
            for i in (0, 1):
                wide_weights("far", i).start()
        ffn_tail("near", middle, lo, hi)
        pl.when(p.has_next)(lambda g=g: block_next(g).start())
        pl.when(p.has_prev)(lambda g=g: block_prev(g).start())

    bulk_keep("far", FAR).start()
    bulk_sib("far", FAR, p.s).start()
    for name in SMALLER:
        save("near", name).start()

    @pl.when(p.inner)
    def _():
        for i in (0, 1):
            remote(
                r.own, r.near_full.at[first_other + i], ssem.at[NEAR + 2], rsem.at[NEAR + 2 + i], other_inner
            ).wait_recv()
            bulk_relay("near", NEAR, first_other + i, i).start()

    def far_tap(k):
        at = pl.ds(pl.multiple_of(base + (k - taps // 2) * SECOND_DILATION, SECOND_DILATION), base)
        lhs = (r.hq_h[:, at, :].reshape(rows, d), r.hq_l[:, at, :].reshape(rows, d))
        conv_weights("far", k).wait()
        r.acc[...] += dot3(lhs, split(r.cw[k]))

    r.acc[...] = jnp.zeros((rows, d), f32)
    far_tap(taps // 2)
    for g in range(len(groups)):
        pl.when(p.has_prev)(lambda g=g: block_next(g).wait_recv())
        pl.when(p.has_next)(lambda g=g: block_prev(g).wait_recv())

    @pl.when(jnp.logical_not(p.inner))
    def _():
        bulk_across("far", FAR).start()

    def halves(w):
        for at in (0, 2 * base):
            h, l = split(r.hq[w, at : at + base, :])
            r.hq_h[w, at : at + base, :] = h
            r.hq_l[w, at : at + base, :] = l

    loop(windows, halves)

    def keep_inner(at):
        return pltpu.make_async_copy(
            r.hq.at[:, pl.ds(at, base)], r.far_full.at[other_inner[1]], ssem.at[FAR + 2]
        )

    def relay_inner(at):
        return bulk_relay("far", FAR, other_inner[1], 0, r.hq.at[:, pl.ds(at, base)])

    inner_at = pl.multiple_of(jnp.where(p.x == 0, 2 * base, 0), base)

    @pl.when(p.inner)
    def _():
        keep_inner(inner_at).start()
        relay_inner(inner_at).start()

    for k in order[1:]:
        far_tap(k)
    conv_tail("far", 0, windows)
    for name in ("mid", "n1", "gr1"):
        save("far", name).start()
    for i in (0, 1):
        wide_weights("far", i).wait()
    ffn("far", 0, windows)

    def finish(w, at, v):
        r.out_buf[at, :] = jnp.where(live(w), v, 0.0)

    ffn_tail("far", finish, 0, windows)
    for name in ("n2", "rs2"):
        save("far", name).start()
    result = pltpu.make_async_copy(r.out_buf, r.output, r.osem.at[2 * len(SAVED)])
    result.start()

    @pl.when(p.inner)
    def _():
        remote(
            r.own, r.far_full.at[other_outer], ssem.at[FAR + 2], rsem.at[FAR + 2 + lax.rem(other_outer, 2)], other_inner
        ).wait_recv()
        bulk_relay("far", FAR, other_outer, 1).start()
        keep_inner(inner_at).wait()
        relay_inner(inner_at).wait_send()
        bulk_relay("far", FAR, other_outer, 1).wait_send()
        for i in (0, 1):
            bulk_relay("near", NEAR, first_other + i, i).wait_send()

    @pl.when(jnp.logical_not(p.inner))
    def _():
        bulk_across("far", FAR).wait_send()
        for full, at in (("near", NEAR), ("far", FAR)):
            for i in (0, 1):
                bulk_relay(full, at, first_other + i, i).wait_recv()

    for full, at in (("near", NEAR), ("far", FAR)):
        bulk_sib(full, at, p.sib_s).wait_recv()
    for full, at in (("near", NEAR), ("far", FAR)):
        bulk_sib(full, at, p.s).wait_send()
        bulk_keep(full, at).wait()
    bulk_across("near", NEAR).wait_send()

    @pl.when(p.has_next)
    def _():
        halo_next().wait_send()
        for g in range(len(groups)):
            block_next(g).wait_send()

    @pl.when(p.has_prev)
    def _():
        halo_prev().wait_send()
        for g in range(len(groups)):
            block_prev(g).wait_send()

    result.wait()
    for side in ("near", "far"):
        for name in SMALLER:
            save(side, name).wait()
        for name in LARGE:
            for b in range(blocks):
                save_part(side, name, b).wait()


def forward(line, lengths, species, table, inputs, near, far):
    windows, base, d = inputs.shape
    taps, ff = near[0].shape[0], near[4].shape[1]
    rows, blocks = windows * base, ff // d
    smem = pl.BlockSpec(memory_space=pltpu.SMEM)
    vmem = pl.BlockSpec(memory_space=pltpu.VMEM)
    hbm = pl.BlockSpec(memory_space=pl.ANY)
    args, specs = [lengths, species, table, inputs], [smem, smem, vmem, vmem]
    for cw, cb, g1, s1, uw, ub, vw, vb, g2, s2 in (near, far):
        args += [cw, uw, vw] + [v.reshape(1, -1) for v in (cb, g1, s1, ub, vb, g2, s2)]
        specs += [hbm] * 3 + [vmem] * 7
    kept = saved_shapes(rows, d, ff)
    full = ((SEQ, windows, base, d), f32)
    outs = [((rows, d), f32), full, full] + 2 * [kept[v] for v in SAVED]
    scratch = 2 * [pltpu.VMEM(*kept[v]) for v in SAVED]
    scratch += [
        pltpu.VMEM((taps, d, d), f32),
        pltpu.VMEM((d, ff), f32),
        pltpu.VMEM((ff, d), f32),
        pltpu.VMEM((rows, d), f32),
        pltpu.VMEM((rows, d), f32),
        pltpu.VMEM((rows, d), f32),
        pltpu.VMEM((rows, d), bf16),
        pltpu.VMEM((rows, d), bf16),
        pltpu.VMEM((windows, base + 2 * HALO, d), f32),
        pltpu.VMEM((windows, 3 * base, d), f32),
        pltpu.VMEM((windows, 3 * base, d), bf16),
        pltpu.VMEM((windows, 3 * base, d), bf16),
        pltpu.VMEM((windows, base, d), f32),
        pltpu.VMEM((windows, base, d), f32),
        pltpu.VMEM((rows, d), f32),
        pltpu.SemaphoreType.DMA((taps,)),
        pltpu.SemaphoreType.DMA((2,)),
        pltpu.SemaphoreType.DMA((2 * len(SAVED) + 1,)),
        pltpu.SemaphoreType.DMA((2, len(SAVED), blocks)),
        pltpu.SemaphoreType.DMA((2, 2, 2)),
        pltpu.SemaphoreType.DMA((20,)),
        pltpu.SemaphoreType.DMA((20,)),
    ]
    got = pl.pallas_call(
        functools.partial(forward_kernel, (windows, base, d, ff, taps, line)),
        out_shape=[jax.ShapeDtypeStruct(*v) for v in outs],
        in_specs=specs,
        out_specs=[hbm] * len(outs),
        scratch_shapes=scratch,
        compiler_params=pltpu.CompilerParams(
            collective_id=0, has_side_effects=True, vmem_limit_bytes=60 * 1024 * 1024
        ),
        name="forward",
    )(*args)
    n = len(SAVED)
    return got[0].reshape(inputs.shape), got[1], got[2], got[3 : 3 + n], got[3 + n :]


RING = 12
FEW = 6
EXCHANGE_REFS = tuple(
    dict(parts=0, c_got=0, x_got=0, y_got=0, r_got=0, yz_got=0, acc=0, final=0, fs=0, fr=0, us=0, ur=0, all_s=0, all_r=0)
)


def line_ring(line, hop):
    return max(RING, hop * (1 + 2 * (line // 2 + 1)) + 1)


def shares(unit):
    outer = 5 * unit // 32
    return outer, unit // 2 - 2 * outer


class Plan:
    def __init__(self, partial, whole, hop, early, whole_tick, later, second_early, second_start, held):
        gap = whole_tick - 2 * hop - early
        self.partial, self.whole, self.hop, self.early, self.gap = partial, whole, hop, early, gap
        self.later, self.second_start, self.held = later, second_start, held
        self.partials = 2 * partial + 1
        self.far_whole = early + gap
        self.shift = gap + whole
        self.before = partial + second_early
        self.near_whole = self.shift + self.before
        self.n = gap + self.partials + 2 * whole
        self.units = self.n - gap

    def at(self, j):
        if isinstance(j, int):
            return j if j < self.early else j - self.gap
        return jnp.where(j < self.early, j, j - self.gap)

    def real(self, j):
        return (j < self.early) | (j >= self.far_whole)

    def is_partial(self, j):
        far_or_first = (j >= self.early + self.shift) & (j < self.near_whole)
        return (j < self.early) | far_or_first | (j >= self.near_whole + self.whole)

    def number(self, j):
        return jnp.where(
            j < self.early, j, jnp.where(j < self.near_whole, j - self.shift, j - self.shift - self.whole)
        )

    def place(self, f):
        if isinstance(f, int):
            return f if f < self.early else f + self.shift + (self.whole if f >= self.before else 0)
        return jnp.where(f < self.early, f, jnp.where(f < self.before, f, f + self.whole) + self.shift)

    def starting(self, t):
        first = (t >= 0) & (t < self.early)
        far = (t >= self.early + self.later) & (t < self.partial + self.later)
        near = (t >= self.second_start) & (t < self.second_start + self.partial + 1)
        return first | far | near, jnp.where(
            first, t, jnp.where(far, t - self.later, t - self.second_start + self.partial)
        )


class Exchange:
    def __init__(self, place, plan, unit, refs):
        self.p, self.plan, self.unit, self.hop = place, plan, unit, plan.hop
        for name in EXCHANGE_REFS:
            setattr(self, name, getattr(refs, name))
        line, hop = place.line, plan.hop
        self.kinds = (((line // 2 - 1, line // 2), line // 2), ((line // 2 - 2, line // 2 + 1), line // 2 + 1))
        self.ring = line_ring(line, hop)
        self.at_y = 3 * hop
        self.ticks = plan.n + self.at_final(0) + self.kinds[0][1] * hop + 1
        y, (outer, mid) = place.y, shares(unit)
        self.own = pl.ds(pl.multiple_of(y * (outer + mid), 8), outer)
        self.others = pl.ds(pl.multiple_of((1 - y) * (outer + mid), 8), outer)
        self.mid = pl.ds(outer, mid)
        self.message = pl.ds(pl.multiple_of(y * outer, 8), outer + mid)

    def at_final(self, kind):
        return self.at_y + (self.kinds[kind][1] + 1) * self.hop

    def kind_is(self, j, kind):
        out = (lax.rem(j, 2) == 1) & (j < self.plan.n - 2 * self.hop)
        return out if kind else jnp.logical_not(out)

    def count(self, kind):
        plan = self.plan
        real = [j for j in range(plan.n) if j < plan.early or j >= plan.far_whole]
        out = len([j for j in real if j % 2 == 1 and j < plan.n - 2 * self.hop])
        return out if kind else len(real) - out

    def slot(self, f):
        return jnp.where(f < self.plan.partial, f, f - self.plan.partial)

    def c_copy(self, f):
        src = self.parts.at[self.slot(f), :, 1 - self.p.c]
        return remote(src, self.c_got.at[lax.rem(f, FEW)], self.fs.at[f, 0], self.fr.at[f, 0], self.p.sib)

    def x_copy(self, f):
        src = self.parts.at[self.slot(f), 1 - self.p.x, self.p.c]
        return remote(src, self.x_got.at[f], self.fs.at[f, 1], self.fr.at[f, 1], self.p.across)

    def y_copy(self, j):
        dst = self.y_got.at[lax.rem(j, RING)]
        return remote(self.acc.at[self.plan.at(j), :, self.others], dst, self.all_s.at[0], self.ur.at[j, 0], self.p.pair)

    def r_copy(self, j, a, to_up, index):
        dst = self.r_got.at[lax.rem(j, self.ring), index]
        device = self.p.up if to_up else self.p.down
        return remote(self.acc.at[self.plan.at(j), a, self.message], dst, self.all_s.at[1 + a], self.ur.at[j, 1 + index], device)

    def yz_copy(self, j, a):
        dst = self.yz_got.at[lax.rem(j, RING)]
        return remote(self.acc.at[self.plan.at(j), a, self.mid], dst, self.us.at[j], self.ur.at[j, 4], self.p.pair)

    def b_copy(self, j, a, to_up, from_acc):
        src = self.acc if from_acc else self.final
        device = self.p.up if to_up else self.p.down
        send = self.all_s.at[3 + 2 * a + (1 if to_up else 0)]
        return remote(src.at[self.plan.at(j), a, self.message], self.final.at[self.plan.at(j), a, self.message], send, self.ur.at[j, 5 + a], device)

    def keep_copy(self, j, a):
        return pltpu.make_async_copy(
            self.acc.at[self.plan.at(j), a, self.message], self.final.at[self.plan.at(j), a, self.message], self.ur.at[j, 5 + a]
        )

    def last_copy(self, j):
        rows = self.final.at[self.plan.at(j), :, self.own]
        return remote(rows, rows, self.all_s.at[7], self.all_r.at[0], self.p.pair)

    def tick(self, t):
        p, n, hop = self.p, self.plan.n, self.hop

        def stage(offset, body, cond=None):
            j = t - offset
            ok = (j >= 0) & (j < n) & self.plan.real(j)
            if cond is not None:
                ok = ok & cond
            pl.when(ok)(lambda: body(j))

        ok, f0 = self.plan.starting(t)
        pl.when(ok)(lambda: self.c_copy(f0).start())

        ok, f1 = self.plan.starting(t - hop)

        @pl.when(ok)
        def _():
            self.c_copy(f1).wait()
            at, slot, j = lax.rem(f1, FEW), self.slot(f1), self.plan.place(f1)
            self.parts[slot, 1 - p.x, p.c, :, :] += self.c_got[at, 1 - p.x]
            self.x_copy(f1).start()
            for a in (0, 1):
                rows = pl.ds(a * (self.unit // 2), self.unit // 2)
                self.acc[self.plan.at(j), a] = self.parts[slot, p.x, p.c, rows, :] + self.c_got[at, p.x, rows, :]

        f2 = t - hop - self.plan.later - self.plan.held
        pl.when((f2 >= self.plan.early) & (f2 < self.plan.partial))(lambda: self.x_copy(f2).wait_send())

        def gather(j):
            @pl.when(self.plan.is_partial(j))
            def _():
                f = self.plan.number(j)
                self.x_copy(f).wait_recv()
                pl.when((f < self.plan.early) | (f >= self.plan.partial))(lambda: self.x_copy(f).wait_send())
                for a in (0, 1):
                    rows = pl.ds(a * (self.unit // 2), self.unit // 2)
                    self.acc[self.plan.at(j), a] += self.x_got[f, rows, :]

            self.y_copy(j).start()

        stage(2 * hop, gather)

        def own_half(j):
            self.y_copy(j).wait_recv()
            self.acc[self.plan.at(j), :, self.own, :] += self.y_got[lax.rem(j, RING)]

        stage(self.at_y, own_half)

        for kind, (roots, reach) in enumerate(self.kinds):
            far = [jnp.abs(p.z - root) for root in roots]
            at_final = self.at_final(kind)

            def turn(offset, body, cond=None, kind=kind):
                mine = self.kind_is(t - offset, kind)
                stage(offset, body, mine if cond is None else mine & cond)

            for a, root in enumerate(roots):
                above, below, here = p.z > root, p.z < root, p.z == root

                def reduce(j, a=a, root=root, above=above, below=below, here=here):
                    def take(index):
                        self.r_copy(j, a, True, index).wait_recv()
                        self.acc[self.plan.at(j), a, self.message, :] += self.r_got[lax.rem(j, self.ring), index]

                    pl.when(((p.z >= root) & p.has_up) | (below & p.has_down))(lambda: take(a))
                    pl.when(here & p.has_down)(lambda: take(2))
                    pl.when(above)(lambda: self.r_copy(j, a, False, a).start())
                    pl.when(p.z < root - 1)(lambda: self.r_copy(j, a, True, a).start())
                    pl.when(p.z == root - 1)(lambda: self.r_copy(j, a, True, 2).start())
                    pl.when(here)(lambda: self.yz_copy(j, a).start())

                turn(self.at_y + (reach - far[a]) * hop, reduce)

            for a, root in enumerate(roots):
                above, below, here = p.z > root, p.z < root, p.z == root

                def forward(j, a=a, above=above, below=below):
                    self.b_copy(j, a, True, False).wait_recv()
                    pl.when(above & p.has_up)(lambda: self.b_copy(j, a, True, False).start())
                    pl.when(below & p.has_down)(lambda: self.b_copy(j, a, False, False).start())

                turn(at_final + far[a] * hop, forward, above | below)

                def settle(j, a=a):
                    self.yz_copy(j, a).wait()
                    self.acc[self.plan.at(j), a, self.mid, :] += self.yz_got[lax.rem(j, RING)]
                    pl.when(p.has_up)(lambda: self.b_copy(j, a, True, True).start())
                    pl.when(p.has_down)(lambda: self.b_copy(j, a, False, True).start())
                    self.keep_copy(j, a).start()

                turn(at_final, settle, here)

            def last(j, roots=roots):
                for a, root in enumerate(roots):
                    pl.when(p.z == root)(lambda a=a: self.keep_copy(j, a).wait())
                self.last_copy(j).start()

            turn(at_final + jnp.maximum(far[0], far[1]) * hop, last)

    def drain(self):
        p = self.p
        own, others = self.final.at[:, :, self.own], self.final.at[:, :, self.others]

        def sent(index, ref):
            remote(ref, ref, self.all_s.at[index], self.all_r.at[0], p.pair).wait_send()

        sent(0, others)
        for kind, (roots, _) in enumerate(self.kinds):
            message = self.final.at[pl.ds(0, self.count(kind)), 0, self.message]
            for a, root in enumerate(roots):
                pl.when(p.z != root)(lambda a=a, message=message: sent(1 + a, message))
                pl.when((p.z >= root) & p.has_up)(lambda a=a, message=message: sent(4 + 2 * a, message))
                pl.when((p.z <= root) & p.has_down)(lambda a=a, message=message: sent(3 + 2 * a, message))
        sent(7, own)
        remote(own, others, self.all_s.at[7], self.all_r.at[0], p.pair).wait_recv()


def exchange_scratch(plan, unit, lanes, line):
    slots = plan.partial + 1
    return dict(
        parts=pltpu.VMEM((slots, 2, 2, unit, lanes), f32),
        c_got=pltpu.VMEM((FEW, 2, unit, lanes), f32),
        x_got=pltpu.VMEM((plan.partials, unit, lanes), f32),
        y_got=pltpu.VMEM((RING, 2, shares(unit)[0], lanes), f32),
        r_got=pltpu.VMEM((line_ring(line, plan.hop), 3, sum(shares(unit)), lanes), f32),
        yz_got=pltpu.VMEM((RING, shares(unit)[1], lanes), f32),
        acc=pltpu.VMEM((plan.units, 2, unit // 2, lanes), f32),
        fs=pltpu.SemaphoreType.DMA((plan.partials, 2)),
        fr=pltpu.SemaphoreType.DMA((plan.partials, 2)),
        us=pltpu.SemaphoreType.DMA((plan.n,)),
        ur=pltpu.SemaphoreType.DMA((plan.n, 7)),
        all_s=pltpu.SemaphoreType.DMA((8,)),
        all_r=pltpu.SemaphoreType.DMA((1,)),
    )


SMALL = ("cb", "g1", "s1", "vb", "g2", "s2", "ub")
SMALL_ROWS = 40
NEAR_AT, FAR_AT, TABLE_AT = 0, 16, 32
CW = 3
FIRST_TICK = 1
ORDER = dict(early=0, whole_tick=10, later=11, second_early=9, second_start=34, held=10)


def backward_kernel(dims, names, plan, *refs):
    windows, base, d, ff, taps, line, unit = dims
    rows = windows * base
    blocks = ff // d
    lanes = d // SEQ
    half = taps // 2
    r = Refs(names, refs)
    p = Place(line)
    per = d // unit
    smalls = 2 * per * blocks

    def loop(n, body):
        def run(i, carry):
            body(i)
            return carry

        lax.fori_loop(0, n, run, 0)

    def live(w):
        where = p.s * base + lax.broadcasted_iota(jnp.int32, (base, 1), 0)
        return where < r.lengths[w]

    def window(w):
        return pl.ds(pl.multiple_of(w * base, base), base)

    which = {name: i for i, name in enumerate(SAVED)}

    def load(name, side):
        return pltpu.make_async_copy(r.of(side, name), getattr(r, name), r.lsem.at[which[name]])

    def load_h(side):
        return pltpu.make_async_copy(r.of(side, "full"), r.h, r.lsem.at[len(SAVED)])

    def load_conv(side, k, i):
        at = lax.rem(i, CW)
        return pltpu.make_async_copy(r.of(side, "conv").at[k], r.cw.at[at], r.csem.at[at])

    def wide_loads(side, b, slot):
        wide = ff // SEQ
        got = []
        for q in range(SEQ):
            at = pl.ds(pl.multiple_of(q * wide + b * lanes, lanes), lanes)
            put = pl.ds(q * lanes, lanes)
            got.append(pltpu.make_async_copy(r.of(side, "up").at[:, at], r.uw.at[slot, :, put], r.wsem.at[slot, q]))
            got.append(
                pltpu.make_async_copy(r.of(side, "down").at[at, :], r.vw.at[slot, put, :], r.wsem.at[slot, SEQ + q])
            )
        return got

    def start(side, *which_names):
        for name in which_names:
            load(name, side).start()

    def wait(side, *which_names):
        for name in which_names:
            load(name, side).wait()

    cot = pltpu.make_async_copy(r.cotangent, r.dy, r.lsem.at[len(SAVED) + 1])
    cot.start()
    start("far", "n2", "rs2", "mid")

    ex = Exchange(p, plan, unit, r)
    r.sums[...] = jnp.zeros(r.sums.shape, f32)
    r.parts[smalls, :, :, SMALL_ROWS:, :] = jnp.zeros((2, 2, unit - SMALL_ROWS, lanes), f32)

    @pl.when(p.s == 0)
    def _():
        r.dp[:, 0:HALO, :] = jnp.zeros((windows, HALO, d), f32)
        r.dw[:, 0:base, :] = jnp.zeros((windows, base, d), f32)

    @pl.when(p.s == SEQ - 1)
    def _():
        r.dp[:, HALO + base :, :] = jnp.zeros((windows, HALO, d), f32)
        r.dw[:, 2 * base :, :] = jnp.zeros((windows, base, d), f32)

    far_pad = half * SECOND_DILATION
    for ref, pad in ((r.dq_near, HALO), (r.dq_far, far_pad)):
        ref[:, 0:pad, :] = jnp.zeros((windows, pad, lanes), f32)
        ref[:, pad + SEQ * base :, :] = jnp.zeros((windows, pad, lanes), f32)

    p.greet(True)

    def add(kind, v):
        r.sums[kind] += jnp.sum(v.reshape(v.shape[0] // 8, 8, d), axis=0)

    def ffn_norm_back(side, at0):
        def body(w):
            at = window(w)
            dy = r.dy[at, :]
            if side == "far":
                dy = jnp.where(live(w), dy, 0.0)
            n = r.n2[at, :]
            add(at0 + 4, dy * n)
            add(at0 + 5, dy)
            dn = dy * r.of(side, "g2")[...]
            rs = r.rs2[at, 0:1]
            df = rs * (dn - row_mean(dn) - n * row_mean(dn * n))
            add(at0 + 3, df)
            h, l = split(df)
            r.df_h[at, :] = h
            r.df_l[at, :] = l
            r.dmid[at, :] = dy
            mh, ml = split(r.mid[at, :])
            r.mid_h[at, :] = mh
            r.mid_l[at, :] = ml

        loop(windows, body)

    def put_units(j, v):
        for i in range(per):
            for q in range(SEQ):
                r.parts[j + i, q // 2, q % 2, :, :] = v[i * unit : (i + 1) * unit, q * lanes : (q + 1) * lanes]

    def ffn_back(b, at0):
        slot = lax.rem(b, 2)
        for copy in wide_loads("far", b, slot):
            copy.wait()
        r.tmp[...] = dot3((r.df_h[...], r.df_l[...]), split(r.vw[slot]), NT)

        def act(i):
            at = pl.ds(pl.multiple_of(i * ROWS, ROWS), ROWS)
            dz = r.tmp[at, :] * r.gp[b, at, :]
            add(at0 + 6 + b, dz)
            h, l = split(dz)
            r.dz_h[at, :] = h
            r.dz_l[at, :] = l
            r.gp[b, at, :] = dz

        loop(rows // ROWS, act)

    def ffn_on(b):
        r.dmid[...] += dot3((r.dz_h[...], r.dz_l[...]), split(r.uw[lax.rem(b, 2)]), NT)

    def down_weights(b):
        put_units(2 * per * b, dot3((r.hid_h[b], r.hid_l[b]), (r.df_h[...], r.df_l[...]), TN))

    def up_weights(b):
        put_units(2 * per * b + per, dot3((r.mid_h[...], r.mid_l[...]), split(r.gp[b]), TN))

    def conv_norm_back(side, at0, put):
        def body(w):
            at = window(w)
            dmid, n = r.dmid[at, :], r.n1[at, :]
            add(at0 + 1, dmid * n)
            add(at0 + 2, dmid)
            dn = dmid * r.of(side, "g1")[...]
            dconv = r.gr1[at, :] * (dn - row_mean(dn) - n * row_mean(dn * n))
            add(at0, dconv)
            put(w, dconv)

        loop(windows, body)

    xs, xr = r.ssem, r.rsem

    def quarter_copies(src, at, pad, dq, sems):
        put = pl.ds(pl.multiple_of(pad + p.s * base, 8), base)
        got = []
        for i, s in enumerate((p.across_s, p.diag_s, p.sib_s)):
            cols = pl.ds(pl.multiple_of(s * lanes, lanes), lanes)
            mine = src.at[:, pl.ds(at, base), cols]
            got.append(remote(mine, dq.at[:, put, :], sems.at[0, i], sems.at[1, i], (p.w, s)))
        return got

    def keep_quarter(src, at, pad, dq):
        cols = pl.ds(pl.multiple_of(p.s * lanes, lanes), lanes)
        dq[:, pl.ds(pl.multiple_of(pad + p.s * base, 8), base), :] = src[:, at : at + base, cols]

    def weight_back(dq, pad, dilation, at, w, lo, hi):
        left = split(r.h[:, pl.ds(w, 1), :, :].reshape(SEQ * base, d))
        right = [
            dq[w, pad - (k - half) * dilation : pad - (k - half) * dilation + SEQ * base, :] for k in range(lo, hi)
        ]
        v = dot3(left, split(jnp.concatenate(right, axis=1)), TN)

        def put(first):
            for k in range(lo, hi):
                for i in range(2 * per):
                    piece = v[i * (unit // 2) : (i + 1) * (unit // 2), (k - lo) * lanes : (k - lo + 1) * lanes]
                    j = at + k * per + i // 2
                    if first:
                        r.acc[j, i % 2] = piece
                    else:
                        r.acc[j, i % 2] += piece

        pl.when(w == 0)(lambda: put(True))
        pl.when(w > 0)(lambda: put(False))

    groups = [(lo, min(lo + 3, taps)) for lo in range(0, taps, 3)]
    own_rows = pl.ds(base, base)

    def block_next():
        return remote(r.dw.at[:, own_rows], r.dw.at[:, pl.ds(0, base)], xs.at[0], xr.at[0], p.next)

    def block_prev():
        return remote(r.dw.at[:, own_rows], r.dw.at[:, pl.ds(2 * base, base)], xs.at[1], xr.at[1], p.prev)

    def far_quarters(w):
        at = pl.ds(w, 1)
        return quarter_copies(r.dw.at[at], base, far_pad, r.dq_far.at[at], r.qsem.at[w])

    def halo_next():
        return remote(r.dp.at[:, pl.ds(base, HALO)], r.dp.at[:, pl.ds(0, HALO)], xs.at[5], xr.at[5], p.next)

    def halo_prev():
        return remote(r.dp.at[:, pl.ds(HALO, HALO)], r.dp.at[:, pl.ds(HALO + base, HALO)], xs.at[6], xr.at[6], p.prev)

    def near_quarters():
        return quarter_copies(r.dp, HALO, HALO, r.dq_near, r.qsem.at[windows])

    def far_norm():
        wait("far", "n1", "gr1")

        def put(w, dconv):
            r.dw[w, base : 2 * base, :] = dconv
            for copy in far_quarters(w):
                copy.start()
            h, l = split(dconv)
            r.dw_h[w, base : 2 * base, :] = h
            r.dw_l[w, base : 2 * base, :] = l

        conv_norm_back("far", FAR_AT, put)
        start("near", "n2", "rs2", "n1", "gr1")
        keep_quarter(r.dw, base, far_pad, r.dq_far)
        r.tmp[...] = jnp.zeros((rows, d), f32)

    def far_tap(k):
        at = pl.ds(pl.multiple_of(base - (k - half) * SECOND_DILATION, SECOND_DILATION), base)
        lhs = (r.dw_h[:, at, :].reshape(rows, d), r.dw_l[:, at, :].reshape(rows, d))
        load_conv("far", k, k).wait()
        r.tmp[...] += dot3(lhs, split(r.cw[lax.rem(k, CW)]), NT)
        pl.when(k + CW < taps)(lambda: load_conv("far", k + CW, k + CW).start())
        pl.when(k + CW >= taps)(lambda: load_conv("near", k + CW - taps, k + CW).start())

    def far_halo():
        pl.when(p.has_prev)(lambda: block_next().wait_recv())
        pl.when(p.has_next)(lambda: block_prev().wait_recv())

        def halves(w):
            for at in (0, 2 * base):
                h, l = split(r.dw[w, at : at + base, :])
                r.dw_h[w, at : at + base, :] = h
                r.dw_l[w, at : at + base, :] = l

        loop(windows, halves)

    def far_end():
        def dx(w):
            at = window(w)
            r.dy[at, :] = r.dmid[at, :] + jnp.where(live(w), r.tmp[at, :], 0.0)

        loop(windows, dx)

    def near_begin():
        wait("near", "n2", "rs2", "mid", "gp", "hid_h", "hid_l")
        ffn_norm_back("near", NEAR_AT)

    def near_norm():
        wait("near", "n1", "gr1")

        def put(w, dconv):
            r.dp[w, HALO : HALO + base, :] = dconv

        conv_norm_back("near", NEAR_AT, put)
        pl.when(p.has_next)(lambda: halo_next().start())
        pl.when(p.has_prev)(lambda: halo_prev().start())
        for copy in near_quarters():
            copy.start()
        keep_quarter(r.dp, HALO, HALO, r.dq_near)

    def near_halo():
        pl.when(p.has_prev)(lambda: halo_next().wait_recv())
        pl.when(p.has_next)(lambda: halo_prev().wait_recv())

    def near_tap(k):
        at = HALO - (k - half) * FIRST_DILATION
        lhs = split(r.dp[:, at : at + base, :].reshape(rows, d))
        load_conv("near", k, taps + k).wait()
        v = dot3(lhs, split(r.cw[(taps + k) % CW]), NT)
        if k == 0:
            r.tmp[...] = v
        else:
            r.tmp[...] += v
        if k + CW < taps:
            load_conv("near", k + CW, taps + k + CW).start()

    def input_grad():
        return pltpu.make_async_copy(r.dy, r.input_grad, r.lsem.at[len(SAVED) + 1])

    def near_end():
        def dx(w):
            at = window(w)
            v = r.dmid[at, :] + jnp.where(live(w), r.tmp[at, :], 0.0)
            r.dy[at, :] = v
            v = jnp.sum(v.reshape(base // 8, 8, d), axis=0)
            species = r.species[w]
            for kind in range(SMALL_ROWS - TABLE_AT):
                r.sums[TABLE_AT + kind] += jnp.where(species == kind, v, 0.0)

        loop(windows, dx)
        input_grad().start()
        small = jnp.sum(r.sums[...], axis=1)
        for q in range(SEQ):
            r.parts[smalls, q // 2, q % 2, 0:SMALL_ROWS, :] = small[:, q * lanes : (q + 1) * lanes]

    cot.wait()
    wait("far", "n2", "rs2", "mid")
    for copy in wide_loads("far", 0, 0):
        copy.start()
    start("far", "gp")
    ffn_norm_back("far", FAR_AT)
    start("far", "hid_h", "hid_l")
    for copy in wide_loads("far", 1, 1):
        copy.start()
    start("far", "n1", "gr1")
    wait("far", "gp")

    at = 0

    def take(n):
        nonlocal at
        at += n
        return at - n

    far_ffn = take(blocks)
    far_norm_at = take(1)
    far_ffn_weights = take(blocks)
    far_weights = take(len(groups) * windows)
    far_taps = take(-(-taps // 2))
    far_end_at = take(1)
    near_begin_at = take(1)
    near_ffn = take(2 * blocks)
    near_norm_at = take(1)
    near_ffn_weights = take(2 * blocks)
    near_taps = take(-(-taps // 2))
    near_end_at = take(1)
    near_weights = take(len(groups) * windows)

    def step(i, carry):
        def when(first, n, body):
            pl.when((i >= first) & (i < first + n))(lambda: body(i - first))

        far = (i >= far_ffn) & (i < far_ffn + blocks)
        far_later = (i >= far_ffn_weights) & (i < far_ffn_weights + blocks)
        near = (i >= near_ffn) & (i < near_ffn + 2 * blocks)
        near_later = (i >= near_ffn_weights) & (i < near_ffn_weights + 2 * blocks)
        near_from = jnp.where(near, near_ffn, near_ffn_weights)
        b = jnp.where(far, i - far_ffn, jnp.where(far_later, i - far_ffn_weights, lax.div(i - near_from, 2)))
        turn = lax.rem(i - near_from, 2)
        pl.when(i == far_ffn_weights)(lambda: wait("far", "hid_h", "hid_l"))

        @pl.when(i == far_norm_at)
        def _():
            load_h("far").start()
            for k in range(CW):
                load_conv("far", k, k).start()

        pl.when(far | (near & (turn == 0)))(lambda: ffn_back(b, jnp.where(near, NEAR_AT, FAR_AT)))

        @pl.when(far | (near & (turn == 1)))
        def _():
            ffn_on(b)

            def fetch(side, b):
                for copy in wide_loads(side, b, lax.rem(b, 2)):
                    copy.start()

            pl.when(near & (b < blocks - 2))(lambda: fetch("near", b + 2))
            pl.when(far & (b < blocks - 2))(lambda: fetch("far", b + 2))
            pl.when(far & (b >= blocks - 2))(lambda: fetch("near", b - (blocks - 2)))

        pl.when(far_later | (near_later & (turn == 0)))(lambda: down_weights(b))
        pl.when(far_later | (near_later & (turn == 1)))(lambda: up_weights(b))
        when(far_norm_at, 1, lambda _: far_norm())

        @pl.when(i == far_weights)
        def _():
            start("near", "mid", "gp", "hid_h", "hid_l")
            for w in range(windows):
                for copy in far_quarters(w):
                    copy.wait()
            pl.when(p.has_next)(lambda: block_next().start())
            pl.when(p.has_prev)(lambda: block_prev().start())
            load_h("far").wait()

        for g, (lo, hi) in enumerate(groups):
            when(
                far_weights + g * windows,
                windows,
                lambda w, lo=lo, hi=hi: weight_back(
                    r.dq_far, far_pad, SECOND_DILATION, plan.far_whole - plan.gap, w, lo, hi
                ),
            )

        @pl.when(i == far_taps)
        def _():
            load_h("near").start()
            far_halo()

        def two_taps(m):
            far_tap(2 * m)
            pl.when(2 * m + 1 < taps)(lambda: far_tap(2 * m + 1))

        when(far_taps, -(-taps // 2), two_taps)
        when(far_end_at, 1, lambda _: far_end())
        when(near_begin_at, 1, lambda _: near_begin())
        when(near_norm_at, 1, lambda _: near_norm())
        pl.when(i == near_taps)(near_halo)
        for k in range(taps):
            when(near_taps + k // 2, 1, lambda _, k=k: near_tap(k))
        when(near_end_at, 1, lambda _: near_end())

        @pl.when(i == near_weights)
        def _():
            for copy in near_quarters():
                copy.wait()
            load_h("near").wait()

        for g, (lo, hi) in enumerate(groups):
            when(
                near_weights + g * windows,
                windows,
                lambda w, lo=lo, hi=hi: weight_back(r.dq_near, HALO, FIRST_DILATION, plan.near_whole - plan.gap, w, lo, hi),
            )
        ex.tick(i - FIRST_TICK)
        return carry

    lax.fori_loop(0, max(at, ex.ticks + FIRST_TICK), step, 0)
    ex.drain()

    @pl.when(p.has_next)
    def _():
        halo_next().wait_send()
        block_next().wait_send()

    @pl.when(p.has_prev)
    def _():
        halo_prev().wait_send()
        block_prev().wait_send()

    input_grad().wait()


def backward(line, lengths, species, table, cotangent, fulls, saved, near, far):
    windows, base, d = cotangent.shape
    taps, ff = near[0].shape[0], near[4].shape[1]
    rows, blocks, lanes = windows * base, ff // d, d // SEQ
    unit, hop = 256, (2 if line <= 4 else 1)
    per = d // unit
    plan = Plan(2 * per * blocks, taps * per, hop, **ORDER)
    n = plan.units
    smem = pl.BlockSpec(memory_space=pltpu.SMEM)
    vmem = pl.BlockSpec(memory_space=pltpu.VMEM)
    hbm = pl.BlockSpec(memory_space=pl.ANY)
    names, args, specs = ["lengths", "species", "cotangent"], [lengths, species, cotangent.reshape(rows, d)], [smem, smem, hbm]
    for side, block, full, kept in zip(("near", "far"), (near, far), fulls, saved, strict=True):
        names += [side + "_" + v for v in ("full", "conv", "up", "down") + SAVED + ("g1", "g2")]
        args += [full, block[0], block[4], block[6], *kept, block[2].reshape(1, -1), block[8].reshape(1, -1)]
        specs += [hbm] * (4 + len(SAVED)) + [vmem] * 2
    names += ["input_grad", "final"]
    scratch = {name: pltpu.VMEM(*v) for name, v in saved_shapes(rows, d, ff).items()}
    for name in ("dy", "dmid", "tmp"):
        scratch[name] = pltpu.VMEM((rows, d), f32)
    for name in ("mid_h", "mid_l", "df_h", "df_l", "dz_h", "dz_l"):
        scratch[name] = pltpu.VMEM((rows, d), bf16)
    scratch.update(
        h=pltpu.VMEM((SEQ, windows, base, d), f32),
        cw=pltpu.VMEM((CW, d, d), f32),
        uw=pltpu.VMEM((2, d, d), f32),
        vw=pltpu.VMEM((2, d, d), f32),
        dp=pltpu.VMEM((windows, base + 2 * HALO, d), f32),
        dw=pltpu.VMEM((windows, 3 * base, d), f32),
        dw_h=pltpu.VMEM((windows, 3 * base, d), bf16),
        dw_l=pltpu.VMEM((windows, 3 * base, d), bf16),
        dq_near=pltpu.VMEM((windows, SEQ * base + 2 * HALO, lanes), f32),
        dq_far=pltpu.VMEM((windows, SEQ * base + taps // 2 * 2 * SECOND_DILATION, lanes), f32),
        sums=pltpu.VMEM((SMALL_ROWS, 8, d), f32),
        lsem=pltpu.SemaphoreType.DMA((len(SAVED) + 2,)),
        csem=pltpu.SemaphoreType.DMA((CW,)),
        wsem=pltpu.SemaphoreType.DMA((2, 2 * SEQ)),
        ssem=pltpu.SemaphoreType.DMA((7,)),
        rsem=pltpu.SemaphoreType.DMA((7,)),
        qsem=pltpu.SemaphoreType.DMA((windows + 1, 2, 3)),
    )
    scratch.update(exchange_scratch(plan, unit, lanes, line))
    names += list(scratch)
    input_grad, final = pl.pallas_call(
        functools.partial(backward_kernel, (windows, base, d, ff, taps, line, unit), names, plan),
        out_shape=[jax.ShapeDtypeStruct((rows, d), f32), jax.ShapeDtypeStruct((n, 2, unit // 2, lanes), f32)],
        in_specs=specs,
        out_specs=[hbm, hbm],
        scratch_shapes=list(scratch.values()),
        compiler_params=pltpu.CompilerParams(
            collective_id=1, has_side_effects=True, vmem_limit_bytes=64 * 1024 * 1024 - 65536
        ),
        name="backward",
    )(*args)

    grads = unpack(plan, windows, rows, blocks, taps, d, ff, unit, final.reshape(n, unit, lanes))
    table_grad, near_grads, far_grads = grads[0], grads[1:11], grads[11:]
    shapes = [(taps, d, lanes), (lanes,), (lanes,), (lanes,), (d, ff // SEQ), (ff // SEQ,), (ff, lanes)] + 3 * [(lanes,)]
    near_grads = [v.reshape(shape) for v, shape in zip(near_grads, shapes, strict=True)]
    far_grads = [v.reshape(shape) for v, shape in zip(far_grads, shapes, strict=True)]
    return input_grad.reshape(cotangent.shape), table_grad, near_grads, far_grads


CHUNK = 10


def unpack_kernel(plan, dims, final, table, *refs):
    blocks, taps, d, ff, unit = dims
    lanes = d // SEQ
    per = d // unit
    outs, held, in_sem, out_sem = refs[:20], refs[20], refs[21], refs[22]
    total = final.shape[0]
    fetches = []
    for j in range(0, total, CHUNK):
        some = pl.ds(j, min(CHUNK, total - j))
        fetches.append(pltpu.make_async_copy(final.at[some], held.at[some], in_sem.at[j // CHUNK]))
    fetched = [False] * len(fetches)
    for fetch in fetches:
        fetch.start()

    def copy(src, dst):
        pltpu.make_async_copy(src, dst, out_sem.at[0]).start()

    def unit_at(j):
        j = plan.at(j)
        if not fetched[j // CHUNK]:
            fetches[j // CHUNK].wait()
            fetched[j // CHUNK] = True
        return held.at[j]

    for side, first, whole in ((outs[10:], 0, plan.far_whole), (outs[:10], plan.partial, plan.near_whole)):
        cw, _, _, _, uw, _, vw, _, _, _ = side
        for i in range(taps * per):
            copy(unit_at(whole + i), cw.at[i // per, pl.ds(i % per * unit, unit)])
        for b in range(blocks):
            cols = pl.ds(b * lanes, lanes)
            for i in range(per):
                f = first + 2 * per * b + i
                for q in range(unit // lanes):
                    row = (i * (unit // lanes) + q) * (ff // SEQ) + b * lanes
                    copy(unit_at(plan.place(f)).at[pl.ds(q * lanes, lanes)], vw.at[pl.ds(row, lanes)])
                copy(unit_at(plan.place(f + per)), uw.at[pl.ds(i * unit, unit), cols])
    small = unit_at(plan.place(plan.partials - 1))
    copy(small.at[pl.ds(TABLE_AT, SMALL_ROWS - TABLE_AT)], table)
    for (_, cb, g1, s1, _, ub, _, vb, g2, s2), at in ((outs[:10], NEAR_AT), (outs[10:], FAR_AT)):
        for i, ref in enumerate((cb, g1, s1, vb, g2, s2)):
            copy(small.at[pl.ds(at + i, 1)], ref)
        for b in range(blocks):
            copy(small.at[pl.ds(at + 6 + b, 1)], ub.at[:, pl.ds(b * lanes, lanes)])
    assert all(fetched)
    for ref in (table, *outs):
        pltpu.make_async_copy(ref, ref, out_sem.at[0]).wait()


def unpack(plan, windows, rows, blocks, taps, d, ff, unit, final):
    lanes = d // SEQ
    one = (1, lanes)
    block = [(taps, d, lanes), one, one, one, (d, ff // SEQ), (1, ff // SEQ), (ff, lanes), one, one, one]
    hbm = pl.BlockSpec(memory_space=pl.ANY)
    outs = [(SMALL_ROWS - TABLE_AT, lanes)] + block + block
    return pl.pallas_call(
        functools.partial(unpack_kernel, plan, (blocks, taps, d, ff, unit)),
        out_shape=[jax.ShapeDtypeStruct(v, f32) for v in outs],
        in_specs=[hbm],
        out_specs=[hbm] * len(outs),
        scratch_shapes=[
            pltpu.VMEM((plan.units, unit, lanes), f32),
            pltpu.SemaphoreType.DMA((-(-plan.units // CHUNK),)),
            pltpu.SemaphoreType.DMA((1,)),
        ],
        compiler_params=pltpu.CompilerParams(vmem_limit_bytes=60 * 1024 * 1024),
        name="unpack",
    )(final)


def on_device(inputs, species, lengths, species_table, *rest):
    near, far, cotangent = rest[:10], rest[10:20], rest[20]
    line = lax.axis_size("win") // 2
    output, near_full, far_full, near_saved, far_saved = forward(
        line, lengths, species, species_table, inputs, near, far
    )
    input_grad, table_grad, near_grads, far_grads = backward(
        line, lengths, species, species_table, cotangent, (near_full, far_full), (near_saved, far_saved), near, far
    )
    return (output, input_grad, table_grad, *near_grads, *far_grads)


def solution(mesh):
    split_windows = P("win", "seq", None)
    block_grads = (P(None, None, "seq"), P("seq"), P("seq"), P("seq"), P(None, "seq"), P("seq"), P(None, "seq"))
    block_grads += (P("seq"), P("seq"), P("seq"))
    return jax.shard_map(
        on_device,
        mesh=mesh,
        in_specs=(split_windows, P("win"), P("win")) + (P(),) * 21 + (split_windows,),
        out_specs=(split_windows, split_windows, P(None, "seq")) + block_grads + block_grads,
        check_vma=False,
    )
```

```python
import functools

import jax
import jax.numpy as jnp
from jax import lax
from jax.experimental import pallas as pl
from jax.experimental.pallas import tpu as pltpu
from jax.sharding import PartitionSpec as P

FIRST_DILATION = 1
SECOND_DILATION = 32
EPS = 1e-05
ROWS = 32
HALO = 8
SEQ = 4
f32, bf16 = jnp.float32, jnp.bfloat16
MESH_ID = pl.DeviceIdType.MESH


def split(v):
    high = v.astype(bf16)
    return high, (v - high.astype(f32)).astype(bf16)


def dot(left, right, dims):
    return lax.dot_general(left, right, (dims, ((), ())), preferred_element_type=f32)


def dot3(left, right, dims=((1,), (0,))):
    (lh, ll), (rh, rl) = left, right
    return dot(lh, rh, dims) + (dot(lh, rl, dims) + dot(ll, rh, dims))


NT = ((1,), (1,))
TN = ((0,), (0,))


def gauss(z):
    size = jnp.abs(z)
    t = 1.0 / (1.0 + (0.3275911 * 0.7071067811865476) * size)
    e = jnp.exp(-0.5 * z * z)
    poly = 0.5 * 1.061405429
    for term in (-1.453152027, 1.421413741, -0.284496736, 0.254829592):
        poly = poly * t + 0.5 * term
    tail = poly * t * e
    return jnp.where(z >= 0, 1.0 - tail, tail), (z * 0.3989422804014327) * e


def row_mean(v):
    return jnp.mean(v, axis=-1, keepdims=True)


def remote(src, dst, send, recv, device):
    return pltpu.make_async_remote_copy(
        src_ref=src, dst_ref=dst, send_sem=send, recv_sem=recv, device_id=device, device_id_type=MESH_ID
    )


class Refs:
    def __init__(self, names, refs):
        for name, ref in zip(names, refs, strict=True):
            setattr(self, name, ref)

    def of(self, side, name):
        return getattr(self, side + "_" + name)


class Place:
    def __init__(self, line):
        w, s = lax.axis_index("win"), lax.axis_index("seq")
        self.w, self.s, self.line = w, s, line
        self.z, self.y = lax.div(w, 2), lax.rem(w, 2)
        self.x, self.c = lax.div(s, 2), lax.rem(s, 2)
        self.sib_s = 2 * self.x + 1 - self.c
        self.across_s = 2 * (1 - self.x) + self.c
        self.diag_s = SEQ - 1 - s
        self.sib, self.across, self.diag = (w, self.sib_s), (w, self.across_s), (w, self.diag_s)
        self.pair = (2 * self.z + 1 - self.y, s)
        self.up, self.down = (w + 2, s), (w - 2, s)
        self.next, self.prev = (w, s + 1), (w, s - 1)
        self.has_up, self.has_down = self.z < line - 1, self.z > 0
        self.has_next, self.has_prev = s < SEQ - 1, s > 0
        self.inner = self.c != self.x

    def greet(self, whole):
        barrier = pltpu.get_barrier_semaphore()

        def signal(device):
            pl.semaphore_signal(barrier, inc=1, device_id=device, device_id_type=MESH_ID)

        for device in (self.sib, self.across, self.diag):
            signal(device)
        if whole:
            signal(self.pair)
            pl.when(self.has_up)(lambda: signal(self.up))
            pl.when(self.has_down)(lambda: signal(self.down))

    def await_all(self, whole):
        line = 1 + self.has_up.astype(jnp.int32) + self.has_down.astype(jnp.int32)
        pl.semaphore_wait(pltpu.get_barrier_semaphore(), 3 + line if whole else 3)


AHEAD = 4
LARGE, SMALLER = ("hid_h", "hid_l", "gp"), ("mid", "n1", "gr1", "n2", "rs2")
SAVED = ("mid", "n1", "gr1", "n2", "rs2", "hid_h", "hid_l", "gp")


def saved_shapes(rows, d, ff):
    blocks = ff // d
    return dict(
        mid=((rows, d), f32),
        n1=((rows, d), f32),
        gr1=((rows, d), f32),
        n2=((rows, d), f32),
        rs2=((rows, 128), f32),
        hid_h=((blocks, rows, d), bf16),
        hid_l=((blocks, rows, d), bf16),
        gp=((blocks, rows, d), f32),
    )


def ff_columns(ref, b, d, parts, lanes):
    wide = d * parts // SEQ
    return [ref[:, pl.ds(pl.multiple_of(q * wide + b * lanes, lanes), lanes)] for q in range(SEQ)]


def ff_rows(ref, b, d, parts, lanes):
    wide = d * parts // SEQ
    return [ref[pl.ds(pl.multiple_of(q * wide + b * lanes, lanes), lanes), :] for q in range(SEQ)]


def forward_kernel(dims, *refs):
    windows, base, d, ff, taps, line = dims
    rows = windows * base
    blocks = ff // d
    lanes = d // SEQ
    names = ["lengths", "species", "table", "inputs"]
    weights = ("conv", "up", "down")
    vectors = ("cb", "g1", "s1", "ub", "vb", "g2", "s2")
    for side in ("near", "far"):
        names += [side + "_" + v for v in weights + vectors]
    names += ["output", "near_full", "far_full"]
    for side in ("near", "far"):
        names += [side + "_out_" + v for v in SAVED]
    for side in ("near", "far"):
        names += [side + "_" + v for v in SAVED]
    names += ["cw", "uw", "vw", "x", "acc", "zb", "mid_h", "mid_l", "hp", "hq", "hq_h", "hq_l", "own"]
    names += ["own2", "out_buf", "csem", "wsem", "osem", "bsem", "gsem", "ssem", "rsem"]
    r = Refs(names, refs)
    p = Place(line)
    p.greet(False)

    def conv_weights(side, k):
        return pltpu.make_async_copy(r.of(side, "conv").at[k], r.cw.at[k], r.csem.at[k])

    def wide_weights(side, i):
        src, dst = (("up", r.uw), ("down", r.vw))[i]
        return pltpu.make_async_copy(r.of(side, src), dst, r.wsem.at[i])

    order = [taps // 2] + [k for k in range(taps) if k != taps // 2]
    for k in order[:AHEAD]:
        conv_weights("near", k).start()

    def live(w):
        where = p.s * base + lax.broadcasted_iota(jnp.int32, (base, 1), 0)
        return where < r.lengths[w]

    def window(w):
        return pl.ds(pl.multiple_of(w * base, base), base)

    def step_rows(i):
        return pl.ds(pl.multiple_of(i * ROWS, ROWS), ROWS)

    def loop(n, body):
        def run(i, carry):
            body(i)
            return carry

        lax.fori_loop(0, n, run, 0)

    def begin(w):
        v = r.inputs[w] + r.table[pl.ds(r.species[w], 1), :]
        r.x[window(w), :] = v
        h = jnp.where(live(w), v, 0.0)
        r.hp[w, HALO : HALO + base, :] = h
        r.own[w] = h

    loop(windows, begin)

    @pl.when(p.s == 0)
    def _():
        r.hp[:, 0:HALO, :] = jnp.zeros((windows, HALO, d), f32)
        r.hq[:, 0:base, :] = jnp.zeros((windows, base, d), f32)

    @pl.when(p.s == SEQ - 1)
    def _():
        r.hp[:, HALO + base :, :] = jnp.zeros((windows, HALO, d), f32)
        r.hq[:, 2 * base :, :] = jnp.zeros((windows, base, d), f32)

    p.await_all(False)
    ssem, rsem = r.ssem, r.rsem

    def halo_next():
        return remote(
            r.hp.at[:, pl.ds(base, HALO)], r.hp.at[:, pl.ds(0, HALO)], ssem.at[0], rsem.at[0], p.next
        )

    def halo_prev():
        return remote(
            r.hp.at[:, pl.ds(HALO, HALO)], r.hp.at[:, pl.ds(HALO + base, HALO)], ssem.at[1], rsem.at[1], p.prev
        )

    pl.when(p.has_next)(lambda: halo_next().start())
    pl.when(p.has_prev)(lambda: halo_prev().start())

    other_inner = (p.w, jnp.where(p.x == 0, 2, 1))
    first_other = 2 * (1 - p.x)
    other_outer = jnp.where(p.x == 0, 3, 0)

    def bulk_own(full):
        return r.own if full == "near" else r.own2

    def bulk_keep(full, at):
        return pltpu.make_async_copy(bulk_own(full), r.of(full, "full").at[p.s], ssem.at[at])

    def bulk_sib(full, at, block, src=None):
        return remote(
            bulk_own(full) if src is None else src, r.of(full, "full").at[block], ssem.at[at + 1], rsem.at[at + 1], p.sib
        )

    def bulk_across(full, at):
        return remote(bulk_own(full), r.of(full, "full").at[p.s], ssem.at[at + 2], rsem.at[at + 2 + lax.rem(p.s, 2)], other_inner)

    def bulk_relay(full, at, block, i, src=None):
        src = r.of(full, "full").at[block] if src is None else src
        return remote(src, r.of(full, "full").at[block], ssem.at[at + 3 + i], rsem.at[at + 4 + i], p.sib)

    NEAR, FAR = 4, 12
    bulk_keep("near", NEAR).start()
    bulk_sib("near", NEAR, p.s).start()
    bulk_across("near", NEAR).start()

    def near_tap(k, lo, hi):
        at = HALO + (k - taps // 2) * FIRST_DILATION
        return dot3(split(r.hp[lo:hi, at : at + base, :].reshape((hi - lo) * base, d)), split(r.cw[k]))

    def conv_tail(side, lo, hi):
        def body(w):
            at = window(w)
            v = r.acc[at, :] + r.of(side, "cb")[...]
            cdf, zd = gauss(v)
            a = v * cdf
            center = a - row_mean(a)
            rs = lax.rsqrt(row_mean(center * center) + EPS)
            n = center * rs
            mid = r.x[at, :] + (n * r.of(side, "g1")[...] + r.of(side, "s1")[...])
            r.of(side, "n1")[at, :] = n
            r.of(side, "gr1")[at, :] = (cdf + zd) * rs
            r.of(side, "mid")[at, :] = mid
            h, l = split(mid)
            r.mid_h[at, :] = h
            r.mid_l[at, :] = l

        loop(hi - lo, lambda i: body(i + lo))

    def ffn(side, lo, hi):
        part = pl.ds(lo * base, (hi - lo) * base)

        def body(b):
            up = jnp.concatenate(ff_columns(r.uw, b, d, blocks, lanes), axis=1)
            r.zb[part, :] = dot3((r.mid_h[part, :], r.mid_l[part, :]), split(up))
            bias = jnp.concatenate(ff_columns(r.of(side, "ub"), b, d, blocks, lanes), axis=1)

            def act(i):
                at = pl.ds(pl.multiple_of(lo * base + i * ROWS, ROWS), ROWS)
                z = r.zb[at, :] + bias
                cdf, zd = gauss(z)
                h, l = split(z * cdf)
                r.of(side, "hid_h")[b, at, :] = h
                r.of(side, "hid_l")[b, at, :] = l
                r.of(side, "gp")[b, at, :] = cdf + zd

            loop((hi - lo) * base // ROWS, act)
            if hi == windows:
                for name in LARGE:
                    save_part(side, name, b).start()
            down = jnp.concatenate(ff_rows(r.vw, b, d, blocks, lanes), axis=0)
            f = dot3((r.of(side, "hid_h")[b, part, :], r.of(side, "hid_l")[b, part, :]), split(down))

            @pl.when(b == 0)
            def _():
                r.acc[part, :] = f

            @pl.when(b > 0)
            def _():
                r.acc[part, :] += f

        loop(blocks, body)

    def ffn_tail(side, keep, lo, hi):
        def body(w):
            at = window(w)
            f = r.acc[at, :] + r.of(side, "vb")[...]
            center = f - row_mean(f)
            rs = lax.rsqrt(row_mean(center * center) + EPS)
            n = center * rs
            r.of(side, "n2")[at, :] = n
            r.of(side, "rs2")[at, :] = jnp.broadcast_to(rs, (base, 128))
            keep(w, at, r.of(side, "mid")[at, :] + (n * r.of(side, "g2")[...] + r.of(side, "s2")[...]))

        loop(hi - lo, lambda i: body(i + lo))

    which = {name: i for i, name in enumerate(SAVED)}

    def save_sem(side, name):
        return r.osem.at[(0 if side == "near" else len(SAVED)) + which[name]]

    def save(side, name):
        return pltpu.make_async_copy(r.of(side, name), r.of(side, "out_" + name), save_sem(side, name))

    def save_part(side, name, b):
        return pltpu.make_async_copy(
            r.of(side, name).at[b], r.of(side, "out_" + name).at[b], r.bsem.at[0 if side == "near" else 1, which[name], b]
        )

    def block_next(g):
        lo, hi = groups[g]
        at = pl.ds(lo, hi - lo)
        return remote(r.own2.at[at], r.hq.at[at, pl.ds(0, base)], r.gsem.at[0, g, 0], r.gsem.at[1, g, 0], p.next)

    def block_prev(g):
        lo, hi = groups[g]
        at = pl.ds(lo, hi - lo)
        return remote(r.own2.at[at], r.hq.at[at, pl.ds(2 * base, base)], r.gsem.at[0, g, 1], r.gsem.at[1, g, 1], p.prev)

    def middle(w, at, v):
        r.x[at, :] = v
        h = jnp.where(live(w), v, 0.0)
        r.hq[w, base : 2 * base, :] = h
        r.own2[w] = h
        hh, hl = split(h)
        r.hq_h[w, base : 2 * base, :] = hh
        r.hq_l[w, base : 2 * base, :] = hl

    groups = ((0, windows - 1), (windows - 1, windows))
    for g, (lo, hi) in enumerate(groups):
        part = pl.ds(lo * base, (hi - lo) * base)
        for n, k in enumerate(order):
            if g == 0:
                conv_weights("near", k).wait()
                if n + AHEAD < taps:
                    conv_weights("near", order[n + AHEAD]).start()
                if n == taps - AHEAD:
                    for i in (0, 1):
                        wide_weights("near", i).start()
            if g == 0 and n == 1:
                pl.when(p.has_prev)(lambda: halo_next().wait_recv())
                pl.when(p.has_next)(lambda: halo_prev().wait_recv())
            v = near_tap(k, lo, hi)
            if n == 0:
                r.acc[part, :] = v
            else:
                r.acc[part, :] += v
        if hi == windows:
            for k in order:
                conv_weights("far", k).start()
        conv_tail("near", lo, hi)
        if g == 0:
            for i in (0, 1):
                wide_weights("near", i).wait()
        ffn("near", lo, hi)
        if hi == windows:
            for i in (0, 1):
                wide_weights("far", i).start()
        ffn_tail("near", middle, lo, hi)
        pl.when(p.has_next)(lambda g=g: block_next(g).start())
        pl.when(p.has_prev)(lambda g=g: block_prev(g).start())

    bulk_keep("far", FAR).start()
    bulk_sib("far", FAR, p.s).start()
    for name in SMALLER:
        save("near", name).start()

    @pl.when(p.inner)
    def _():
        for i in (0, 1):
            remote(
                r.own, r.near_full.at[first_other + i], ssem.at[NEAR + 2], rsem.at[NEAR + 2 + i], other_inner
            ).wait_recv()
            bulk_relay("near", NEAR, first_other + i, i).start()

    def far_tap(k, lo, hi):
        at = pl.ds(pl.multiple_of(base + (k - taps // 2) * SECOND_DILATION, SECOND_DILATION), base)
        some = (hi - lo) * base
        lhs = (r.hq_h[lo:hi, at, :].reshape(some, d), r.hq_l[lo:hi, at, :].reshape(some, d))
        if lo == 0:
            conv_weights("far", k).wait()
        return dot3(lhs, split(r.cw[k]))

    def far_conv(g, first, some):
        lo, hi = groups[g]
        part = pl.ds(lo * base, (hi - lo) * base)
        for k in some:
            v = far_tap(k, lo, hi)
            if k == first:
                r.acc[part, :] = v
            else:
                r.acc[part, :] += v

    def take_halo(g):
        lo, hi = groups[g]
        pl.when(p.has_prev)(lambda: block_next(g).wait_recv())
        pl.when(p.has_next)(lambda: block_prev(g).wait_recv())

        def halves(w):
            for at in (0, 2 * base):
                h, l = split(r.hq[w, at : at + base, :])
                r.hq_h[w, at : at + base, :] = h
                r.hq_l[w, at : at + base, :] = l

        loop(hi - lo, lambda i: halves(i + lo))

    far_conv(0, order[0], order[:1])
    take_halo(0)
    far_conv(0, order[0], order[1:])
    far_conv(1, order[0], order[:1])
    take_halo(1)

    @pl.when(jnp.logical_not(p.inner))
    def _():
        bulk_across("far", FAR).start()

    def keep_inner(at):
        return pltpu.make_async_copy(
            r.hq.at[:, pl.ds(at, base)], r.far_full.at[other_inner[1]], ssem.at[FAR + 2]
        )

    def relay_inner(at):
        return bulk_relay("far", FAR, other_inner[1], 0, r.hq.at[:, pl.ds(at, base)])

    inner_at = pl.multiple_of(jnp.where(p.x == 0, 2 * base, 0), base)

    @pl.when(p.inner)
    def _():
        keep_inner(inner_at).start()
        relay_inner(inner_at).start()

    far_conv(1, order[0], order[1:])
    conv_tail("far", 0, windows)
    for name in ("mid", "n1", "gr1"):
        save("far", name).start()
    for i in (0, 1):
        wide_weights("far", i).wait()
    ffn("far", 0, windows)

    def finish(w, at, v):
        r.out_buf[at, :] = jnp.where(live(w), v, 0.0)

    ffn_tail("far", finish, 0, windows)
    for name in ("n2", "rs2"):
        save("far", name).start()
    result = pltpu.make_async_copy(r.out_buf, r.output, r.osem.at[2 * len(SAVED)])
    result.start()

    @pl.when(p.inner)
    def _():
        remote(
            r.own, r.far_full.at[other_outer], ssem.at[FAR + 2], rsem.at[FAR + 2 + lax.rem(other_outer, 2)], other_inner
        ).wait_recv()
        bulk_relay("far", FAR, other_outer, 1).start()
        keep_inner(inner_at).wait()
        relay_inner(inner_at).wait_send()
        bulk_relay("far", FAR, other_outer, 1).wait_send()
        for i in (0, 1):
            bulk_relay("near", NEAR, first_other + i, i).wait_send()

    @pl.when(jnp.logical_not(p.inner))
    def _():
        bulk_across("far", FAR).wait_send()
        for full, at in (("near", NEAR), ("far", FAR)):
            for i in (0, 1):
                bulk_relay(full, at, first_other + i, i).wait_recv()

    for full, at in (("near", NEAR), ("far", FAR)):
        bulk_sib(full, at, p.sib_s).wait_recv()
    for full, at in (("near", NEAR), ("far", FAR)):
        bulk_sib(full, at, p.s).wait_send()
        bulk_keep(full, at).wait()
    bulk_across("near", NEAR).wait_send()

    @pl.when(p.has_next)
    def _():
        halo_next().wait_send()
        for g in range(len(groups)):
            block_next(g).wait_send()

    @pl.when(p.has_prev)
    def _():
        halo_prev().wait_send()
        for g in range(len(groups)):
            block_prev(g).wait_send()

    result.wait()
    for side in ("near", "far"):
        for name in SMALLER:
            save(side, name).wait()
        for name in LARGE:
            for b in range(blocks):
                save_part(side, name, b).wait()


def forward(line, lengths, species, table, inputs, near, far):
    windows, base, d = inputs.shape
    taps, ff = near[0].shape[0], near[4].shape[1]
    rows, blocks = windows * base, ff // d
    smem = pl.BlockSpec(memory_space=pltpu.SMEM)
    vmem = pl.BlockSpec(memory_space=pltpu.VMEM)
    hbm = pl.BlockSpec(memory_space=pl.ANY)
    args, specs = [lengths, species, table, inputs], [smem, smem, vmem, vmem]
    for cw, cb, g1, s1, uw, ub, vw, vb, g2, s2 in (near, far):
        args += [cw, uw, vw] + [v.reshape(1, -1) for v in (cb, g1, s1, ub, vb, g2, s2)]
        specs += [hbm] * 3 + [vmem] * 7
    kept = saved_shapes(rows, d, ff)
    full = ((SEQ, windows, base, d), f32)
    outs = [((rows, d), f32), full, full] + 2 * [kept[v] for v in SAVED]
    scratch = 2 * [pltpu.VMEM(*kept[v]) for v in SAVED]
    scratch += [
        pltpu.VMEM((taps, d, d), f32),
        pltpu.VMEM((d, ff), f32),
        pltpu.VMEM((ff, d), f32),
        pltpu.VMEM((rows, d), f32),
        pltpu.VMEM((rows, d), f32),
        pltpu.VMEM((rows, d), f32),
        pltpu.VMEM((rows, d), bf16),
        pltpu.VMEM((rows, d), bf16),
        pltpu.VMEM((windows, base + 2 * HALO, d), f32),
        pltpu.VMEM((windows, 3 * base, d), f32),
        pltpu.VMEM((windows, 3 * base, d), bf16),
        pltpu.VMEM((windows, 3 * base, d), bf16),
        pltpu.VMEM((windows, base, d), f32),
        pltpu.VMEM((windows, base, d), f32),
        pltpu.VMEM((rows, d), f32),
        pltpu.SemaphoreType.DMA((taps,)),
        pltpu.SemaphoreType.DMA((2,)),
        pltpu.SemaphoreType.DMA((2 * len(SAVED) + 1,)),
        pltpu.SemaphoreType.DMA((2, len(SAVED), blocks)),
        pltpu.SemaphoreType.DMA((2, 2, 2)),
        pltpu.SemaphoreType.DMA((20,)),
        pltpu.SemaphoreType.DMA((20,)),
    ]
    got = pl.pallas_call(
        functools.partial(forward_kernel, (windows, base, d, ff, taps, line)),
        out_shape=[jax.ShapeDtypeStruct(*v) for v in outs],
        in_specs=specs,
        out_specs=[hbm] * len(outs),
        scratch_shapes=scratch,
        compiler_params=pltpu.CompilerParams(
            collective_id=0, has_side_effects=True, vmem_limit_bytes=60 * 1024 * 1024
        ),
        name="forward",
    )(*args)
    n = len(SAVED)
    return got[0].reshape(inputs.shape), got[1], got[2], got[3 : 3 + n], got[3 + n :]


RING = 12
FEW = 6
EXCHANGE_REFS = tuple(
    dict(parts=0, c_got=0, x_got=0, y_got=0, r_got=0, yz_got=0, acc=0, final=0, fs=0, fr=0, us=0, ur=0, all_s=0, all_r=0)
)


def line_ring(line, hop):
    return max(RING, hop * (1 + 2 * (line // 2 + 1)) + 1)


def shares(unit):
    outer = 5 * unit // 32
    return outer, unit // 2 - 2 * outer


class Plan:
    def __init__(self, partial, whole, hop, early, whole_tick, later, second_early, second_start, held):
        gap = whole_tick - 2 * hop - early
        self.partial, self.whole, self.hop, self.early, self.gap = partial, whole, hop, early, gap
        self.later, self.second_start, self.held = later, second_start, held
        self.partials = 2 * partial + 1
        self.far_whole = early + gap
        self.shift = gap + whole
        self.before = partial + second_early
        self.near_whole = self.shift + self.before
        self.n = gap + self.partials + 2 * whole
        self.units = self.n - gap

    def at(self, j):
        if isinstance(j, int):
            return j if j < self.early else j - self.gap
        return jnp.where(j < self.early, j, j - self.gap)

    def real(self, j):
        return (j < self.early) | (j >= self.far_whole)

    def is_partial(self, j):
        far_or_first = (j >= self.early + self.shift) & (j < self.near_whole)
        return (j < self.early) | far_or_first | (j >= self.near_whole + self.whole)

    def number(self, j):
        return jnp.where(
            j < self.early, j, jnp.where(j < self.near_whole, j - self.shift, j - self.shift - self.whole)
        )

    def place(self, f):
        if isinstance(f, int):
            return f if f < self.early else f + self.shift + (self.whole if f >= self.before else 0)
        return jnp.where(f < self.early, f, jnp.where(f < self.before, f, f + self.whole) + self.shift)

    def starting(self, t):
        first = (t >= 0) & (t < self.early)
        far = (t >= self.early + self.later) & (t < self.partial + self.later)
        near = (t >= self.second_start) & (t < self.second_start + self.partial + 1)
        return first | far | near, jnp.where(
            first, t, jnp.where(far, t - self.later, t - self.second_start + self.partial)
        )


class Exchange:
    def __init__(self, place, plan, unit, refs):
        self.p, self.plan, self.unit, self.hop = place, plan, unit, plan.hop
        for name in EXCHANGE_REFS:
            setattr(self, name, getattr(refs, name))
        line, hop = place.line, plan.hop
        self.kinds = (((line // 2 - 1, line // 2), line // 2), ((line // 2 - 2, line // 2 + 1), line // 2 + 1))
        self.ring = line_ring(line, hop)
        self.at_y = 3 * hop
        self.ticks = plan.n + self.at_final(0) + self.kinds[0][1] * hop + 1
        y, (outer, mid) = place.y, shares(unit)
        self.own = pl.ds(pl.multiple_of(y * (outer + mid), 8), outer)
        self.others = pl.ds(pl.multiple_of((1 - y) * (outer + mid), 8), outer)
        self.mid = pl.ds(outer, mid)
        self.message = pl.ds(pl.multiple_of(y * outer, 8), outer + mid)

    def at_final(self, kind):
        return self.at_y + (self.kinds[kind][1] + 1) * self.hop

    def kind_is(self, j, kind):
        out = (lax.rem(j, 2) == 1) & (j < self.plan.n - 2 * self.hop)
        return out if kind else jnp.logical_not(out)

    def count(self, kind):
        plan = self.plan
        real = [j for j in range(plan.n) if j < plan.early or j >= plan.far_whole]
        out = len([j for j in real if j % 2 == 1 and j < plan.n - 2 * self.hop])
        return out if kind else len(real) - out

    def slot(self, f):
        return jnp.where(f < self.plan.partial, f, f - self.plan.partial)

    def c_copy(self, f):
        src = self.parts.at[self.slot(f), :, 1 - self.p.c]
        return remote(src, self.c_got.at[lax.rem(f, FEW)], self.fs.at[f, 0], self.fr.at[f, 0], self.p.sib)

    def x_copy(self, f):
        src = self.parts.at[self.slot(f), 1 - self.p.x, self.p.c]
        return remote(src, self.x_got.at[f], self.fs.at[f, 1], self.fr.at[f, 1], self.p.across)

    def y_copy(self, j):
        dst = self.y_got.at[lax.rem(j, RING)]
        return remote(self.acc.at[self.plan.at(j), :, self.others], dst, self.all_s.at[0], self.ur.at[j, 0], self.p.pair)

    def r_copy(self, j, a, to_up, index):
        dst = self.r_got.at[lax.rem(j, self.ring), index]
        device = self.p.up if to_up else self.p.down
        return remote(self.acc.at[self.plan.at(j), a, self.message], dst, self.all_s.at[1 + a], self.ur.at[j, 1 + index], device)

    def yz_copy(self, j, a):
        dst = self.yz_got.at[lax.rem(j, RING)]
        return remote(self.acc.at[self.plan.at(j), a, self.mid], dst, self.us.at[j], self.ur.at[j, 4], self.p.pair)

    def b_copy(self, j, a, to_up, from_acc):
        src = self.acc if from_acc else self.final
        device = self.p.up if to_up else self.p.down
        send = self.all_s.at[3 + 2 * a + (1 if to_up else 0)]
        return remote(src.at[self.plan.at(j), a, self.message], self.final.at[self.plan.at(j), a, self.message], send, self.ur.at[j, 5 + a], device)

    def keep_copy(self, j, a):
        return pltpu.make_async_copy(
            self.acc.at[self.plan.at(j), a, self.message], self.final.at[self.plan.at(j), a, self.message], self.ur.at[j, 5 + a]
        )

    def last_copy(self, j):
        rows = self.final.at[self.plan.at(j), :, self.own]
        return remote(rows, rows, self.all_s.at[7], self.all_r.at[0], self.p.pair)

    def tick(self, t):
        p, n, hop = self.p, self.plan.n, self.hop

        def stage(offset, body, cond=None):
            j = t - offset
            ok = (j >= 0) & (j < n) & self.plan.real(j)
            if cond is not None:
                ok = ok & cond
            pl.when(ok)(lambda: body(j))

        ok, f0 = self.plan.starting(t)
        pl.when(ok)(lambda: self.c_copy(f0).start())

        ok, f1 = self.plan.starting(t - hop)

        @pl.when(ok)
        def _():
            self.c_copy(f1).wait()
            at, slot, j = lax.rem(f1, FEW), self.slot(f1), self.plan.place(f1)
            self.parts[slot, 1 - p.x, p.c, :, :] += self.c_got[at, 1 - p.x]
            self.x_copy(f1).start()
            for a in (0, 1):
                rows = pl.ds(a * (self.unit // 2), self.unit // 2)
                self.acc[self.plan.at(j), a] = self.parts[slot, p.x, p.c, rows, :] + self.c_got[at, p.x, rows, :]

        f2 = t - hop - self.plan.later - self.plan.held
        pl.when((f2 >= self.plan.early) & (f2 < self.plan.partial))(lambda: self.x_copy(f2).wait_send())

        def gather(j):
            @pl.when(self.plan.is_partial(j))
            def _():
                f = self.plan.number(j)
                self.x_copy(f).wait_recv()
                pl.when((f < self.plan.early) | (f >= self.plan.partial))(lambda: self.x_copy(f).wait_send())
                for a in (0, 1):
                    rows = pl.ds(a * (self.unit // 2), self.unit // 2)
                    self.acc[self.plan.at(j), a] += self.x_got[f, rows, :]

            self.y_copy(j).start()

        stage(2 * hop, gather)

        def own_half(j):
            self.y_copy(j).wait_recv()
            self.acc[self.plan.at(j), :, self.own, :] += self.y_got[lax.rem(j, RING)]

        stage(self.at_y, own_half)

        for kind, (roots, reach) in enumerate(self.kinds):
            far = [jnp.abs(p.z - root) for root in roots]
            at_final = self.at_final(kind)

            def turn(offset, body, cond=None, kind=kind):
                mine = self.kind_is(t - offset, kind)
                stage(offset, body, mine if cond is None else mine & cond)

            for a, root in enumerate(roots):
                above, below, here = p.z > root, p.z < root, p.z == root

                def reduce(j, a=a, root=root, above=above, below=below, here=here):
                    def take(index):
                        self.r_copy(j, a, True, index).wait_recv()
                        self.acc[self.plan.at(j), a, self.message, :] += self.r_got[lax.rem(j, self.ring), index]

                    pl.when(((p.z >= root) & p.has_up) | (below & p.has_down))(lambda: take(a))
                    pl.when(here & p.has_down)(lambda: take(2))
                    pl.when(above)(lambda: self.r_copy(j, a, False, a).start())
                    pl.when(p.z < root - 1)(lambda: self.r_copy(j, a, True, a).start())
                    pl.when(p.z == root - 1)(lambda: self.r_copy(j, a, True, 2).start())
                    pl.when(here)(lambda: self.yz_copy(j, a).start())

                turn(self.at_y + (reach - far[a]) * hop, reduce)

            for a, root in enumerate(roots):
                above, below, here = p.z > root, p.z < root, p.z == root

                def forward(j, a=a, above=above, below=below):
                    self.b_copy(j, a, True, False).wait_recv()
                    pl.when(above & p.has_up)(lambda: self.b_copy(j, a, True, False).start())
                    pl.when(below & p.has_down)(lambda: self.b_copy(j, a, False, False).start())

                turn(at_final + far[a] * hop, forward, above | below)

                def settle(j, a=a):
                    self.yz_copy(j, a).wait()
                    self.acc[self.plan.at(j), a, self.mid, :] += self.yz_got[lax.rem(j, RING)]
                    pl.when(p.has_up)(lambda: self.b_copy(j, a, True, True).start())
                    pl.when(p.has_down)(lambda: self.b_copy(j, a, False, True).start())
                    self.keep_copy(j, a).start()

                turn(at_final, settle, here)

            def last(j, roots=roots):
                for a, root in enumerate(roots):
                    pl.when(p.z == root)(lambda a=a: self.keep_copy(j, a).wait())
                self.last_copy(j).start()

            turn(at_final + jnp.maximum(far[0], far[1]) * hop, last)

    def drain(self):
        p = self.p
        own, others = self.final.at[:, :, self.own], self.final.at[:, :, self.others]

        def sent(index, ref):
            remote(ref, ref, self.all_s.at[index], self.all_r.at[0], p.pair).wait_send()

        sent(0, others)
        for kind, (roots, _) in enumerate(self.kinds):
            message = self.final.at[pl.ds(0, self.count(kind)), 0, self.message]
            for a, root in enumerate(roots):
                pl.when(p.z != root)(lambda a=a, message=message: sent(1 + a, message))
                pl.when((p.z >= root) & p.has_up)(lambda a=a, message=message: sent(4 + 2 * a, message))
                pl.when((p.z <= root) & p.has_down)(lambda a=a, message=message: sent(3 + 2 * a, message))
        sent(7, own)
        remote(own, others, self.all_s.at[7], self.all_r.at[0], p.pair).wait_recv()


def exchange_scratch(plan, unit, lanes, line):
    slots = plan.partial + 1
    return dict(
        parts=pltpu.VMEM((slots, 2, 2, unit, lanes), f32),
        c_got=pltpu.VMEM((FEW, 2, unit, lanes), f32),
        x_got=pltpu.VMEM((plan.partials, unit, lanes), f32),
        y_got=pltpu.VMEM((RING, 2, shares(unit)[0], lanes), f32),
        r_got=pltpu.VMEM((line_ring(line, plan.hop), 3, sum(shares(unit)), lanes), f32),
        yz_got=pltpu.VMEM((RING, shares(unit)[1], lanes), f32),
        acc=pltpu.VMEM((plan.units, 2, unit // 2, lanes), f32),
        fs=pltpu.SemaphoreType.DMA((plan.partials, 2)),
        fr=pltpu.SemaphoreType.DMA((plan.partials, 2)),
        us=pltpu.SemaphoreType.DMA((plan.n,)),
        ur=pltpu.SemaphoreType.DMA((plan.n, 7)),
        all_s=pltpu.SemaphoreType.DMA((8,)),
        all_r=pltpu.SemaphoreType.DMA((1,)),
    )


SMALL = ("cb", "g1", "s1", "vb", "g2", "s2", "ub")
SMALL_ROWS = 40
NEAR_AT, FAR_AT, TABLE_AT = 0, 16, 32
CW = 3
FIRST_TICK = 1
ORDER = dict(early=0, whole_tick=10, later=11, second_early=9, second_start=34, held=10)


def backward_kernel(dims, names, plan, *refs):
    windows, base, d, ff, taps, line, unit = dims
    rows = windows * base
    blocks = ff // d
    lanes = d // SEQ
    half = taps // 2
    r = Refs(names, refs)
    p = Place(line)
    per = d // unit
    smalls = 2 * per * blocks

    def loop(n, body):
        def run(i, carry):
            body(i)
            return carry

        lax.fori_loop(0, n, run, 0)

    def live(w):
        where = p.s * base + lax.broadcasted_iota(jnp.int32, (base, 1), 0)
        return where < r.lengths[w]

    def window(w):
        return pl.ds(pl.multiple_of(w * base, base), base)

    which = {name: i for i, name in enumerate(SAVED)}

    def load(name, side):
        return pltpu.make_async_copy(r.of(side, name), getattr(r, name), r.lsem.at[which[name]])

    def load_h(side):
        return pltpu.make_async_copy(r.of(side, "full"), r.h, r.lsem.at[len(SAVED)])

    def load_conv(side, k, i):
        at = lax.rem(i, CW)
        return pltpu.make_async_copy(r.of(side, "conv").at[k], r.cw.at[at], r.csem.at[at])

    def wide_loads(side, b, slot):
        wide = ff // SEQ
        got = []
        for q in range(SEQ):
            at = pl.ds(pl.multiple_of(q * wide + b * lanes, lanes), lanes)
            put = pl.ds(q * lanes, lanes)
            got.append(pltpu.make_async_copy(r.of(side, "up").at[:, at], r.uw.at[slot, :, put], r.wsem.at[slot, q]))
            got.append(
                pltpu.make_async_copy(r.of(side, "down").at[at, :], r.vw.at[slot, put, :], r.wsem.at[slot, SEQ + q])
            )
        return got

    def start(side, *which_names):
        for name in which_names:
            load(name, side).start()

    def wait(side, *which_names):
        for name in which_names:
            load(name, side).wait()

    cot = pltpu.make_async_copy(r.cotangent, r.dy, r.lsem.at[len(SAVED) + 1])
    cot.start()
    start("far", "n2", "rs2", "mid")

    p.greet(True)
    ex = Exchange(p, plan, unit, r)
    r.sums[...] = jnp.zeros(r.sums.shape, f32)
    r.parts[smalls, :, :, SMALL_ROWS:, :] = jnp.zeros((2, 2, unit - SMALL_ROWS, lanes), f32)

    @pl.when(p.s == 0)
    def _():
        r.dp[:, 0:HALO, :] = jnp.zeros((windows, HALO, d), f32)
        r.dw[:, 0:base, :] = jnp.zeros((windows, base, d), f32)

    @pl.when(p.s == SEQ - 1)
    def _():
        r.dp[:, HALO + base :, :] = jnp.zeros((windows, HALO, d), f32)
        r.dw[:, 2 * base :, :] = jnp.zeros((windows, base, d), f32)

    far_pad = half * SECOND_DILATION
    for ref, pad in ((r.dq_near, HALO), (r.dq_far, far_pad)):
        ref[:, 0:pad, :] = jnp.zeros((windows, pad, lanes), f32)
        ref[:, pad + SEQ * base :, :] = jnp.zeros((windows, pad, lanes), f32)

    def add(kind, v):
        r.sums[kind] += jnp.sum(v.reshape(v.shape[0] // 8, 8, d), axis=0)

    def ffn_norm_back(side, at0):
        def body(w):
            at = window(w)
            dy = r.dy[at, :]
            if side == "far":
                dy = jnp.where(live(w), dy, 0.0)
            n = r.n2[at, :]
            add(at0 + 4, dy * n)
            add(at0 + 5, dy)
            dn = dy * r.of(side, "g2")[...]
            rs = r.rs2[at, 0:1]
            df = rs * (dn - row_mean(dn) - n * row_mean(dn * n))
            add(at0 + 3, df)
            h, l = split(df)
            r.df_h[at, :] = h
            r.df_l[at, :] = l
            r.dmid[at, :] = dy
            mh, ml = split(r.mid[at, :])
            r.mid_h[at, :] = mh
            r.mid_l[at, :] = ml

        loop(windows, body)

    def put_units(j, v):
        for i in range(per):
            for q in range(SEQ):
                r.parts[j + i, q // 2, q % 2, :, :] = v[i * unit : (i + 1) * unit, q * lanes : (q + 1) * lanes]

    def ffn_back(b, at0):
        slot = lax.rem(b, 2)
        for copy in wide_loads("far", b, slot):
            copy.wait()
        r.tmp[...] = dot3((r.df_h[...], r.df_l[...]), split(r.vw[slot]), NT)

        def act(i):
            at = pl.ds(pl.multiple_of(i * ROWS, ROWS), ROWS)
            dz = r.tmp[at, :] * r.gp[b, at, :]
            add(at0 + 6 + b, dz)
            h, l = split(dz)
            r.dz_h[at, :] = h
            r.dz_l[at, :] = l
            r.gp[b, at, :] = dz

        loop(rows // ROWS, act)

    def ffn_on(b):
        r.dmid[...] += dot3((r.dz_h[...], r.dz_l[...]), split(r.uw[lax.rem(b, 2)]), NT)

    def down_weights(b):
        put_units(2 * per * b, dot3((r.hid_h[b], r.hid_l[b]), (r.df_h[...], r.df_l[...]), TN))

    def up_weights(b):
        put_units(2 * per * b + per, dot3((r.mid_h[...], r.mid_l[...]), split(r.gp[b]), TN))

    def conv_norm_back(side, at0, put):
        def body(w):
            at = window(w)
            dmid, n = r.dmid[at, :], r.n1[at, :]
            add(at0 + 1, dmid * n)
            add(at0 + 2, dmid)
            dn = dmid * r.of(side, "g1")[...]
            dconv = r.gr1[at, :] * (dn - row_mean(dn) - n * row_mean(dn * n))
            add(at0, dconv)
            put(w, dconv)

        loop(windows, body)

    xs, xr = r.ssem, r.rsem

    def quarter_copies(src, at, pad, dq, sems):
        put = pl.ds(pl.multiple_of(pad + p.s * base, 8), base)
        got = []
        for i, s in enumerate((p.across_s, p.diag_s, p.sib_s)):
            cols = pl.ds(pl.multiple_of(s * lanes, lanes), lanes)
            mine = src.at[:, pl.ds(at, base), cols]
            got.append(remote(mine, dq.at[:, put, :], sems.at[0, i], sems.at[1, i], (p.w, s)))
        return got

    def keep_quarter(src, at, pad, dq):
        cols = pl.ds(pl.multiple_of(p.s * lanes, lanes), lanes)
        dq[:, pl.ds(pl.multiple_of(pad + p.s * base, 8), base), :] = src[:, at : at + base, cols]

    def weight_back(dq, pad, dilation, at, w, lo, hi):
        left = split(r.h[:, pl.ds(w, 1), :, :].reshape(SEQ * base, d))
        right = [
            dq[w, pad - (k - half) * dilation : pad - (k - half) * dilation + SEQ * base, :] for k in range(lo, hi)
        ]
        v = dot3(left, split(jnp.concatenate(right, axis=1)), TN)

        def put(first):
            for k in range(lo, hi):
                for i in range(2 * per):
                    piece = v[i * (unit // 2) : (i + 1) * (unit // 2), (k - lo) * lanes : (k - lo + 1) * lanes]
                    j = at + k * per + i // 2
                    if first:
                        r.acc[j, i % 2] = piece
                    else:
                        r.acc[j, i % 2] += piece

        pl.when(w == 0)(lambda: put(True))
        pl.when(w > 0)(lambda: put(False))

    groups = [(lo, min(lo + 3, taps)) for lo in range(0, taps, 3)]
    own_rows = pl.ds(base, base)

    def block_next():
        return remote(r.dw.at[:, own_rows], r.dw.at[:, pl.ds(0, base)], xs.at[0], xr.at[0], p.next)

    def block_prev():
        return remote(r.dw.at[:, own_rows], r.dw.at[:, pl.ds(2 * base, base)], xs.at[1], xr.at[1], p.prev)

    def far_quarters(w):
        at = pl.ds(w, 1)
        return quarter_copies(r.dw.at[at], base, far_pad, r.dq_far.at[at], r.qsem.at[w])

    def halo_next():
        return remote(r.dp.at[:, pl.ds(base, HALO)], r.dp.at[:, pl.ds(0, HALO)], xs.at[5], xr.at[5], p.next)

    def halo_prev():
        return remote(r.dp.at[:, pl.ds(HALO, HALO)], r.dp.at[:, pl.ds(HALO + base, HALO)], xs.at[6], xr.at[6], p.prev)

    def near_quarters():
        return quarter_copies(r.dp, HALO, HALO, r.dq_near, r.qsem.at[windows])

    def far_norm():
        wait("far", "n1", "gr1")

        def put(w, dconv):
            r.dw[w, base : 2 * base, :] = dconv
            for copy in far_quarters(w):
                copy.start()
            h, l = split(dconv)
            r.dw_h[w, base : 2 * base, :] = h
            r.dw_l[w, base : 2 * base, :] = l

        conv_norm_back("far", FAR_AT, put)
        start("near", "n2", "rs2", "n1", "gr1")
        keep_quarter(r.dw, base, far_pad, r.dq_far)
        r.tmp[...] = jnp.zeros((rows, d), f32)

    def far_tap(k):
        at = pl.ds(pl.multiple_of(base - (k - half) * SECOND_DILATION, SECOND_DILATION), base)
        lhs = (r.dw_h[:, at, :].reshape(rows, d), r.dw_l[:, at, :].reshape(rows, d))
        load_conv("far", k, k).wait()
        r.tmp[...] += dot3(lhs, split(r.cw[lax.rem(k, CW)]), NT)
        pl.when(k + CW < taps)(lambda: load_conv("far", k + CW, k + CW).start())
        pl.when(k + CW >= taps)(lambda: load_conv("near", k + CW - taps, k + CW).start())

    def far_halo():
        pl.when(p.has_prev)(lambda: block_next().wait_recv())
        pl.when(p.has_next)(lambda: block_prev().wait_recv())

        def halves(w):
            for at in (0, 2 * base):
                h, l = split(r.dw[w, at : at + base, :])
                r.dw_h[w, at : at + base, :] = h
                r.dw_l[w, at : at + base, :] = l

        loop(windows, halves)

    def far_end():
        def dx(w):
            at = window(w)
            r.dy[at, :] = r.dmid[at, :] + jnp.where(live(w), r.tmp[at, :], 0.0)

        loop(windows, dx)

    def near_begin():
        wait("near", "n2", "rs2", "mid", "gp", "hid_h", "hid_l")
        ffn_norm_back("near", NEAR_AT)

    def near_norm():
        wait("near", "n1", "gr1")

        def put(w, dconv):
            r.dp[w, HALO : HALO + base, :] = dconv

        conv_norm_back("near", NEAR_AT, put)
        pl.when(p.has_next)(lambda: halo_next().start())
        pl.when(p.has_prev)(lambda: halo_prev().start())
        for copy in near_quarters():
            copy.start()
        keep_quarter(r.dp, HALO, HALO, r.dq_near)

    def near_halo():
        pl.when(p.has_prev)(lambda: halo_next().wait_recv())
        pl.when(p.has_next)(lambda: halo_prev().wait_recv())

    def near_tap(k):
        at = HALO - (k - half) * FIRST_DILATION
        lhs = split(r.dp[:, at : at + base, :].reshape(rows, d))
        load_conv("near", k, taps + k).wait()
        v = dot3(lhs, split(r.cw[(taps + k) % CW]), NT)
        if k == 0:
            r.tmp[...] = v
        else:
            r.tmp[...] += v
        if k + CW < taps:
            load_conv("near", k + CW, taps + k + CW).start()

    def input_grad():
        return pltpu.make_async_copy(r.dy, r.input_grad, r.lsem.at[len(SAVED) + 1])

    def near_end():
        def dx(w):
            at = window(w)
            v = r.dmid[at, :] + jnp.where(live(w), r.tmp[at, :], 0.0)
            r.dy[at, :] = v
            v = jnp.sum(v.reshape(base // 8, 8, d), axis=0)
            species = r.species[w]
            for kind in range(SMALL_ROWS - TABLE_AT):
                r.sums[TABLE_AT + kind] += jnp.where(species == kind, v, 0.0)

        loop(windows, dx)
        input_grad().start()
        small = jnp.sum(r.sums[...], axis=1)
        for q in range(SEQ):
            r.parts[smalls, q // 2, q % 2, 0:SMALL_ROWS, :] = small[:, q * lanes : (q + 1) * lanes]

    cot.wait()
    wait("far", "n2", "rs2", "mid")
    for copy in wide_loads("far", 0, 0):
        copy.start()
    start("far", "gp")
    ffn_norm_back("far", FAR_AT)
    start("far", "hid_h", "hid_l")
    for copy in wide_loads("far", 1, 1):
        copy.start()
    start("far", "n1", "gr1")
    wait("far", "gp")
    p.await_all(True)

    at = 0

    def take(n):
        nonlocal at
        at += n
        return at - n

    far_ffn = take(blocks)
    far_norm_at = take(1)
    far_ffn_weights = take(blocks)
    far_weights = take(len(groups) * windows)
    far_taps = take(-(-taps // 2))
    far_end_at = take(1)
    near_begin_at = take(1)
    near_ffn = take(2 * blocks)
    near_norm_at = take(1)
    near_ffn_weights = take(2 * blocks)
    near_taps = take(-(-taps // 2))
    near_end_at = take(1)
    near_weights = take(len(groups) * windows)

    def step(i, carry):
        def when(first, n, body):
            pl.when((i >= first) & (i < first + n))(lambda: body(i - first))

        far = (i >= far_ffn) & (i < far_ffn + blocks)
        far_later = (i >= far_ffn_weights) & (i < far_ffn_weights + blocks)
        near = (i >= near_ffn) & (i < near_ffn + 2 * blocks)
        near_later = (i >= near_ffn_weights) & (i < near_ffn_weights + 2 * blocks)
        near_from = jnp.where(near, near_ffn, near_ffn_weights)
        b = jnp.where(far, i - far_ffn, jnp.where(far_later, i - far_ffn_weights, lax.div(i - near_from, 2)))
        turn = lax.rem(i - near_from, 2)
        pl.when(i == far_ffn_weights)(lambda: wait("far", "hid_h", "hid_l"))

        @pl.when(i == far_norm_at)
        def _():
            load_h("far").start()
            for k in range(CW):
                load_conv("far", k, k).start()

        pl.when(far | (near & (turn == 0)))(lambda: ffn_back(b, jnp.where(near, NEAR_AT, FAR_AT)))

        @pl.when(far | (near & (turn == 1)))
        def _():
            ffn_on(b)

            def fetch(side, b):
                for copy in wide_loads(side, b, lax.rem(b, 2)):
                    copy.start()

            pl.when(near & (b < blocks - 2))(lambda: fetch("near", b + 2))
            pl.when(far & (b < blocks - 2))(lambda: fetch("far", b + 2))
            pl.when(far & (b >= blocks - 2))(lambda: fetch("near", b - (blocks - 2)))

        pl.when(far_later | (near_later & (turn == 0)))(lambda: down_weights(b))
        pl.when(far_later | (near_later & (turn == 1)))(lambda: up_weights(b))
        when(far_norm_at, 1, lambda _: far_norm())

        @pl.when(i == far_weights)
        def _():
            start("near", "mid", "gp", "hid_h", "hid_l")
            for w in range(windows):
                for copy in far_quarters(w):
                    copy.wait()
            pl.when(p.has_next)(lambda: block_next().start())
            pl.when(p.has_prev)(lambda: block_prev().start())
            load_h("far").wait()

        for g, (lo, hi) in enumerate(groups):
            when(
                far_weights + g * windows,
                windows,
                lambda w, lo=lo, hi=hi: weight_back(
                    r.dq_far, far_pad, SECOND_DILATION, plan.far_whole - plan.gap, w, lo, hi
                ),
            )

        @pl.when(i == far_taps)
        def _():
            load_h("near").start()
            far_halo()

        def two_taps(m):
            far_tap(2 * m)
            pl.when(2 * m + 1 < taps)(lambda: far_tap(2 * m + 1))

        when(far_taps, -(-taps // 2), two_taps)
        when(far_end_at, 1, lambda _: far_end())
        when(near_begin_at, 1, lambda _: near_begin())
        when(near_norm_at, 1, lambda _: near_norm())
        pl.when(i == near_taps)(near_halo)
        for k in range(taps):
            when(near_taps + k // 2, 1, lambda _, k=k: near_tap(k))
        when(near_end_at, 1, lambda _: near_end())

        @pl.when(i == near_weights)
        def _():
            for copy in near_quarters():
                copy.wait()
            load_h("near").wait()

        for g, (lo, hi) in enumerate(groups):
            when(
                near_weights + g * windows,
                windows,
                lambda w, lo=lo, hi=hi: weight_back(r.dq_near, HALO, FIRST_DILATION, plan.near_whole - plan.gap, w, lo, hi),
            )
        ex.tick(i - FIRST_TICK)
        return carry

    lax.fori_loop(0, max(at, ex.ticks + FIRST_TICK), step, 0)
    ex.drain()

    @pl.when(p.has_next)
    def _():
        halo_next().wait_send()
        block_next().wait_send()

    @pl.when(p.has_prev)
    def _():
        halo_prev().wait_send()
        block_prev().wait_send()

    input_grad().wait()


def backward(line, lengths, species, table, cotangent, fulls, saved, near, far):
    windows, base, d = cotangent.shape
    taps, ff = near[0].shape[0], near[4].shape[1]
    rows, blocks, lanes = windows * base, ff // d, d // SEQ
    unit, hop = 256, (2 if line <= 4 else 1)
    per = d // unit
    plan = Plan(2 * per * blocks, taps * per, hop, **ORDER)
    n = plan.units
    smem = pl.BlockSpec(memory_space=pltpu.SMEM)
    vmem = pl.BlockSpec(memory_space=pltpu.VMEM)
    hbm = pl.BlockSpec(memory_space=pl.ANY)
    names, args, specs = ["lengths", "species", "cotangent"], [lengths, species, cotangent.reshape(rows, d)], [smem, smem, hbm]
    for side, block, full, kept in zip(("near", "far"), (near, far), fulls, saved, strict=True):
        names += [side + "_" + v for v in ("full", "conv", "up", "down") + SAVED + ("g1", "g2")]
        args += [full, block[0], block[4], block[6], *kept, block[2].reshape(1, -1), block[8].reshape(1, -1)]
        specs += [hbm] * (4 + len(SAVED)) + [vmem] * 2
    names += ["input_grad", "final"]
    scratch = {name: pltpu.VMEM(*v) for name, v in saved_shapes(rows, d, ff).items()}
    for name in ("dy", "dmid", "tmp"):
        scratch[name] = pltpu.VMEM((rows, d), f32)
    for name in ("mid_h", "mid_l", "df_h", "df_l", "dz_h", "dz_l"):
        scratch[name] = pltpu.VMEM((rows, d), bf16)
    scratch.update(
        h=pltpu.VMEM((SEQ, windows, base, d), f32),
        cw=pltpu.VMEM((CW, d, d), f32),
        uw=pltpu.VMEM((2, d, d), f32),
        vw=pltpu.VMEM((2, d, d), f32),
        dp=pltpu.VMEM((windows, base + 2 * HALO, d), f32),
        dw=pltpu.VMEM((windows, 3 * base, d), f32),
        dw_h=pltpu.VMEM((windows, 3 * base, d), bf16),
        dw_l=pltpu.VMEM((windows, 3 * base, d), bf16),
        dq_near=pltpu.VMEM((windows, SEQ * base + 2 * HALO, lanes), f32),
        dq_far=pltpu.VMEM((windows, SEQ * base + taps // 2 * 2 * SECOND_DILATION, lanes), f32),
        sums=pltpu.VMEM((SMALL_ROWS, 8, d), f32),
        lsem=pltpu.SemaphoreType.DMA((len(SAVED) + 2,)),
        csem=pltpu.SemaphoreType.DMA((CW,)),
        wsem=pltpu.SemaphoreType.DMA((2, 2 * SEQ)),
        ssem=pltpu.SemaphoreType.DMA((7,)),
        rsem=pltpu.SemaphoreType.DMA((7,)),
        qsem=pltpu.SemaphoreType.DMA((windows + 1, 2, 3)),
    )
    scratch.update(exchange_scratch(plan, unit, lanes, line))
    names += list(scratch)
    input_grad, final = pl.pallas_call(
        functools.partial(backward_kernel, (windows, base, d, ff, taps, line, unit), names, plan),
        out_shape=[jax.ShapeDtypeStruct((rows, d), f32), jax.ShapeDtypeStruct((n, 2, unit // 2, lanes), f32)],
        in_specs=specs,
        out_specs=[hbm, hbm],
        scratch_shapes=list(scratch.values()),
        compiler_params=pltpu.CompilerParams(
            collective_id=1, has_side_effects=True, vmem_limit_bytes=64 * 1024 * 1024 - 65536
        ),
        name="backward",
    )(*args)

    grads = unpack(plan, windows, rows, blocks, taps, d, ff, unit, final.reshape(n, unit, lanes))
    table_grad, near_grads, far_grads = grads[0], grads[1:11], grads[11:]
    shapes = [(taps, d, lanes), (lanes,), (lanes,), (lanes,), (d, ff // SEQ), (ff // SEQ,), (ff, lanes)] + 3 * [(lanes,)]
    near_grads = [v.reshape(shape) for v, shape in zip(near_grads, shapes, strict=True)]
    far_grads = [v.reshape(shape) for v, shape in zip(far_grads, shapes, strict=True)]
    return input_grad.reshape(cotangent.shape), table_grad, near_grads, far_grads


CHUNK = 10


def unpack_kernel(plan, dims, final, table, *refs):
    blocks, taps, d, ff, unit = dims
    lanes = d // SEQ
    per = d // unit
    outs, held, in_sem, out_sem = refs[:20], refs[20], refs[21], refs[22]
    total = final.shape[0]
    fetches = []
    for j in range(0, total, CHUNK):
        some = pl.ds(j, min(CHUNK, total - j))
        fetches.append(pltpu.make_async_copy(final.at[some], held.at[some], in_sem.at[j // CHUNK]))
    fetched = [False] * len(fetches)
    for fetch in fetches:
        fetch.start()

    def copy(src, dst):
        pltpu.make_async_copy(src, dst, out_sem.at[0]).start()

    def unit_at(j):
        j = plan.at(j)
        if not fetched[j // CHUNK]:
            fetches[j // CHUNK].wait()
            fetched[j // CHUNK] = True
        return held.at[j]

    for side, first, whole in ((outs[10:], 0, plan.far_whole), (outs[:10], plan.partial, plan.near_whole)):
        cw, _, _, _, uw, _, vw, _, _, _ = side
        for i in range(taps * per):
            copy(unit_at(whole + i), cw.at[i // per, pl.ds(i % per * unit, unit)])
        for b in range(blocks):
            cols = pl.ds(b * lanes, lanes)
            for i in range(per):
                f = first + 2 * per * b + i
                for q in range(unit // lanes):
                    row = (i * (unit // lanes) + q) * (ff // SEQ) + b * lanes
                    copy(unit_at(plan.place(f)).at[pl.ds(q * lanes, lanes)], vw.at[pl.ds(row, lanes)])
                copy(unit_at(plan.place(f + per)), uw.at[pl.ds(i * unit, unit), cols])
    small = unit_at(plan.place(plan.partials - 1))
    copy(small.at[pl.ds(TABLE_AT, SMALL_ROWS - TABLE_AT)], table)
    for (_, cb, g1, s1, _, ub, _, vb, g2, s2), at in ((outs[:10], NEAR_AT), (outs[10:], FAR_AT)):
        for i, ref in enumerate((cb, g1, s1, vb, g2, s2)):
            copy(small.at[pl.ds(at + i, 1)], ref)
        for b in range(blocks):
            copy(small.at[pl.ds(at + 6 + b, 1)], ub.at[:, pl.ds(b * lanes, lanes)])
    assert all(fetched)
    for ref in (table, *outs):
        pltpu.make_async_copy(ref, ref, out_sem.at[0]).wait()


def unpack(plan, windows, rows, blocks, taps, d, ff, unit, final):
    lanes = d // SEQ
    one = (1, lanes)
    block = [(taps, d, lanes), one, one, one, (d, ff // SEQ), (1, ff // SEQ), (ff, lanes), one, one, one]
    hbm = pl.BlockSpec(memory_space=pl.ANY)
    outs = [(SMALL_ROWS - TABLE_AT, lanes)] + block + block
    return pl.pallas_call(
        functools.partial(unpack_kernel, plan, (blocks, taps, d, ff, unit)),
        out_shape=[jax.ShapeDtypeStruct(v, f32) for v in outs],
        in_specs=[hbm],
        out_specs=[hbm] * len(outs),
        scratch_shapes=[
            pltpu.VMEM((plan.units, unit, lanes), f32),
            pltpu.SemaphoreType.DMA((-(-plan.units // CHUNK),)),
            pltpu.SemaphoreType.DMA((1,)),
        ],
        compiler_params=pltpu.CompilerParams(vmem_limit_bytes=60 * 1024 * 1024),
        name="unpack",
    )(final)


def on_device(inputs, species, lengths, species_table, *rest):
    near, far, cotangent = rest[:10], rest[10:20], rest[20]
    line = lax.axis_size("win") // 2
    output, near_full, far_full, near_saved, far_saved = forward(
        line, lengths, species, species_table, inputs, near, far
    )
    input_grad, table_grad, near_grads, far_grads = backward(
        line, lengths, species, species_table, cotangent, (near_full, far_full), (near_saved, far_saved), near, far
    )
    return (output, input_grad, table_grad, *near_grads, *far_grads)


def solution(mesh):
    split_windows = P("win", "seq", None)
    block_grads = (P(None, None, "seq"), P("seq"), P("seq"), P("seq"), P(None, "seq"), P("seq"), P(None, "seq"))
    block_grads += (P("seq"), P("seq"), P("seq"))
    return jax.shard_map(
        on_device,
        mesh=mesh,
        in_specs=(split_windows, P("win"), P("win")) + (P(),) * 21 + (split_windows,),
        out_specs=(split_windows, split_windows, P(None, "seq")) + block_grads + block_grads,
        check_vma=False,
    )
```
